32 devices in a mesh: ctx: 8 (over y, x, core), tp: 4 (over z).
Axes of the slice: x: 2, y: 2, z: 4, core: 2. Of those that a mesh axis runs over, the one named last changes fastest.
Arguments:
- tokens: bfloat16 [4096, 2304], P('ctx'), may hold values from -6 to 6
- block_map: int32 [8, 2], replicated, may hold values from 0 to 15, as said below
- w_query: bfloat16 [2304, 2048], P('ctx', 'tp'), may hold values from -0.125 to 0.125
- w_key: bfloat16 [2304, 1024], P('ctx', 'tp'), may hold values from -0.125 to 0.125
- w_value: bfloat16 [2304, 1024], P('ctx', 'tp'), may hold values from -0.125 to 0.125
- w_out: bfloat16 [2048, 2304], P('tp', 'ctx'), may hold values from -0.125 to 0.125
- w_gate: bfloat16 [2304, 9216], P('ctx', 'tp'), may hold values from -0.125 to 0.125
- w_up: bfloat16 [2304, 9216], P('ctx', 'tp'), may hold values from -0.125 to 0.125
- w_down: bfloat16 [9216, 2304], P('tp', 'ctx'), may hold values from -0.0625 to 0.0625
- norm_gains: bfloat16 [4, 2304], P(None, 'ctx'), may hold values from 0.25 to 1.75
- cotangent: bfloat16 [4096, 2304], P('ctx'), may hold values from -6 to 6
Outputs:
- layer_out: bfloat16 [4096, 2304], P('ctx')
- input_grad: float32 [4096, 2304], P('ctx')
- grad_query: float32 [2304, 2048], P('ctx', 'tp')
- grad_key: float32 [2304, 1024], P('ctx', 'tp')
- grad_value: float32 [2304, 1024], P('ctx', 'tp')
- grad_out: float32 [2048, 2304], P('tp', 'ctx')
- grad_gate: float32 [2304, 9216], P('ctx', 'tp')
- grad_up: float32 [2304, 9216], P('ctx', 'tp')
- grad_down: float32 [9216, 2304], P('tp', 'ctx')
- grad_gains: float32 [4, 2304], P(None, 'ctx')
The draws below stay inside these ranges and needn't reach their ends.
Inputs may be any that keep to these rules, and one draw needn't show every extreme that they name: Every block number appears exactly once in block_map.
All inputs are finite; a program needn't handle non-finite values.
Results may differ from the reference program's by a relative error of at most 0.025.
Values may be sent and summed in bfloat16 or wider, within the bound.
No kernel may reach another device: no remote copies, remote signals or barrier semaphores. Data moves between devices by JAX's collectives and lax.ppermute only.
A program may use at most 192 MiB of HBM per device.

```python
import math
from functools import partial
import jax
import jax.numpy as jnp
from jax import lax

D = 2304
HEADS = 8
KV_HEADS = 4
HD = 256
FF = 9216
WINDOW = 4096
BLOCK = 256
BLOCKS = 16
TOKENS = 4096
SEQ_LEN = 4096


def draw_block_map(key, part):
    key = jax.random.fold_in(key, 7)
    return jax.random.permutation(key, BLOCKS).reshape(BLOCKS // 2, 2).astype(jnp.int32)


def levels(own_key, dims, pieces, least, top_value):
    level = 1.0
    for position, blocks in pieces:
        steps = jax.random.uniform(jax.random.fold_in(jax.random.fold_in(own_key, 6), position), (blocks,), jnp.float32, least / len(pieces), top_value / len(pieces))
        level = level * jnp.repeat(jnp.exp(steps), dims[position] // blocks).reshape((-1,) + (1,) * (len(dims) - 1 - position))
    return level


def bell_draw(key, extent, scale, limit, split=(), held_as=jnp.bfloat16):
    values = jax.random.normal(key, extent, jnp.float32) * scale
    if len(split) > 0:
        values = levels(key, extent, split, -0.22, 0.18) * values
    return jnp.clip(values, min=-limit, max=limit).astype(held_as)


def setup_inputs(seed: int = 0) -> dict:
    splits = jax.random.split(jax.random.key(seed), 12)
    return {
        "tokens": bell_draw(splits[0], (TOKENS, D), 1.0, 6.0, ((0, 8),)),
        "block_map": draw_block_map(jax.random.fold_in(splits[11], 71), 0),
        "w_query": bell_draw(splits[2], (D, HEADS * HD), D ** -0.5, 0.125, ((0, 8), (1, 4))),
        "w_key": bell_draw(splits[3], (D, KV_HEADS * HD), D ** -0.5, 0.125, ((0, 8), (1, 4))),
        "w_value": bell_draw(splits[4], (D, KV_HEADS * HD), D ** -0.5, 0.125, ((0, 8), (1, 4))),
        "w_out": bell_draw(splits[5], (HEADS * HD, D), (HEADS * HD) ** -0.5, 0.125, ((0, 4), (1, 8))),
        "w_gate": bell_draw(splits[6], (D, FF), D ** -0.5, 0.125, ((0, 8), (1, 4))),
        "w_up": bell_draw(splits[7], (D, FF), D ** -0.5, 0.125, ((0, 8), (1, 4))),
        "w_down": bell_draw(splits[8], (FF, D), FF ** -0.5, 0.0625, ((0, 4), (1, 8))),
        "norm_gains": jnp.clip(1.0 + 0.15 * jax.random.normal(splits[9], (4, D), jnp.float32), 0.25, 1.75).astype(jnp.bfloat16),
        "cotangent": bell_draw(splits[10], (TOKENS, D), 1.0, 6.0, ((0, 8),)),
    }


@jax.custom_vjp
def low(v):
    return lax.optimization_barrier(v.astype(jnp.bfloat16)).astype(jnp.float32)

@jax.custom_vjp
def low_back(v):
    return v

def low_keep(v):
    return (low(v), None)

def low_pass(kept, grad):
    return (grad,)

def back_keep(v):
    return (v, None)

def back_low(kept, grad):
    return (low(grad),)
low.defvjp(low_keep, low_pass)
low_back.defvjp(back_keep, back_low)
epsilon = 1e-06
soft_cap = 50.0
masked_score = -1e+30
highest = lax.Precision.HIGHEST

def product(left, right):
    return jnp.dot(left, right, precision=highest, preferred_element_type=jnp.float32)

def rms_scale(values):
    return lax.rsqrt(lax.optimization_barrier(jnp.mean(values * values, axis=-1, keepdims=True)) + epsilon)

def angle_tables(positions):
    half_dim = HD // 2
    frequency = jnp.power(10000.0, -2.0 * jnp.arange(half_dim, dtype=jnp.float32) / HD)
    phases = positions.astype(jnp.float32)[:, None] * frequency[None, :]
    phases = jnp.concatenate([phases, phases], axis=-1)
    return (jnp.cos(phases), jnp.sin(phases))

def rotate(values, cosine, sine_table):
    half_dim = values.shape[-1] // 2
    turned = jnp.concatenate([-values[..., half_dim:], values[..., :half_dim]], axis=-1)
    return values * cosine + turned * sine_table

def forward(global_index, inputs, w_query, w_key, w_value, w_out, w_gate, w_up, w_down, gains):
    seq_ids = global_index // SEQ_LEN
    cosine, sine_table = angle_tables(global_index % SEQ_LEN)
    group_size = HEADS // KV_HEADS
    normed_in = low(inputs * rms_scale(inputs) * gains[0])
    query_raw = low_back(product(normed_in, w_query)).reshape(TOKENS, HEADS, HD).transpose(1, 0, 2)
    key_raw = low_back(product(normed_in, w_key)).reshape(TOKENS, KV_HEADS, HD).transpose(1, 0, 2)
    values = low(low_back(product(normed_in, w_value))).reshape(TOKENS, KV_HEADS, HD).transpose(1, 0, 2)
    queries = low(rotate(query_raw, cosine, sine_table) * HD ** (-0.5)).reshape(KV_HEADS, group_size, TOKENS, HD)
    keys_all = low(rotate(key_raw, cosine, sine_table))
    query_rows = math.gcd(512, TOKENS)
    blocks_count = TOKENS // query_rows
    query_blocks = queries.reshape(KV_HEADS, group_size, blocks_count, query_rows, HD).transpose(2, 0, 1, 3, 4)
    index_blocks = global_index.reshape(blocks_count, query_rows)

    def attend(block_item):
        query_block, query_index = block_item
        raw_scores = low_back(jnp.einsum('hgqd,hkd->hgqk', query_block, keys_all, precision=highest))
        capped = soft_cap * jnp.tanh(raw_scores / soft_cap)
        distance = query_index[:, None] - global_index[None, :]
        allowed = (query_index[:, None] // SEQ_LEN == seq_ids[None, :]) & (distance >= 0) & (distance < WINDOW)
        capped = jnp.where(allowed, capped, masked_score)
        row_top = lax.optimization_barrier(jnp.max(capped, axis=-1, keepdims=True))
        weights = jnp.exp(capped - row_top)
        probs = low(weights / lax.optimization_barrier(jnp.sum(weights, axis=-1, keepdims=True)))
        return jnp.einsum('hgqk,hkd->hgqd', probs, values, precision=highest)
    attended = lax.map(jax.checkpoint(attend), (query_blocks, index_blocks))
    attn_flat = low(low_back(attended.transpose(0, 3, 1, 2, 4).reshape(TOKENS, HEADS * HD)))
    branch = low_back(product(attn_flat, w_out))
    residual = inputs + branch * rms_scale(branch) * gains[1]
    normed_mid = low(residual * rms_scale(residual) * gains[2])
    gate_pre = low_back(product(normed_mid, w_gate))
    up_pre = low_back(product(normed_mid, w_up))
    hidden = low(jax.nn.gelu(gate_pre, approximate=True) * up_pre)
    mlp_out = low_back(product(hidden, w_down))
    return residual + mlp_out * rms_scale(mlp_out) * gains[3]

def reference(tokens, block_map, w_query, w_key, w_value, w_out, w_gate, w_up, w_down, norm_gains, cotangent):
    dealt = block_map.reshape(-1).astype(jnp.int32)
    global_index = (dealt[:, None] * BLOCK + jnp.arange(BLOCK, dtype=jnp.int32)[None, :]).reshape(-1)
    floats = [array_in.astype(jnp.float32) for array_in in (tokens, w_query, w_key, w_value, w_out, w_gate, w_up, w_down, norm_gains)]
    result, pull_back = jax.vjp(partial(forward, global_index), *floats)
    grads = pull_back(cotangent.astype(jnp.float32))
    return (result.astype(jnp.bfloat16), grads[0], grads[1], grads[2], grads[3], grads[4], grads[5], grads[6], grads[7], grads[8])
```

```python
from functools import partial

import jax
import jax.numpy as jnp
from jax import lax
from jax.experimental import pallas as pl
from jax.experimental.pallas import tpu as pltpu
from jax.sharding import PartitionSpec as P

HD = 256
WINDOW = 4096


epsilon = 1e-06
soft_cap = 50.0
LOG2E = 1.4426950408889634


def rms_scale(values):
    return lax.rsqrt(jnp.mean(values * values, axis=-1, keepdims=True) + epsilon)


def norm_back(values, row_scale, gain_row, gradient):
    normed = values * row_scale
    weighted = gradient * gain_row
    gain_grad = jnp.sum(gradient * normed, axis=0)
    value_grad = row_scale * (
        weighted - normed * jnp.mean(weighted * normed, axis=-1, keepdims=True)
    )
    return (value_grad, gain_grad)


def angle_tables(positions):
    half_dim = HD // 2
    frequency = jnp.power(10000.0, -2.0 * jnp.arange(half_dim, dtype=jnp.float32) / HD)
    phases = positions.astype(jnp.float32)[:, None] * frequency[None, :]
    phases = jnp.concatenate([phases, phases], axis=-1)
    return (jnp.cos(phases), jnp.sin(phases))


def rotate(values, cosine, sine_table):
    half_dim = values.shape[-1] // 2
    turned = jnp.concatenate([-values[..., half_dim:], values[..., :half_dim]], axis=-1)
    return values * cosine + turned * sine_table


def unrotate(gradient, cosine, sine_table):
    half_dim = gradient.shape[-1] // 2
    weighted = gradient * sine_table
    turned = jnp.concatenate([weighted[..., half_dim:], -weighted[..., :half_dim]], axis=-1)
    return gradient * cosine + turned


def matmul(left, right):
    return jnp.dot(left, right, preferred_element_type=jnp.float32)


def matmul_nt(left, right):
    return lax.dot_general(left, right, (((1,), (1,)), ((), ())), preferred_element_type=jnp.float32)


def tie(value, *others):
    return lax.optimization_barrier((value,) + others)[0]


def block_lists(ids_ref, first, key_blocks, own, seq_blocks, reach, list_ref):
    def look(slot, count):
        other = ids_ref[first + slot]
        gap = own - other
        whole = (gap > 0) & (gap < reach) & (own // seq_blocks == other // seq_blocks)
        list_ref[count] = slot
        return count + whole.astype(jnp.int32)

    return lax.fori_loop(0, key_blocks, look, jnp.int32(0))


def find_block(ids_ref, first, key_blocks, wanted):
    def look(slot, found):
        return jnp.where(ids_ref[first + slot] == wanted, slot, found)

    return lax.fori_loop(0, key_blocks, look, jnp.int32(-1))


def attend_kernel(
    ids_ref, own_ref, q_ref, k_ref, v_ref, o_ref, l_ref, acc_ref, sum_ref, list_ref,
    *, blk, heads, key_blocks, seq_blocks, reach
):
    chunk = pl.program_id(0)
    first = chunk * key_blocks
    q_blocks = q_ref.shape[0] // blk

    @pl.when(chunk == 0)
    def _():
        acc_ref[...] = jnp.zeros_like(acc_ref)
        sum_ref[...] = jnp.zeros_like(sum_ref)

    def tile(b, slot, mask):
        rows = pl.ds(pl.multiple_of(slot * blk, blk), blk)
        keys = k_ref[rows, :]
        vals = v_ref[rows, :]
        for h in range(heads):
            query = q_ref[b * blk : (b + 1) * blk, h * HD : (h + 1) * HD]
            capped = jnp.tanh(matmul_nt(query, keys) * (1.0 / soft_cap))
            weights = jnp.exp2(capped * (soft_cap * LOG2E))
            if mask is not None:
                weights = jnp.where(mask, weights, 0.0)
            at = (slice(b * blk, (b + 1) * blk), slice(h * HD, (h + 1) * HD))
            lanes = (slice(b * blk, (b + 1) * blk), slice(h * 128, (h + 1) * 128))
            part = weights[:, :128]
            for piece in range(1, blk // 128):
                part = part + weights[:, piece * 128 : (piece + 1) * 128]
            sum_ref[lanes] += part
            acc_ref[at] += matmul(weights.astype(jnp.bfloat16), vals)

    row_no = lax.broadcasted_iota(jnp.int32, (blk, blk), 0)
    col_no = lax.broadcasted_iota(jnp.int32, (blk, blk), 1)
    for b in range(q_blocks):
        own = own_ref[b]
        count = block_lists(ids_ref, first, key_blocks, own, seq_blocks, reach, list_ref)

        def pair(step, carry):
            tile(b, list_ref[2 * step], None)
            tile(b, list_ref[2 * step + 1], None)
            return carry

        lax.fori_loop(0, count // 2, pair, 0)

        @pl.when(count % 2 == 1)
        def _():
            tile(b, list_ref[count - 1], None)

        diagonal = find_block(ids_ref, first, key_blocks, own)

        @pl.when(diagonal >= 0)
        def _():
            tile(b, diagonal, row_no >= col_no)

        if reach < seq_blocks:
            edge = find_block(ids_ref, first, key_blocks, own - reach)

            @pl.when((edge >= 0) & (own % seq_blocks >= reach))
            def _():
                tile(b, edge, row_no < col_no)

    @pl.when(chunk == pl.num_programs(0) - 1)
    def _():
        for b in range(q_blocks):
            for h in range(heads):
                at = (slice(b * blk, (b + 1) * blk), slice(h * HD, (h + 1) * HD))
                lanes = (slice(b * blk, (b + 1) * blk), slice(h * 128, (h + 1) * 128))
                total = jnp.sum(sum_ref[lanes], axis=-1, keepdims=True)
                o_ref[at] = acc_ref[at] / total
                l_ref[lanes] = jnp.broadcast_to(total, (blk, 128))


def attend(ids, own, queries, kv_all, blk, seq_blocks):
    rows, width = queries.shape
    heads = width // HD
    total = kv_all.shape[0]
    chunk_rows = min(total, 4096)
    kernel = partial(
        attend_kernel, blk=blk, heads=heads, key_blocks=chunk_rows // blk, seq_blocks=seq_blocks,
        reach=WINDOW // blk,
    )
    whole = lambda i, *_: (0, 0)
    return pl.pallas_call(
        kernel,
        out_shape=(
            jax.ShapeDtypeStruct((rows, width), jnp.float32),
            jax.ShapeDtypeStruct((rows, heads * 128), jnp.float32),
        ),
        grid_spec=pltpu.PrefetchScalarGridSpec(
            num_scalar_prefetch=2,
            grid=(total // chunk_rows,),
            in_specs=[
                pl.BlockSpec((rows, width), whole),
                pl.BlockSpec((chunk_rows, HD), lambda i, *_: (i, 0)),
                pl.BlockSpec((chunk_rows, HD), lambda i, *_: (i, 1)),
            ],
            out_specs=[
                pl.BlockSpec((rows, width), whole),
                pl.BlockSpec((rows, heads * 128), whole),
            ],
            scratch_shapes=[
                pltpu.VMEM((rows, width), jnp.float32),
                pltpu.VMEM((rows, heads * 128), jnp.float32),
                pltpu.SMEM((chunk_rows // blk + 1,), jnp.int32),
            ],
        ),
        compiler_params=pltpu.CompilerParams(vmem_limit_bytes=40 * 2**20),
        cost_estimate=pl.CostEstimate(
            flops=4 * rows * width * total, bytes_accessed=8 * rows * width + 4 * total * HD,
            transcendentals=2 * rows * heads * total,
        ),
        name="attend",
    )(ids, own, queries, kv_all, kv_all)


def attend_back_kernel(
    ids_ref, own_ref, q_ref, do_ref, lse_ref, delta_ref, k_ref, v_ref, kt_ref, dq_ref, dkv_ref,
    dqt_ref, dk_ref, dv_ref, list_ref, *, blk, heads, key_blocks, seq_blocks, reach
):
    chunk = pl.program_id(0)
    first = chunk * key_blocks
    q_blocks = q_ref.shape[0] // blk

    @pl.when(chunk == 0)
    def _():
        dqt_ref[...] = jnp.zeros_like(dqt_ref)

    dk_ref[...] = jnp.zeros_like(dk_ref)
    dv_ref[...] = jnp.zeros_like(dv_ref)

    def tile(b, slot, mask):
        start = pl.multiple_of(slot * blk, blk)
        rows = pl.ds(start, blk)
        keys = k_ref[rows, :]
        vals = v_ref[rows, :]
        turned = kt_ref[:, rows]
        cols = slice(b * blk, (b + 1) * blk)
        dk_part = None
        for h in range(heads):
            query = q_ref[cols, h * HD : (h + 1) * HD]
            out_grad = do_ref[cols, h * HD : (h + 1) * HD]
            tangent = jnp.tanh(matmul_nt(keys, query) * (1.0 / soft_cap))
            probs = jnp.exp2(tangent * (soft_cap * LOG2E) - lse_ref[h : h + 1, cols])
            if mask is not None:
                probs = jnp.where(mask, probs, 0.0)
            prob_grad = matmul_nt(vals, out_grad)
            score = (
                probs * (prob_grad - delta_ref[h : h + 1, cols]) * (1.0 - tangent * tangent)
            ).astype(jnp.bfloat16)
            dk_new = matmul(score, query)
            dv_new = matmul(probs.astype(jnp.bfloat16), out_grad)
            dk_part = dk_new if dk_part is None else dk_part + dk_new
            dv_part = dv_new if h == 0 else dv_part + dv_new
            dqt_ref[h * HD : (h + 1) * HD, cols] += matmul(turned, score)
        dk_ref[rows, :] += dk_part
        dv_ref[rows, :] += dv_part

    key_no = lax.broadcasted_iota(jnp.int32, (blk, blk), 0)
    query_no = lax.broadcasted_iota(jnp.int32, (blk, blk), 1)
    for b in range(q_blocks):
        own = own_ref[b]
        count = block_lists(ids_ref, first, key_blocks, own, seq_blocks, reach, list_ref)

        def pair(step, carry):
            tile(b, list_ref[2 * step], None)
            tile(b, list_ref[2 * step + 1], None)
            return carry

        lax.fori_loop(0, count // 2, pair, 0)

        @pl.when(count % 2 == 1)
        def _():
            tile(b, list_ref[count - 1], None)

        diagonal = find_block(ids_ref, first, key_blocks, own)

        @pl.when(diagonal >= 0)
        def _():
            tile(b, diagonal, query_no >= key_no)

        if reach < seq_blocks:
            edge = find_block(ids_ref, first, key_blocks, own - reach)

            @pl.when((edge >= 0) & (own % seq_blocks >= reach))
            def _():
                tile(b, edge, query_no < key_no)

    dkv_ref[:, :HD] = dk_ref[...].astype(jnp.bfloat16)
    dkv_ref[:, HD:] = dv_ref[...].astype(jnp.bfloat16)

    @pl.when(chunk == pl.num_programs(0) - 1)
    def _():
        for h in range(heads):
            dq_ref[:, h * HD : (h + 1) * HD] = dqt_ref[h * HD : (h + 1) * HD, :].T


def attend_back(ids, own, queries, out_grad, lse, delta, kv_all, key_turned, blk, seq_blocks):
    rows, width = queries.shape
    heads = width // HD
    total = kv_all.shape[0]
    chunk_rows = min(total, 4096)
    kernel = partial(
        attend_back_kernel, blk=blk, heads=heads, key_blocks=chunk_rows // blk,
        seq_blocks=seq_blocks, reach=WINDOW // blk,
    )
    whole = lambda i, *_: (0, 0)
    return pl.pallas_call(
        kernel,
        out_shape=(
            jax.ShapeDtypeStruct((rows, width), jnp.float32),
            jax.ShapeDtypeStruct((total, 2 * HD), jnp.bfloat16),
        ),
        grid_spec=pltpu.PrefetchScalarGridSpec(
            num_scalar_prefetch=2,
            grid=(total // chunk_rows,),
            in_specs=[
                pl.BlockSpec((rows, width), whole),
                pl.BlockSpec((rows, width), whole),
                pl.BlockSpec((heads, rows), whole),
                pl.BlockSpec((heads, rows), whole),
                pl.BlockSpec((chunk_rows, HD), lambda i, *_: (i, 0)),
                pl.BlockSpec((chunk_rows, HD), lambda i, *_: (i, 1)),
                pl.BlockSpec((HD, chunk_rows), lambda i, *_: (0, i)),
            ],
            out_specs=[
                pl.BlockSpec((rows, width), whole),
                pl.BlockSpec((chunk_rows, 2 * HD), lambda i, *_: (i, 0)),
            ],
            scratch_shapes=[
                pltpu.VMEM((width, rows), jnp.float32),
                pltpu.VMEM((chunk_rows, HD), jnp.float32),
                pltpu.VMEM((chunk_rows, HD), jnp.float32),
                pltpu.SMEM((chunk_rows // blk + 1,), jnp.int32),
            ],
        ),
        compiler_params=pltpu.CompilerParams(vmem_limit_bytes=56 * 2**20),
        cost_estimate=pl.CostEstimate(
            flops=10 * rows * width * total, bytes_accessed=8 * rows * width + 10 * total * HD,
            transcendentals=2 * rows * heads * total,
        ),
        name="attend_back",
    )(ids, own, queries, out_grad, lse, delta, kv_all, kv_all, key_turned)


def swap(value, bit):
    pairs = [(i, i ^ bit) for i in range(lax.axis_size("ctx"))]
    return lax.ppermute(value, "ctx", pairs)


def paired():
    return lax.axis_size("ctx") == 8


def gather_relative(piece):
    half = piece.shape[0] // 2
    by_x = swap(piece, 2)
    by_y = swap(piece, 4)
    corner = (swap(by_x[:half], 4), swap(by_y[half:], 2))
    column = jnp.concatenate([piece, by_x, by_y, *corner], axis=0)
    return column, swap(column, 1)


def slots():
    return (0, 2, 4, 6, 1, 3, 5, 7)


def gather_rows(piece):
    if not paired():
        return lax.all_gather(piece, "ctx", axis=0, tiled=True)
    me = lax.axis_index("ctx")
    rows = piece.shape[0]
    column, other = gather_relative(piece)
    full = jnp.zeros((8 * rows, piece.shape[1]), piece.dtype)
    for source, base in ((column, 0), (other, 1)):
        for place, bits in enumerate((0, 2, 4, 6)):
            block = source[place * rows : (place + 1) * rows]
            full = lax.dynamic_update_slice(full, block, ((me ^ (bits + base)) * rows, 0))
    return full


def scatter_quads(own, by_x, by_y, corner):
    half = own.shape[0] // 2
    from_x = swap(corner[:half], 2)
    from_y = swap(corner[half:], 4)
    by_y = jnp.concatenate([by_y[:half] + from_x, by_y[half:]], axis=0)
    by_x = jnp.concatenate([by_x[:half], by_x[half:] + from_y], axis=0)
    last_x = swap(by_x, 2)
    last_y = swap(by_y, 4)
    return (
        own.astype(jnp.float32) + last_x.astype(jnp.float32) + last_y.astype(jnp.float32)
    )


def scatter_rows(whole):
    if not paired():
        return lax.psum_scatter(whole, "ctx", scatter_dimension=0, tiled=True).astype(jnp.float32)
    me = lax.axis_index("ctx")
    chip, core = me // 2, me % 2
    rows = whole.shape[0] // 8
    blocks = whole.reshape(4, 2, rows, whole.shape[1])
    theirs = lax.dynamic_index_in_dim(blocks, 1 - core, 1, keepdims=False)
    mine = lax.dynamic_index_in_dim(blocks, core, 1, keepdims=False)
    mine = mine + swap(theirs, 1)
    pick = lambda bits: lax.dynamic_index_in_dim(mine, chip ^ bits, 0, keepdims=False)
    return scatter_quads(pick(0), pick(1), pick(2), pick(3))


def scatter_relative(whole):
    rows = whole.shape[0] // 8
    mine = whole[: 4 * rows] + swap(whole[4 * rows :], 1)
    return scatter_quads(*(mine[k * rows : (k + 1) * rows] for k in range(4)))


def gather_gains(piece):
    if not paired():
        return lax.all_gather(piece, "ctx", axis=1, tiled=True)
    me = lax.axis_index("ctx")
    stack = piece[None]
    for bit in (1, 2, 4):
        other = swap(stack, bit)
        low = (me & bit) == 0
        stack = jnp.where(
            low, jnp.concatenate([stack, other], axis=0), jnp.concatenate([other, stack], axis=0)
        )
    return stack.transpose(1, 0, 2).reshape(piece.shape[0], 8 * piece.shape[1])


def scatter_gains(whole):
    if not paired():
        return lax.psum_scatter(
            whole.astype(jnp.bfloat16), "ctx", scatter_dimension=1, tiled=True
        ).astype(jnp.float32)
    me = lax.axis_index("ctx")
    columns = whole.shape[1] // 8
    stack = whole.reshape(whole.shape[0], 8, columns).transpose(1, 0, 2)
    for bit in (4, 2, 1):
        half = stack.shape[0] // 2
        low = (me & bit) == 0
        theirs = jnp.where(low, stack[half:], stack[:half])
        mine = jnp.where(low, stack[:half], stack[half:])
        stack = mine + swap(theirs, bit)
    return stack[0]


def body(
    tokens, block_map, w_query, w_key, w_value, w_out, w_gate, w_up, w_down, norm_gains, cotangent
):
    ctx_count = lax.axis_size("ctx")
    tok_dev = tokens.shape[0]
    block_rows = tok_dev // 2
    seq_count = max(1, ctx_count // 16)
    seq_len = tok_dev * ctx_count // seq_count
    seq_blocks = seq_len // block_rows
    me = lax.axis_index("ctx")
    heads_dev = w_query.shape[1] // HD
    own_ids = lax.dynamic_index_in_dim(block_map, me, 0, keepdims=False)
    offsets = jnp.arange(block_rows, dtype=jnp.int32)
    own_index = (own_ids[:, None] * block_rows + offsets[None, :]).reshape(-1)
    cosine, sine_table = angle_tables(own_index % seq_len)
    head_cos = cosine[:, None, :]
    head_sin = sine_table[:, None, :]

    full_gains = gather_gains(norm_gains)
    gains = full_gains.astype(jnp.float32)
    full_qkv = gather_rows(jnp.concatenate([w_query, w_key, w_value], axis=1))
    q_width = heads_dev * HD
    inputs = tokens.astype(jnp.float32)
    in_scale = rms_scale(inputs)
    normed_in = (inputs * in_scale * gains[0]).astype(jnp.bfloat16)
    projected = matmul(normed_in, full_qkv)
    query_raw = projected[:, :q_width].reshape(tok_dev, heads_dev, HD)
    key_raw = projected[:, q_width : q_width + HD]
    value_raw = projected[:, q_width + HD :]
    queries = (rotate(query_raw, head_cos, head_sin) * HD ** (-0.5)).astype(jnp.bfloat16)
    queries = queries.reshape(tok_dev, q_width)
    key_rows = rotate(key_raw, cosine, sine_table).astype(jnp.bfloat16)
    kv_local = jnp.concatenate([key_rows, value_raw.astype(jnp.bfloat16)], axis=-1)

    w_out = tie(w_out, full_qkv)
    full_out_t = gather_rows(w_out.T)
    if paired():
        column, other = gather_relative(kv_local)
        kv_all = jnp.concatenate([column, other], axis=0)
        key_ids = jnp.concatenate(
            [lax.dynamic_index_in_dim(block_map, me ^ k, 0, keepdims=False) for k in slots()]
        )
    else:
        kv_all = lax.all_gather(kv_local, "ctx", axis=0, tiled=True)
        key_ids = block_map.reshape(-1)
    w_gate, w_up, w_down, kv_all = lax.optimization_barrier((w_gate, w_up, w_down, kv_all))
    full_gate = lax.all_gather(w_gate, "ctx", axis=0, tiled=True)
    full_up = gather_rows(w_up)
    full_down = lax.all_gather(w_down, "ctx", axis=1, tiled=True)

    attended, totals = attend(key_ids, own_ids, queries, kv_all, block_rows, seq_blocks)
    attn_flat = attended.astype(jnp.bfloat16)
    branch_part = matmul_nt(attn_flat, full_out_t).astype(jnp.bfloat16)
    branch = lax.psum(branch_part, "tp")
    branch, full_gate, full_up = lax.optimization_barrier((branch, full_gate, full_up))
    branch = branch.astype(jnp.float32)
    branch_scale = rms_scale(branch)
    residual = inputs + branch * branch_scale * gains[1]
    resid_scale = rms_scale(residual)
    normed_mid = (residual * resid_scale * gains[2]).astype(jnp.bfloat16)
    gate_pre = matmul(normed_mid, full_gate)
    up_pre = matmul(normed_mid, full_up)
    active, gelu_back = jax.vjp(partial(jax.nn.gelu, approximate=True), gate_pre)
    hidden = (active * up_pre).astype(jnp.bfloat16)
    mlp_out = lax.psum(matmul(hidden, full_down).astype(jnp.bfloat16), "tp").astype(jnp.float32)
    mlp_scale = rms_scale(mlp_out)
    result = (residual + mlp_out * mlp_scale * gains[3]).astype(jnp.bfloat16)
    out_grad = cotangent.astype(jnp.float32)
    mlp_grad, gain_four = norm_back(mlp_out, mlp_scale, gains[3], out_grad)
    mlp_low = mlp_grad.astype(jnp.bfloat16)
    hidden_grad = matmul(mlp_low, full_down.T)
    gate_low = gelu_back(hidden_grad * up_pre)[0].astype(jnp.bfloat16)
    up_low = (hidden_grad * active).astype(jnp.bfloat16)
    mid_part = (matmul(gate_low, full_gate.T) + matmul(up_low, full_up.T)).astype(jnp.bfloat16)
    mid_part, hidden_t, mlp_t, gate_t, up_t = lax.optimization_barrier(
        (mid_part, hidden, mlp_low, gate_low, up_low)
    )
    mid_sum = lax.psum(mid_part, "tp")
    down_grad = matmul(hidden_t.T, mlp_t).astype(jnp.bfloat16)
    down_shard = lax.psum_scatter(down_grad, "ctx", scatter_dimension=1, tiled=True)
    gate_grad = matmul(normed_mid.T, gate_t).astype(jnp.bfloat16)
    gate_shard = scatter_rows(gate_grad)
    up_grad = matmul(normed_mid.T, up_t).astype(jnp.bfloat16)
    key_turned = kv_all[:, :HD].T
    log_total = jnp.log2(totals.reshape(tok_dev, heads_dev, 128)[:, :, 0]).T
    mid_sum, up_grad, key_turned, gate_shard = lax.optimization_barrier(
        (mid_sum, up_grad, key_turned, gate_shard)
    )
    mid_grad = mid_sum.astype(jnp.float32)
    up_shard = lax.psum_scatter(up_grad, "ctx", scatter_dimension=0, tiled=True)
    resid_part, gain_three = norm_back(residual, resid_scale, gains[2], mid_grad)
    resid_grad = out_grad + resid_part
    branch_grad, gain_two = norm_back(branch, branch_scale, gains[1], resid_grad)
    branch_low = branch_grad.astype(jnp.bfloat16)
    attn_grad = matmul(branch_low, full_out_t)
    attn_grad_low = attn_grad.astype(jnp.bfloat16)
    row_dot = jnp.sum(
        (attn_grad_low.astype(jnp.float32) * attended).reshape(tok_dev, heads_dev, HD), axis=-1
    ).T
    query_grad, kv_terms = attend_back(
        key_ids, own_ids, queries, attn_grad_low, log_total, row_dot, kv_all, key_turned,
        block_rows, seq_blocks,
    )
    kv_terms, down_shard = lax.optimization_barrier((kv_terms, down_shard))
    down_shard = down_shard.astype(jnp.float32)
    if paired():
        kv_grad = scatter_relative(kv_terms)
    else:
        kv_grad = lax.psum_scatter(
            kv_terms, "ctx", scatter_dimension=0, tiled=True
        ).astype(jnp.float32)
    key_low = unrotate(kv_grad[:, :HD], cosine, sine_table).astype(jnp.bfloat16)
    value_low = kv_grad[:, HD:].astype(jnp.bfloat16)
    query_low = (
        unrotate(query_grad.reshape(tok_dev, heads_dev, HD) * HD ** (-0.5), head_cos, head_sin)
        .astype(jnp.bfloat16)
        .reshape(tok_dev, q_width)
    )
    qkv_low = jnp.concatenate([query_low, key_low, value_low], axis=1)
    in_part = matmul(qkv_low, full_qkv.T).astype(jnp.bfloat16)
    in_part, qkv_low, branch_t = lax.optimization_barrier((in_part, qkv_low, branch_low))
    in_sum = lax.psum(in_part, "tp")
    qkv_grad = matmul(normed_in.T, qkv_low).astype(jnp.bfloat16)
    qkv_shard = scatter_rows(qkv_grad)
    out_weight_grad = matmul(branch_t.T, attn_flat).astype(jnp.bfloat16)
    out_shard = scatter_rows(out_weight_grad)
    in_sum, out_shard, up_shard, qkv_shard = lax.optimization_barrier(
        (in_sum, out_shard, up_shard, qkv_shard)
    )
    in_grad = in_sum.astype(jnp.float32)
    input_part, gain_one = norm_back(inputs, in_scale, gains[0], in_grad)
    input_grad = resid_grad + input_part
    gain_grads = jnp.stack([gain_one, gain_two, gain_three, gain_four])
    gains_shard = scatter_gains(gain_grads)
    return (
        result,
        input_grad,
        qkv_shard[:, :q_width],
        qkv_shard[:, q_width : q_width + HD],
        qkv_shard[:, q_width + HD :],
        out_shard.T,
        gate_shard,
        up_shard.astype(jnp.float32),
        down_shard,
        gains_shard,
    )


def solution(mesh):
    in_specs = (
        P("ctx", None),
        P(),
        P("ctx", "tp"),
        P("ctx", "tp"),
        P("ctx", "tp"),
        P("tp", "ctx"),
        P("ctx", "tp"),
        P("ctx", "tp"),
        P("tp", "ctx"),
        P(None, "ctx"),
        P("ctx", None),
    )
    out_specs = (
        P("ctx", None),
        P("ctx", None),
        P("ctx", "tp"),
        P("ctx", "tp"),
        P("ctx", "tp"),
        P("tp", "ctx"),
        P("ctx", "tp"),
        P("ctx", "tp"),
        P("tp", "ctx"),
        P(None, "ctx"),
    )
    return jax.shard_map(body, mesh=mesh, in_specs=in_specs, out_specs=out_specs, check_vma=False)
```

```python
from functools import partial

import jax
import jax.numpy as jnp
from jax import lax
from jax.experimental import pallas as pl
from jax.experimental.pallas import tpu as pltpu
from jax.sharding import PartitionSpec as P

HD = 256
HALF = 128
WINDOW = 4096
KEY_CHUNK = 4096


epsilon = 1e-06
soft_cap = 50.0
LOG2E = 1.4426950408889634


def rms_scale(values):
    return lax.rsqrt(jnp.mean(values * values, axis=-1, keepdims=True) + epsilon)


def angle_tables(positions):
    frequency = jnp.power(10000.0, -2.0 * jnp.arange(HALF, dtype=jnp.float32) / HD)
    phases = positions.astype(jnp.float32)[:, None] * frequency[None, :]
    return (jnp.cos(phases), jnp.sin(phases))


def matmul(left, right):
    return jnp.dot(left, right, preferred_element_type=jnp.float32)


def matmul_nt(left, right):
    return lax.dot_general(left, right, (((1,), (1,)), ((), ())), preferred_element_type=jnp.float32)


def tie(value, *others):
    return lax.optimization_barrier((value,) + others)[0]


def call(kernel, out_shape, args, name, scalars=0, scratch=(), flops=0, mem=60, space=None):
    spec = pl.BlockSpec(memory_space=pltpu.VMEM if space is None else space)
    outs = jax.tree.map(lambda _: spec, out_shape)
    size = sum(a.size * a.dtype.itemsize for a in args)
    size += sum(a.size * a.dtype.itemsize for a in jax.tree.leaves(out_shape))
    return pl.pallas_call(
        kernel,
        out_shape=out_shape,
        in_specs=[pl.BlockSpec(memory_space=pltpu.SMEM)] * scalars + [spec] * (len(args) - scalars),
        out_specs=outs,
        scratch_shapes=list(scratch),
        compiler_params=pltpu.CompilerParams(vmem_limit_bytes=mem * 2**20),
        cost_estimate=pl.CostEstimate(flops=flops, bytes_accessed=size, transcendentals=0),
        name=name,
    )(*args)


def swap(value, bit):
    pairs = [(i, i ^ bit) for i in range(lax.axis_size("ctx"))]
    return lax.ppermute(value, "ctx", pairs)


def paired():
    return lax.axis_size("ctx") == 8


def nearby(piece):
    return swap(piece, 2), swap(piece, 4)


def gather_pieces(piece, near=None):
    half = piece.shape[0] // 2
    by_x, by_y = nearby(piece) if near is None else near
    mine = (piece, by_x, by_y, swap(by_x[:half], 4), swap(by_y[half:], 2))
    return mine + tuple(swap(part, 1) for part in mine)


def piece_rows(rows):
    me = lax.axis_index("ctx")
    places = [(me ^ bit) * rows for bit in (0, 2, 4, 6, 6, 1, 3, 5, 7, 7)]
    shift = [0, 0, 0, 0, rows // 2] * 2
    return jnp.stack(places).astype(jnp.int32) + jnp.array(shift, jnp.int32)


def assemble_kernel(rows_ref, *refs):
    *pieces, whole, sems = refs
    copies = []
    for k, piece in enumerate(pieces):
        first = pl.multiple_of(rows_ref[k], 16)
        copy = pltpu.make_async_copy(piece, whole.at[pl.ds(first, piece.shape[0])], sems.at[k])
        copy.start()
        copies.append(copy)
    for copy in copies:
        copy.wait()


def assemble(pieces):
    rows, width = pieces[0].shape
    shape = jax.ShapeDtypeStruct((8 * rows, width), pieces[0].dtype)
    return call(
        assemble_kernel, shape, (piece_rows(rows), *pieces), "assemble", scalars=1,
        scratch=[pltpu.SemaphoreType.DMA((len(pieces),))], space=pl.ANY,
    )


def scatter_corner(own, by_x, by_y, corner):
    half = own.shape[0] // 2
    from_x = swap(corner[:half], 2)
    from_y = swap(corner[half:], 4)
    by_y = jnp.concatenate([by_y[:half] + from_x, by_y[half:]], axis=0)
    by_x = jnp.concatenate([by_x[:half], by_x[half:] + from_y], axis=0)
    return own, by_x, by_y


def scatter_start(whole):
    if not paired():
        return (lax.psum_scatter(whole, "ctx", scatter_dimension=0, tiled=True),)
    me = lax.axis_index("ctx")
    chip, core = me // 2, me % 2
    rows = whole.shape[0] // 8
    blocks = whole.reshape(4, 2, rows, whole.shape[1])
    theirs = lax.dynamic_index_in_dim(blocks, 1 - core, 1, keepdims=False)
    mine = lax.dynamic_index_in_dim(blocks, core, 1, keepdims=False)
    mine = mine + swap(theirs, 1)
    pick = lambda bits: lax.dynamic_index_in_dim(mine, chip ^ bits, 0, keepdims=False)
    return scatter_corner(pick(0), pick(1), pick(2), pick(3))


def scatter_finish(blocks):
    if len(blocks) == 1:
        return blocks
    own, by_x, by_y = blocks
    return own, swap(by_x, 2), swap(by_y, 4)


def add_terms(terms):
    total = terms[0].astype(jnp.float32)
    for term in terms[1:]:
        total = total + term.astype(jnp.float32)
    return total


def gather_gains(piece):
    if not paired():
        return lax.all_gather(piece, "ctx", axis=1, tiled=True)
    me = lax.axis_index("ctx")

    def ordered(bit, mine, other):
        low = (me & bit) == 0
        return jnp.concatenate([jnp.where(low, mine, other), jnp.where(low, other, mine)], axis=0)

    chip = ordered(1, piece[None], swap(piece[None], 1))
    row = ordered(2, chip, swap(chip, 2))
    stack = ordered(4, row, ordered(2, swap(chip, 4), swap(chip, 6)))
    return stack.transpose(1, 0, 2).reshape(piece.shape[0], 8 * piece.shape[1])


def scatter_gains(whole):
    if not paired():
        return lax.psum_scatter(whole, "ctx", scatter_dimension=1, tiled=True)
    me = lax.axis_index("ctx")
    columns = whole.shape[1] // 8
    stack = whole.reshape(whole.shape[0], 8, columns).transpose(1, 0, 2)
    for bit in (4, 2, 1):
        half = stack.shape[0] // 2
        low = (me & bit) == 0
        theirs = jnp.where(low, stack[half:], stack[:half])
        mine = jnp.where(low, stack[:half], stack[half:])
        stack = mine + swap(theirs, bit)
    return stack[0]


def sum_small_tp(value):
    count = lax.axis_size("tp")
    bit = 1
    while bit < count:
        value = value + lax.ppermute(value, "tp", [(i, i ^ bit) for i in range(count)])
        bit *= 2
    return value


def pack_kernel(a_ref, b_ref, c_ref, out_ref):
    one, two = a_ref.shape[1], a_ref.shape[1] + b_ref.shape[1]
    out_ref[:, :one] = a_ref[...]
    out_ref[:, one:two] = b_ref[...]
    out_ref[:, two:] = c_ref[...]


def pack(first, second, third):
    width = first.shape[1] + second.shape[1] + third.shape[1]
    shape = jax.ShapeDtypeStruct((first.shape[0], width), first.dtype)
    return call(pack_kernel, shape, (first, second, third), "pack")


def place(rows_ref, pieces, whole_ref):
    for k, piece in enumerate(pieces):
        whole_ref[pl.ds(pl.multiple_of(rows_ref[k], 16), piece.shape[0]), :] = piece[...]


def project_kernel(rows_ref, in_ref, cos_ref, sin_ref, *refs, heads, parts):
    pieces, (q_ref, kv_ref) = refs[:parts], refs[parts : parts + 2]
    if parts > 1:
        full_ref = refs[parts + 2]
        place(rows_ref, pieces, full_ref)
    else:
        full_ref = pieces[0]
    for n in range(heads + 2):
        raw = matmul(in_ref[...], full_ref[:, n * HD : (n + 1) * HD])
        if n <= heads:
            low, high = raw[:, :HALF], raw[:, HALF:]
            cosine, sine = cos_ref[...], sin_ref[...]
            low, high = low * cosine - high * sine, high * cosine + low * sine
            if n < heads:
                q_ref[:, n * HD : n * HD + HALF] = (low * HD ** (-0.5)).astype(jnp.bfloat16)
                q_ref[:, n * HD + HALF : (n + 1) * HD] = (high * HD ** (-0.5)).astype(jnp.bfloat16)
            else:
                kv_ref[:, :HALF] = low.astype(jnp.bfloat16)
                kv_ref[:, HALF:HD] = high.astype(jnp.bfloat16)
        else:
            kv_ref[:, HD:] = raw.astype(jnp.bfloat16)


def project(normed, cosine, sine, pieces, heads):
    rows, depth = normed.shape
    width = pieces[0].shape[1]
    low = lambda n: jax.ShapeDtypeStruct((rows, n), jnp.bfloat16)
    shapes = [low(heads * HD), low(2 * HD)]
    if len(pieces) > 1:
        shapes.append(jax.ShapeDtypeStruct((depth, width), jnp.bfloat16))
        places = piece_rows(pieces[0].shape[0])
    else:
        places = jnp.zeros((1,), jnp.int32)
    found = call(
        partial(project_kernel, heads=heads, parts=len(pieces)), tuple(shapes),
        (places, normed, cosine, sine, *pieces), "project", scalars=1,
        flops=2 * rows * depth * width,
    )
    return found if len(pieces) > 1 else (*found, pieces[0])


def out_project_kernel(rows_ref, attn_ref, *refs, parts):
    pieces, branch_ref = refs[:parts], refs[parts]
    if parts > 1:
        full_ref = refs[parts + 1]
        place(rows_ref, pieces, full_ref)
    else:
        full_ref = pieces[0]
    for n in range(0, branch_ref.shape[1], 256):
        part = matmul_nt(attn_ref[...], full_ref[n : n + 256, :])
        branch_ref[:, n : n + 256] = part.astype(jnp.bfloat16)


def out_project(attn, pieces, depth):
    rows, width = attn.shape
    shapes = [jax.ShapeDtypeStruct((rows, depth), jnp.bfloat16)]
    if len(pieces) > 1:
        shapes.append(jax.ShapeDtypeStruct((depth, width), jnp.bfloat16))
        places = piece_rows(pieces[0].shape[0])
    else:
        places = jnp.zeros((1,), jnp.int32)
    found = call(
        partial(out_project_kernel, parts=len(pieces)), tuple(shapes), (places, attn, *pieces),
        "out_project", scalars=1, flops=2 * rows * depth * width,
    )
    return found if len(pieces) > 1 else (*found, pieces[0])


def join_kernel(cos_ref, sin_ref, query_ref, full_ref, *refs):
    *terms, low_ref, part_ref = refs
    total = terms[0][...].astype(jnp.float32)
    for term in terms[1:]:
        total = total + term[...].astype(jnp.float32)
    width = query_ref.shape[1]
    cosine, sine = cos_ref[...], sin_ref[...]
    low, high = total[:, :HALF], total[:, HALF:HD]
    low_ref[:, :width] = query_ref[...]
    low_ref[:, width : width + HALF] = (low * cosine + high * sine).astype(jnp.bfloat16)
    low_ref[:, width + HALF : width + HD] = (high * cosine - low * sine).astype(jnp.bfloat16)
    low_ref[:, width + HD :] = total[:, HD:].astype(jnp.bfloat16)
    for n in range(0, part_ref.shape[1], 256):
        part = matmul_nt(low_ref[...], full_ref[n : n + 256, :])
        part_ref[:, n : n + 256] = part.astype(jnp.bfloat16)


def join(cosine, sine, query_low, full_qkv, terms):
    rows = query_low.shape[0]
    depth, width = full_qkv.shape
    low = lambda n: jax.ShapeDtypeStruct((rows, n), jnp.bfloat16)
    return call(
        join_kernel, (low(width), low(depth)), (cosine, sine, query_low, full_qkv, *terms), "join",
        flops=2 * rows * depth * width,
    )


GROUP = 16


def rms_of(values):
    return lax.rsqrt(jnp.mean(values * values, axis=-1, keepdims=True) + epsilon)


def norm_back(normed, scale, weighted):
    return scale * (weighted - normed * jnp.mean(weighted * normed, axis=-1, keepdims=True))


def fold(values):
    total = values[:8]
    for row in range(8, values.shape[0], 8):
        total = total + values[row : row + 8]
    return total


def wide(ref, rows):
    return ref[rows, :].astype(jnp.float32)


def walk(count, step):
    def run(index, carry):
        step(pl.ds(pl.multiple_of(index * GROUP, GROUP), GROUP))
        return carry

    lax.fori_loop(0, count // GROUP, run, 0, unroll=2)


def mid_kernel(tok_ref, branch_ref, gains_ref, out_ref):
    def step(rows):
        branch = wide(branch_ref, rows)
        residual = wide(tok_ref, rows) + branch * rms_of(branch) * gains_ref[1:2, :]
        out_ref[rows, :] = (residual * rms_of(residual) * gains_ref[2:3, :]).astype(jnp.bfloat16)

    walk(tok_ref.shape[0], step)


def top_kernel(tok_ref, branch_ref, mlp_ref, cot_ref, gains_ref, out_ref, grad_ref, sum_ref, acc_ref):
    @pl.when(pl.program_id(0) == 0)
    def _():
        acc_ref[...] = jnp.zeros_like(acc_ref)

    def step(rows):
        branch = wide(branch_ref, rows)
        residual = wide(tok_ref, rows) + branch * rms_of(branch) * gains_ref[1:2, :]
        mlp = wide(mlp_ref, rows)
        scale = rms_of(mlp)
        normed = mlp * scale
        out_ref[rows, :] = (residual + normed * gains_ref[3:4, :]).astype(jnp.bfloat16)
        out_grad = wide(cot_ref, rows)
        acc_ref[...] += fold(out_grad * normed)
        grad_ref[rows, :] = norm_back(normed, scale, out_grad * gains_ref[3:4, :]).astype(jnp.bfloat16)

    walk(tok_ref.shape[0], step)

    @pl.when(pl.program_id(0) == pl.num_programs(0) - 1)
    def _():
        sum_ref[...] = jnp.sum(acc_ref[...], axis=0, keepdims=True)


def low_kernel(
    tok_ref, branch_ref, mid_ref, cot_ref, gains_ref, resid_ref, grad_ref, sum_ref, acc_ref
):
    @pl.when(pl.program_id(0) == 0)
    def _():
        acc_ref[...] = jnp.zeros_like(acc_ref)

    def step(rows):
        branch = wide(branch_ref, rows)
        branch_scale = rms_of(branch)
        branch_normed = branch * branch_scale
        residual = wide(tok_ref, rows) + branch_normed * gains_ref[1:2, :]
        scale = rms_of(residual)
        normed = residual * scale
        mid_grad = wide(mid_ref, rows)
        acc_ref[:8, :] += fold(mid_grad * normed)
        grad = wide(cot_ref, rows) + norm_back(normed, scale, mid_grad * gains_ref[2:3, :])
        resid_ref[rows, :] = grad
        acc_ref[8:, :] += fold(grad * branch_normed)
        grad_ref[rows, :] = norm_back(
            branch_normed, branch_scale, grad * gains_ref[1:2, :]
        ).astype(jnp.bfloat16)

    walk(tok_ref.shape[0], step)

    @pl.when(pl.program_id(0) == pl.num_programs(0) - 1)
    def _():
        sum_ref[0:1, :] = jnp.sum(acc_ref[:8, :], axis=0, keepdims=True)
        sum_ref[1:2, :] = jnp.sum(acc_ref[8:, :], axis=0, keepdims=True)


def end_kernel(tok_ref, sum_ref, resid_ref, gains_ref, out_ref):
    def step(rows):
        values = wide(tok_ref, rows)
        scale = rms_of(values)
        weighted = wide(sum_ref, rows) * gains_ref[0:1, :]
        out_ref[rows, :] = resid_ref[rows, :] + norm_back(values * scale, scale, weighted)

    walk(tok_ref.shape[0], step)


def by_rows(kernel, args, gains, kinds, sums, name, block=128):
    rows, depth = args[0].shape
    tile = pl.BlockSpec((block, depth), lambda i: (i, 0))
    whole = lambda n: pl.BlockSpec((n, depth), lambda i: (0, 0))
    shapes = [jax.ShapeDtypeStruct((rows, depth), kind) for kind in kinds]
    out_specs = [tile] * len(kinds)
    scratch = []
    if sums:
        shapes.append(jax.ShapeDtypeStruct((sums, depth), jnp.float32))
        out_specs.append(whole(sums))
        scratch.append(pltpu.VMEM((8 * sums, depth), jnp.float32))
    size = sum(a.size * a.dtype.itemsize for a in (*args, *shapes))
    found = pl.pallas_call(
        kernel,
        out_shape=tuple(shapes),
        grid=(rows // block,),
        in_specs=[tile] * len(args) + [whole(gains.shape[0])],
        out_specs=out_specs,
        scratch_shapes=scratch,
        compiler_params=pltpu.CompilerParams(vmem_limit_bytes=60 * 2**20),
        cost_estimate=pl.CostEstimate(flops=0, bytes_accessed=size, transcendentals=0),
        name=name,
    )(*args, gains)
    return found if len(found) > 1 else found[0]


UNITS = 256


def units_kernel(in_ref, gate_ref, up_ref, hidden_ref, active_ref, slope_ref):
    gate = matmul(in_ref[...], gate_ref[...])
    up = matmul(in_ref[...], up_ref[...])
    root = (2.0 / jnp.pi) ** 0.5
    square = gate * gate
    bend = jnp.tanh(root * gate * (1.0 + 0.044715 * square))
    half = 0.5 * (1.0 + bend)
    active = gate * half
    slope = half + 0.5 * gate * (1.0 - bend * bend) * (root * (1.0 + 3 * 0.044715 * square))
    hidden_ref[...] = (active * up).astype(jnp.bfloat16)
    active_ref[...] = active.astype(jnp.bfloat16)
    slope_ref[...] = (slope * up).astype(jnp.bfloat16)


def units(normed, full_gate, full_up):
    rows, depth = normed.shape
    count = full_gate.shape[1]
    column = lambda n: pl.BlockSpec((n, UNITS), lambda i: (0, i))
    return pl.pallas_call(
        units_kernel,
        out_shape=tuple(jax.ShapeDtypeStruct((rows, count), jnp.bfloat16) for _ in range(3)),
        grid=(count // UNITS,),
        in_specs=[pl.BlockSpec((rows, depth), lambda i: (0, 0)), column(depth), column(depth)],
        out_specs=[column(rows)] * 3,
        compiler_params=pltpu.CompilerParams(vmem_limit_bytes=60 * 2**20),
        cost_estimate=pl.CostEstimate(
            flops=4 * rows * depth * count, bytes_accessed=4 * depth * count,
            transcendentals=rows * count,
        ),
        name="units",
    )(normed, full_gate, full_up)


def down_kernel(hidden_ref, down_ref, out_ref):
    out_ref[...] = matmul_nt(hidden_ref[...], down_ref[...]).astype(jnp.bfloat16)


def project_down(hidden, full_down_t):
    rows, count = hidden.shape
    depth = full_down_t.shape[0]
    return pl.pallas_call(
        down_kernel,
        out_shape=jax.ShapeDtypeStruct((rows, depth), jnp.bfloat16),
        grid=(depth // UNITS,),
        in_specs=[
            pl.BlockSpec((rows, count), lambda i: (0, 0)),
            pl.BlockSpec((UNITS, count), lambda i: (i, 0)),
        ],
        out_specs=pl.BlockSpec((rows, UNITS), lambda i: (0, i)),
        compiler_params=pltpu.CompilerParams(vmem_limit_bytes=60 * 2**20),
        cost_estimate=pl.CostEstimate(
            flops=2 * rows * depth * count, bytes_accessed=2 * depth * count, transcendentals=0
        ),
        name="project_down",
    )(hidden, full_down_t)


def units_back_kernel(
    grad_ref, down_ref, gate_ref, up_ref, active_ref, slope_ref, dg_ref, du_ref, out_ref, acc_ref
):
    @pl.when(pl.program_id(0) == 0)
    def _():
        acc_ref[...] = jnp.zeros_like(acc_ref)

    hidden_grad = matmul(grad_ref[...], down_ref[...])
    gate_low = (hidden_grad * slope_ref[...].astype(jnp.float32)).astype(jnp.bfloat16)
    up_low = (hidden_grad * active_ref[...].astype(jnp.float32)).astype(jnp.bfloat16)
    dg_ref[...] = gate_low
    du_ref[...] = up_low
    for n in range(0, acc_ref.shape[1], 256):
        acc_ref[:, n : n + 256] += matmul_nt(gate_low, gate_ref[n : n + 256, :]) + matmul_nt(
            up_low, up_ref[n : n + 256, :]
        )

    @pl.when(pl.program_id(0) == pl.num_programs(0) - 1)
    def _():
        out_ref[...] = acc_ref[...].astype(jnp.bfloat16)


def units_back(mlp_low, full_down_t, full_gate, full_up, active, slope):
    rows, depth = mlp_low.shape
    count = active.shape[1]
    column = lambda n: pl.BlockSpec((n, UNITS), lambda i: (0, i))
    whole = pl.BlockSpec((rows, depth), lambda i: (0, 0))
    low = lambda n: jax.ShapeDtypeStruct((rows, n), jnp.bfloat16)
    return pl.pallas_call(
        units_back_kernel,
        out_shape=(low(count), low(count), low(depth)),
        grid=(count // UNITS,),
        in_specs=[whole, column(depth), column(depth), column(depth), column(rows), column(rows)],
        out_specs=[column(rows), column(rows), whole],
        scratch_shapes=[pltpu.VMEM((rows, depth), jnp.float32)],
        compiler_params=pltpu.CompilerParams(vmem_limit_bytes=60 * 2**20),
        cost_estimate=pl.CostEstimate(
            flops=6 * rows * depth * count, bytes_accessed=6 * depth * count, transcendentals=0
        ),
        name="units_back",
    )(mlp_low, full_down_t, full_gate, full_up, active, slope)


def slot_block(map_ref, me, slot, swapped):
    device = slot >> 1
    if swapped:
        device = me ^ (((device & 3) << 1) | (device >> 2))
    return map_ref[device * 2 + (slot & 1)]


def block_list(lookup, key_blocks, own, seq_blocks, reach, list_ref):
    def look(slot, count):
        other = lookup(slot)
        gap = own - other
        whole = (gap > 0) & (gap < reach) & (own // seq_blocks == other // seq_blocks)
        list_ref[count] = slot
        return count + whole.astype(jnp.int32)

    return lax.fori_loop(0, key_blocks, look, jnp.int32(0))


def find_block(lookup, key_blocks, wanted):
    def look(slot, found):
        return jnp.where(lookup(slot) == wanted, slot, found)

    return lax.fori_loop(0, key_blocks, look, jnp.int32(-1))


def visit_blocks(map_ref, me, chunk, q_blocks, key_blocks, seq_blocks, reach, swapped, list_ref, tile, blk, keys_first):
    first = chunk * key_blocks
    lookup = lambda slot: slot_block(map_ref, me, first + slot, swapped)
    row_no = lax.broadcasted_iota(jnp.int32, (blk, blk), 0)
    col_no = lax.broadcasted_iota(jnp.int32, (blk, blk), 1)
    query_no, key_no = (col_no, row_no) if keys_first else (row_no, col_no)
    for b in range(q_blocks):
        own = map_ref[me * q_blocks + b]
        count = block_list(lookup, key_blocks, own, seq_blocks, reach, list_ref)

        def pair(step, carry):
            tile(b, list_ref[2 * step], None)
            tile(b, list_ref[2 * step + 1], None)
            return carry

        lax.fori_loop(0, count // 2, pair, 0)

        @pl.when(count % 2 == 1)
        def _():
            tile(b, list_ref[count - 1], None)

        diagonal = find_block(lookup, key_blocks, own)

        @pl.when(diagonal >= 0)
        def _():
            tile(b, diagonal, query_no >= key_no)

        if reach < seq_blocks:
            edge = find_block(lookup, key_blocks, own - reach)

            @pl.when((edge >= 0) & (own % seq_blocks >= reach))
            def _():
                tile(b, edge, query_no < key_no)


def attend_kernel(
    map_ref, me_ref, q_ref, *refs, blk, heads, parts, key_blocks, seq_blocks, reach
):
    pieces = refs[:parts]
    o_ref, low_ref, l_ref = refs[parts : parts + 3]
    chunk = pl.program_id(0)
    if parts > 1:
        kv_ref = refs[parts + 3]
        row = 0
        for piece in pieces:
            kv_ref[row : row + piece.shape[0], :] = piece[...]
            row += piece.shape[0]
    else:
        kv_ref = pieces[0]
    acc_ref, sum_ref, list_ref = refs[-3:]
    q_blocks = q_ref.shape[0] // blk

    @pl.when(chunk == 0)
    def _():
        acc_ref[...] = jnp.zeros_like(acc_ref)
        sum_ref[...] = jnp.zeros_like(sum_ref)

    def tile(b, slot, mask):
        rows = pl.ds(pl.multiple_of(slot * blk, blk), blk)
        keys = kv_ref[rows, :HD]
        vals = kv_ref[rows, HD:]
        for h in range(heads):
            query = q_ref[b * blk : (b + 1) * blk, h * HD : (h + 1) * HD]
            capped = jnp.tanh(matmul_nt(query, keys) * (1.0 / soft_cap))
            weights = jnp.exp2(capped * (soft_cap * LOG2E))
            if mask is not None:
                weights = jnp.where(mask, weights, 0.0)
            at = (slice(b * blk, (b + 1) * blk), slice(h * HD, (h + 1) * HD))
            lanes = (slice(b * blk, (b + 1) * blk), slice(h * 128, (h + 1) * 128))
            part = weights[:, :128]
            for piece in range(1, blk // 128):
                part = part + weights[:, piece * 128 : (piece + 1) * 128]
            sum_ref[lanes] += part
            acc_ref[at] += matmul(weights.astype(jnp.bfloat16), vals)

    visit_blocks(
        map_ref, me_ref[0], chunk, q_blocks, key_blocks, seq_blocks, reach, parts > 1, list_ref,
        tile, blk, False,
    )

    @pl.when(chunk == pl.num_programs(0) - 1)
    def _():
        for b in range(q_blocks):
            for h in range(heads):
                at = (slice(b * blk, (b + 1) * blk), slice(h * HD, (h + 1) * HD))
                lanes = (slice(b * blk, (b + 1) * blk), slice(h * 128, (h + 1) * 128))
                total = jnp.sum(sum_ref[lanes], axis=-1, keepdims=True)
                result = acc_ref[at] / total
                o_ref[at] = result
                low_ref[at] = result.astype(jnp.bfloat16)
                l_ref[lanes] = jnp.broadcast_to(total, (blk, 128))


def attend(block_map, me, queries, pieces, blk, seq_blocks):
    rows, width = queries.shape
    heads = width // HD
    total = sum(piece.shape[0] for piece in pieces)
    joined = len(pieces) > 1
    chunk_rows = total if joined else min(total, KEY_CHUNK)
    kernel = partial(
        attend_kernel, blk=blk, heads=heads, parts=len(pieces), key_blocks=chunk_rows // blk,
        seq_blocks=seq_blocks, reach=WINDOW // blk,
    )
    whole = lambda i, *_: (0, 0)
    if joined:
        kv_specs = [pl.BlockSpec(piece.shape, whole) for piece in pieces]
    else:
        kv_specs = [pl.BlockSpec((chunk_rows, 2 * HD), lambda i, *_: (i, 0))]
    out_shape = [
        jax.ShapeDtypeStruct((rows, width), jnp.float32),
        jax.ShapeDtypeStruct((rows, width), jnp.bfloat16),
        jax.ShapeDtypeStruct((rows, heads * 128), jnp.float32),
    ]
    if joined:
        out_shape.append(jax.ShapeDtypeStruct((total, 2 * HD), jnp.bfloat16))
    found = pl.pallas_call(
        kernel,
        out_shape=tuple(out_shape),
        grid_spec=pltpu.PrefetchScalarGridSpec(
            num_scalar_prefetch=2,
            grid=(total // chunk_rows,),
            in_specs=[pl.BlockSpec((rows, width), whole), *kv_specs],
            out_specs=[pl.BlockSpec(shape.shape, whole) for shape in out_shape],
            scratch_shapes=[
                pltpu.VMEM((rows, width), jnp.float32),
                pltpu.VMEM((rows, heads * 128), jnp.float32),
                pltpu.SMEM((chunk_rows // blk + 1,), jnp.int32),
            ],
        ),
        compiler_params=pltpu.CompilerParams(vmem_limit_bytes=60 * 2**20),
        cost_estimate=pl.CostEstimate(
            flops=4 * rows * width * total, bytes_accessed=8 * rows * width + 8 * total * HD,
            transcendentals=2 * rows * heads * total,
        ),
        name="attend",
    )(block_map, me, queries, *pieces)
    return found if joined else (*found, pieces[0])


def attend_back_kernel(
    map_ref, me_ref, da_ref, out_ref, o_ref, l_ref, q_ref, kv_ref, kt_ref, cos_ref, sin_ref, *refs,
    blk, heads, swapped, key_blocks, seq_blocks, reach
):
    dq_ref, *dkv_refs = refs[: 3 if swapped else 2]
    do_ref, stat_ref, dqt_ref, dk_ref, dv_ref, list_ref = refs[3 if swapped else 2 :]
    chunk = pl.program_id(0)
    q_blocks = q_ref.shape[0] // blk

    @pl.when(chunk == 0)
    def _():
        dqt_ref[...] = jnp.zeros_like(dqt_ref)
        for h in range(heads):
            at = slice(h * HD, (h + 1) * HD)
            out_grad = matmul(da_ref[...], out_ref[:, at]).astype(jnp.bfloat16)
            do_ref[:, at] = out_grad
            delta = jnp.sum(out_grad.astype(jnp.float32) * o_ref[:, at], axis=-1, keepdims=True)
            stat_ref[heads + h : heads + h + 1, :] = jnp.broadcast_to(
                delta, (delta.shape[0], 128)
            ).T[:1, :]
            stat_ref[h : h + 1, :] = jnp.log2(l_ref[:, h * 128 : (h + 1) * 128]).T[:1, :]

    dk_ref[...] = jnp.zeros_like(dk_ref)
    dv_ref[...] = jnp.zeros_like(dv_ref)

    def tile(b, slot, mask):
        rows = pl.ds(pl.multiple_of(slot * blk, blk), blk)
        keys = kv_ref[rows, :HD]
        vals = kv_ref[rows, HD:]
        turned = kt_ref[:, rows]
        cols = slice(b * blk, (b + 1) * blk)
        for h in range(heads):
            query = q_ref[cols, h * HD : (h + 1) * HD]
            out_grad = do_ref[cols, h * HD : (h + 1) * HD]
            tangent = jnp.tanh(matmul_nt(keys, query) * (1.0 / soft_cap))
            probs = jnp.exp2(tangent * (soft_cap * LOG2E) - stat_ref[h : h + 1, cols])
            if mask is not None:
                probs = jnp.where(mask, probs, 0.0)
            prob_grad = matmul_nt(vals, out_grad)
            score = (
                probs * (prob_grad - stat_ref[heads + h : heads + h + 1, cols])
                * (1.0 - tangent * tangent)
            ).astype(jnp.bfloat16)
            dk_new = matmul(score, query)
            dv_new = matmul(probs.astype(jnp.bfloat16), out_grad)
            dk_part = dk_new if h == 0 else dk_part + dk_new
            dv_part = dv_new if h == 0 else dv_part + dv_new
            dqt_ref[h * HD : (h + 1) * HD, cols] += matmul(turned, score)
        dk_ref[rows, :] += dk_part
        dv_ref[rows, :] += dv_part

    visit_blocks(
        map_ref, me_ref[0], chunk, q_blocks, key_blocks, seq_blocks, reach, swapped, list_ref,
        tile, blk, True,
    )

    row = 0
    for dkv_ref in dkv_refs:
        count = dkv_ref.shape[0]
        dkv_ref[:, :HD] = dk_ref[row : row + count, :].astype(jnp.bfloat16)
        dkv_ref[:, HD:] = dv_ref[row : row + count, :].astype(jnp.bfloat16)
        row += count

    @pl.when(chunk == pl.num_programs(0) - 1)
    def _():
        cosine, sine = cos_ref[...], sin_ref[...]
        for h in range(heads):
            low = dqt_ref[h * HD : h * HD + HALF, :].T * HD ** (-0.5)
            high = dqt_ref[h * HD + HALF : (h + 1) * HD, :].T * HD ** (-0.5)
            dq_ref[:, h * HD : h * HD + HALF] = (low * cosine + high * sine).astype(jnp.bfloat16)
            dq_ref[:, h * HD + HALF : (h + 1) * HD] = (high * cosine - low * sine).astype(
                jnp.bfloat16
            )


def attend_back(
    block_map, me, branch_low, full_out_t, attended, totals, queries, kv_all, key_turned, cosine,
    sine, blk, seq_blocks, swapped
):
    rows, width = queries.shape
    heads = width // HD
    depth = branch_low.shape[1]
    total = kv_all.shape[0]
    chunk_rows = total if swapped else min(total, KEY_CHUNK)
    kernel = partial(
        attend_back_kernel, blk=blk, heads=heads, swapped=swapped, key_blocks=chunk_rows // blk,
        seq_blocks=seq_blocks, reach=WINDOW // blk,
    )
    whole = lambda i, *_: (0, 0)
    part = total // 2 if swapped else total
    dkv_shapes = [jax.ShapeDtypeStruct((part, 2 * HD), jnp.bfloat16)] * (2 if swapped else 1)
    dkv_specs = [pl.BlockSpec((min(part, chunk_rows), 2 * HD), lambda i, *_: (i, 0))] * len(dkv_shapes)
    return pl.pallas_call(
        kernel,
        out_shape=(jax.ShapeDtypeStruct((rows, width), jnp.bfloat16), *dkv_shapes),
        grid_spec=pltpu.PrefetchScalarGridSpec(
            num_scalar_prefetch=2,
            grid=(total // chunk_rows,),
            in_specs=[
                pl.BlockSpec((rows, depth), whole),
                pl.BlockSpec((depth, width), whole),
                pl.BlockSpec((rows, width), whole),
                pl.BlockSpec((rows, heads * 128), whole),
                pl.BlockSpec((rows, width), whole),
                pl.BlockSpec((chunk_rows, 2 * HD), lambda i, *_: (i, 0)),
                pl.BlockSpec((HD, chunk_rows), lambda i, *_: (0, i)),
                pl.BlockSpec((rows, HALF), whole),
                pl.BlockSpec((rows, HALF), whole),
            ],
            out_specs=[pl.BlockSpec((rows, width), whole), *dkv_specs],
            scratch_shapes=[
                pltpu.VMEM((rows, width), jnp.bfloat16),
                pltpu.VMEM((2 * heads, rows), jnp.float32),
                pltpu.VMEM((width, rows), jnp.float32),
                pltpu.VMEM((chunk_rows, HD), jnp.float32),
                pltpu.VMEM((chunk_rows, HD), jnp.float32),
                pltpu.SMEM((chunk_rows // blk + 1,), jnp.int32),
            ],
        ),
        compiler_params=pltpu.CompilerParams(vmem_limit_bytes=60 * 2**20),
        cost_estimate=pl.CostEstimate(
            flops=10 * rows * width * total, bytes_accessed=16 * rows * width + 10 * total * HD,
            transcendentals=2 * rows * heads * total,
        ),
        name="attend_back",
    )(
        block_map, me, branch_low, full_out_t, attended, totals, queries, kv_all, key_turned,
        cosine, sine,
    )


def body(
    tokens, block_map, w_query, w_key, w_value, w_out, w_gate, w_up, w_down, norm_gains, cotangent
):
    ctx_count = lax.axis_size("ctx")
    tok_dev, depth = tokens.shape
    block_rows = tok_dev // 2
    seq_count = max(1, ctx_count // 16)
    seq_len = tok_dev * ctx_count // seq_count
    seq_blocks = seq_len // block_rows
    me = lax.axis_index("ctx")
    me_list = me.reshape(1).astype(jnp.int32)
    heads_dev = w_query.shape[1] // HD
    q_width = heads_dev * HD
    flat_map = block_map.reshape(-1).astype(jnp.int32)
    pairs = paired()

    gains = gather_gains(norm_gains).astype(jnp.float32)
    if pairs:
        qkv_shard = pack(w_query, w_key, w_value)
        near = lax.optimization_barrier((*nearby(qkv_shard), gains))
        gains = near[2]
        qkv_pieces = gather_pieces(qkv_shard, near[:2])
        out_shard = tie(w_out, qkv_pieces[3], qkv_pieces[4]).T
        out_near = nearby(out_shard)
    else:
        qkv_shard = jnp.concatenate([w_query, w_key, w_value], axis=1)
        qkv_pieces = (lax.all_gather(qkv_shard, "ctx", axis=0, tiled=True),)
        out_pieces = (lax.all_gather(w_out.T, "ctx", axis=0, tiled=True),)
    own_ids = lax.dynamic_index_in_dim(block_map, me, 0, keepdims=False)
    offsets = jnp.arange(block_rows, dtype=jnp.int32)
    own_index = (own_ids[:, None] * block_rows + offsets[None, :]).reshape(-1)
    cosine, sine = angle_tables(own_index % seq_len)
    inputs = tokens.astype(jnp.float32)
    in_scale = rms_scale(inputs)
    normed_in = (inputs * in_scale * gains[0]).astype(jnp.bfloat16)
    queries, kv_local, full_qkv = project(normed_in, cosine, sine, qkv_pieces, heads_dev)
    if pairs:
        kv_local, *out_near = lax.optimization_barrier((kv_local, *out_near))
        kv_pieces = gather_pieces(kv_local)
        out_pieces = gather_pieces(tie(out_shard, *kv_pieces[1:3]), out_near)
        late = (*kv_pieces[3:5], *out_pieces[3:5])
    else:
        kv_pieces = (lax.all_gather(kv_local, "ctx", axis=0, tiled=True),)
        late = kv_pieces
    w_gate, w_up, w_down, *_ = lax.optimization_barrier((w_gate, w_up, w_down, *late))
    if pairs:
        gate_near = nearby(w_gate)
    attended, attn_flat, totals, kv_all = attend(
        flat_map, me_list, queries, kv_pieces, block_rows, seq_blocks
    )
    branch_part, full_out_t = out_project(attn_flat, out_pieces, depth)
    if pairs:
        branch_part, *gate_near = lax.optimization_barrier((branch_part, *gate_near))
        full_gate = assemble(gather_pieces(w_gate, gate_near))
    else:
        full_gate = lax.all_gather(w_gate, "ctx", axis=0, tiled=True)
    branch = lax.psum(branch_part, "tp")
    full_up = lax.all_gather(w_up, "ctx", axis=0, tiled=True)
    if pairs:
        full_down_t = assemble(gather_pieces(w_down.T))
    else:
        full_down_t = lax.all_gather(w_down.T, "ctx", axis=0, tiled=True)
    branch, full_gate, full_up, full_down_t = lax.optimization_barrier(
        (branch, full_gate, full_up, full_down_t)
    )
    normed_mid = by_rows(mid_kernel, (tokens, branch), gains, (jnp.bfloat16,), 0, "mid_norms")
    hidden, active, slope = units(normed_mid, full_gate, full_up)
    mlp_out = lax.psum(project_down(hidden, full_down_t), "tp")
    result, mlp_low, gain_four = by_rows(
        top_kernel, (tokens, branch, mlp_out, cotangent), gains, (jnp.bfloat16, jnp.bfloat16), 1,
        "top_norms",
    )
    gate_low, up_low, mid_part = units_back(mlp_low, full_down_t, full_gate, full_up, active, slope)
    mid_part, hidden_t, mlp_t, gate_t, up_t = lax.optimization_barrier(
        (mid_part, hidden, mlp_low, gate_low, up_low)
    )
    mid_sum = lax.psum(mid_part, "tp")
    down_grad = matmul(hidden_t.T, mlp_t).astype(jnp.bfloat16)
    down_shard = lax.psum_scatter(down_grad, "ctx", scatter_dimension=1, tiled=True)
    gate_grad = matmul(normed_mid.T, gate_t).astype(jnp.bfloat16)
    gate_blocks = scatter_start(gate_grad)
    up_grad = matmul(normed_mid.T, up_t).astype(jnp.bfloat16)
    key_turned = kv_all[:, :HD].T
    mid_sum, up_grad, key_turned, gate_blocks = lax.optimization_barrier(
        (mid_sum, up_grad, key_turned, gate_blocks)
    )
    gate_terms = scatter_finish(gate_blocks)
    resid_grad, branch_low, gain_mid = by_rows(
        low_kernel, (tokens, branch, mid_sum, cotangent), gains, (jnp.float32, jnp.bfloat16), 2,
        "low_norms",
    )
    query_low, *kv_terms = attend_back(
        flat_map, me_list, branch_low, full_out_t, attended, totals, queries, kv_all, key_turned,
        cosine, sine, block_rows, seq_blocks, pairs,
    )
    *kv_terms, down_shard, gate_terms = lax.optimization_barrier((*kv_terms, down_shard, gate_terms))
    gate_shard = add_terms(gate_terms)
    if pairs:
        mine = kv_terms[0] + swap(kv_terms[1], 1)
        kv_sums = scatter_finish(
            scatter_corner(*(mine[k * tok_dev : (k + 1) * tok_dev] for k in range(4)))
        )
    else:
        kv_sums = (lax.psum_scatter(kv_terms[0], "ctx", scatter_dimension=0, tiled=True),)
    qkv_low, in_part = join(cosine, sine, query_low, full_qkv, kv_sums)
    in_part, qkv_low, branch_t, up_grad = lax.optimization_barrier(
        (in_part, qkv_low, branch_low, up_grad)
    )
    in_sum = lax.psum(in_part, "tp")
    up_shard = lax.psum_scatter(up_grad, "ctx", scatter_dimension=0, tiled=True)
    gain_one = jnp.sum(in_part.astype(jnp.float32) * (inputs * in_scale), axis=0)
    gain_one = sum_small_tp(gain_one)
    gains_shard = scatter_gains(jnp.concatenate([gain_one[None], gain_mid[1:], gain_mid[:1], gain_four]))
    qkv_grad = matmul(normed_in.T, qkv_low).astype(jnp.bfloat16)
    qkv_shard = add_terms(scatter_finish(scatter_start(qkv_grad)))
    out_weight_grad = matmul(branch_t.T, attn_flat).astype(jnp.bfloat16)
    out_grad_t = add_terms(scatter_finish(scatter_start(out_weight_grad)))
    shards = (
        qkv_shard[:, :q_width],
        qkv_shard[:, q_width : q_width + HD],
        qkv_shard[:, q_width + HD :],
        out_grad_t.T,
        gate_shard,
        up_shard.astype(jnp.float32),
        down_shard.astype(jnp.float32),
        gains_shard,
    )
    in_sum, shards = lax.optimization_barrier((in_sum, shards))
    input_grad = by_rows(
        end_kernel, (tokens, in_sum, resid_grad), gains, (jnp.float32,), 0, "end_norms"
    )
    return (result, input_grad, *shards)


def solution(mesh):
    in_specs = (
        P("ctx", None),
        P(),
        P("ctx", "tp"),
        P("ctx", "tp"),
        P("ctx", "tp"),
        P("tp", "ctx"),
        P("ctx", "tp"),
        P("ctx", "tp"),
        P("tp", "ctx"),
        P(None, "ctx"),
        P("ctx", None),
    )
    out_specs = (
        P("ctx", None),
        P("ctx", None),
        P("ctx", "tp"),
        P("ctx", "tp"),
        P("ctx", "tp"),
        P("tp", "ctx"),
        P("ctx", "tp"),
        P("ctx", "tp"),
        P("tp", "ctx"),
        P(None, "ctx"),
    )
    return jax.shard_map(body, mesh=mesh, in_specs=in_specs, out_specs=out_specs, check_vma=False)
```

```python
from functools import partial

import jax
import jax.numpy as jnp
from jax import lax
from jax.experimental import pallas as pl
from jax.experimental.pallas import tpu as pltpu
from jax.sharding import PartitionSpec as P

HD = 256
HALF = 128
WINDOW = 4096
KEY_CHUNK = 4096
MOST = 60 * 2**20


epsilon = 1e-06
soft_cap = 50.0
LOG2E = 1.4426950408889634


def rms_scale(values):
    return lax.rsqrt(jnp.mean(values * values, axis=-1, keepdims=True) + epsilon)


def angle_tables(positions):
    frequency = jnp.power(10000.0, -2.0 * jnp.arange(HALF, dtype=jnp.float32) / HD)
    phases = positions.astype(jnp.float32)[:, None] * frequency[None, :]
    return (jnp.cos(phases), jnp.sin(phases))


def matmul(left, right):
    return jnp.dot(left, right, preferred_element_type=jnp.float32)


def matmul_nt(left, right):
    return lax.dot_general(left, right, (((1,), (1,)), ((), ())), preferred_element_type=jnp.float32)


def tie(value, *others):
    return lax.optimization_barrier((value,) + others)[0]


def tie_all(values, *others):
    return lax.optimization_barrier((*values, *others))[: len(values)]


def call(kernel, out_shape, args, name, scalars=0, scratch=(), flops=0, mem=32, space=None):
    spec = pl.BlockSpec(memory_space=pltpu.VMEM if space is None else space)
    outs = jax.tree.map(lambda _: spec, out_shape)
    size = sum(a.size * a.dtype.itemsize for a in args)
    size += sum(a.size * a.dtype.itemsize for a in jax.tree.leaves(out_shape))
    return pl.pallas_call(
        kernel,
        out_shape=out_shape,
        in_specs=[pl.BlockSpec(memory_space=pltpu.SMEM)] * scalars + [spec] * (len(args) - scalars),
        out_specs=outs,
        scratch_shapes=list(scratch),
        compiler_params=pltpu.CompilerParams(vmem_limit_bytes=mem * 2**20),
        cost_estimate=pl.CostEstimate(flops=flops, bytes_accessed=size, transcendentals=0),
        name=name,
    )(*args)


def swap(value, bit):
    pairs = [(i, i ^ bit) for i in range(lax.axis_size("ctx"))]
    return lax.ppermute(value, "ctx", pairs)


def paired():
    return lax.axis_size("ctx") == 8


def nearby(piece):
    return swap(piece, 2), swap(piece, 4)


def gather_pieces(piece, near=None):
    half = piece.shape[0] // 2
    by_x, by_y = nearby(piece) if near is None else near
    mine = (piece, by_x, by_y, swap(by_x[:half], 4), swap(by_y[half:], 2))
    return mine + tuple(swap(part, 1) for part in mine)


def piece_rows(rows):
    me = lax.axis_index("ctx")
    places = [(me ^ bit) * rows for bit in (0, 2, 4, 6, 6, 1, 3, 5, 7, 7)]
    shift = [0, 0, 0, 0, rows // 2] * 2
    return jnp.stack(places).astype(jnp.int32) + jnp.array(shift, jnp.int32)


def places_of(pieces):
    return piece_rows(pieces[0].shape[0]) if len(pieces) > 1 else jnp.zeros((1,), jnp.int32)


def place(rows_ref, pieces, whole_ref):
    for k, piece in enumerate(pieces):
        whole_ref[pl.ds(pl.multiple_of(rows_ref[k], 16), piece.shape[0]), :] = piece[...]


def assemble_kernel(rows_ref, *refs):
    place(rows_ref, refs[:-1], refs[-1])


def assemble(pieces, grid=1):
    if len(pieces) == 1:
        return pieces[0]
    rows, width = pieces[0].shape
    column = lambda n: pl.BlockSpec((n, width // grid), lambda i: (0, i))
    return pl.pallas_call(
        assemble_kernel,
        out_shape=jax.ShapeDtypeStruct((8 * rows, width), pieces[0].dtype),
        grid=(grid,),
        in_specs=[pl.BlockSpec(memory_space=pltpu.SMEM)] + [column(p.shape[0]) for p in pieces],
        out_specs=column(8 * rows),
        compiler_params=pltpu.CompilerParams(vmem_limit_bytes=MOST),
        cost_estimate=pl.CostEstimate(flops=0, bytes_accessed=32 * rows * width, transcendentals=0),
        name="assemble",
    )(piece_rows(rows), *pieces)


def scatter_corner(own, by_x, by_y, corner):
    half = own.shape[0] // 2
    from_x = swap(corner[:half], 2)
    from_y = swap(corner[half:], 4)
    by_y = jnp.concatenate([by_y[:half] + from_x, by_y[half:]], axis=0)
    by_x = jnp.concatenate([by_x[:half], by_x[half:] + from_y], axis=0)
    return own, by_x, by_y


def scatter_start(whole):
    if not paired():
        return (lax.psum_scatter(whole, "ctx", scatter_dimension=0, tiled=True),)
    me = lax.axis_index("ctx")
    chip, core = me // 2, me % 2
    rows = whole.shape[0] // 8
    blocks = whole.reshape(4, 2, rows, whole.shape[1])
    theirs = lax.dynamic_index_in_dim(blocks, 1 - core, 1, keepdims=False)
    mine = lax.dynamic_index_in_dim(blocks, core, 1, keepdims=False)
    mine = mine + swap(theirs, 1)
    pick = lambda bits: lax.dynamic_index_in_dim(mine, chip ^ bits, 0, keepdims=False)
    return scatter_corner(pick(0), pick(1), pick(2), pick(3))


def scatter_finish(blocks):
    if len(blocks) == 1:
        return blocks
    own, by_x, by_y = blocks
    return own, swap(by_x, 2), swap(by_y, 4)


def add_terms(terms):
    total = terms[0].astype(jnp.float32)
    for term in terms[1:]:
        total = total + term.astype(jnp.float32)
    return total


def scatter_gains(whole):
    if not paired():
        return lax.psum_scatter(whole, "ctx", scatter_dimension=1, tiled=True)
    me = lax.axis_index("ctx")
    columns = whole.shape[1] // 8
    stack = whole.reshape(whole.shape[0], 8, columns).transpose(1, 0, 2)
    for bit in (4, 2, 1):
        half = stack.shape[0] // 2
        low = (me & bit) == 0
        theirs = jnp.where(low, stack[half:], stack[:half])
        mine = jnp.where(low, stack[:half], stack[half:])
        stack = mine + swap(theirs, bit)
    return stack[0]


def sum_small_tp(value):
    count = lax.axis_size("tp")
    bit = 1
    while bit < count:
        value = value + lax.ppermute(value, "tp", [(i, i ^ bit) for i in range(count)])
        bit *= 2
    return value


def pack_kernel(a_ref, b_ref, c_ref, gains_ref, out_ref):
    one, two = a_ref.shape[1], a_ref.shape[1] + b_ref.shape[1]
    three = two + c_ref.shape[1]
    out_ref[:, :one] = a_ref[...]
    out_ref[:, one:two] = b_ref[...]
    out_ref[:, two:three] = c_ref[...]
    out_ref[:, three:] = jnp.broadcast_to(gains_ref[:, :1], (gains_ref.shape[0], HALF))
    for k in range(1, gains_ref.shape[1]):
        lane = lax.broadcasted_iota(jnp.int32, (gains_ref.shape[0], HALF), 1)
        column = jnp.broadcast_to(gains_ref[:, k : k + 1], lane.shape)
        out_ref[:, three:] = jnp.where(lane == k, column, out_ref[:, three:])


def pack(first, second, third, gains):
    width = first.shape[1] + second.shape[1] + third.shape[1] + HALF
    shape = jax.ShapeDtypeStruct((first.shape[0], width), first.dtype)
    return call(pack_kernel, shape, (first, second, third, gains), "pack")


def project_kernel(rows_ref, in_ref, cos_ref, sin_ref, *refs, heads, parts):
    pieces, (q_ref, kv_ref) = refs[:parts], refs[parts : parts + 2]
    if parts > 1:
        full_ref = refs[parts + 2]
        place(rows_ref, pieces, full_ref)
    else:
        full_ref = pieces[0]
    gain = full_ref[:, (heads + 2) * HD : (heads + 2) * HD + 1].astype(jnp.float32)
    for n in range(heads + 2):
        weight = (full_ref[:, n * HD : (n + 1) * HD].astype(jnp.float32) * gain).astype(jnp.bfloat16)
        raw = matmul(in_ref[...], weight)
        if n <= heads:
            low, high = raw[:, :HALF], raw[:, HALF:]
            cosine, sine = cos_ref[...], sin_ref[...]
            low, high = low * cosine - high * sine, high * cosine + low * sine
            if n < heads:
                q_ref[:, n * HD : n * HD + HALF] = (low * HD ** (-0.5)).astype(jnp.bfloat16)
                q_ref[:, n * HD + HALF : (n + 1) * HD] = (high * HD ** (-0.5)).astype(jnp.bfloat16)
            else:
                kv_ref[:, :HALF] = low.astype(jnp.bfloat16)
                kv_ref[:, HALF:HD] = high.astype(jnp.bfloat16)
        else:
            kv_ref[:, HD:] = raw.astype(jnp.bfloat16)


def project(normed, cosine, sine, pieces, heads):
    rows, depth = normed.shape
    width = pieces[0].shape[1]
    low = lambda n: jax.ShapeDtypeStruct((rows, n), jnp.bfloat16)
    scratch = [pltpu.VMEM((depth, width), jnp.bfloat16)] if len(pieces) > 1 else []
    return call(
        partial(project_kernel, heads=heads, parts=len(pieces)), (low(heads * HD), low(2 * HD)),
        (places_of(pieces), normed, cosine, sine, *pieces), "project", scalars=1, scratch=scratch,
        flops=2 * rows * depth * width,
    )


def out_project_kernel(rows_ref, attn_ref, *refs, parts):
    pieces, branch_ref = refs[:parts], refs[parts]
    if parts > 1:
        full_ref = refs[parts + 1]
        place(rows_ref, pieces, full_ref)
    else:
        full_ref = pieces[0]
    for n in range(0, branch_ref.shape[1], 256):
        part = matmul_nt(attn_ref[...], full_ref[n : n + 256, :])
        branch_ref[:, n : n + 256] = part.astype(jnp.bfloat16)


def out_project(attn, pieces, depth):
    rows, width = attn.shape
    scratch = [pltpu.VMEM((depth, width), jnp.bfloat16)] if len(pieces) > 1 else []
    return call(
        partial(out_project_kernel, parts=len(pieces)),
        jax.ShapeDtypeStruct((rows, depth), jnp.bfloat16), (places_of(pieces), attn, *pieces),
        "out_project", scalars=1, scratch=scratch, flops=2 * rows * depth * width,
    )


def join_kernel(cos_ref, sin_ref, query_ref, full_ref, *refs):
    *terms, low_ref, part_ref = refs
    total = terms[0][...].astype(jnp.float32)
    for term in terms[1:]:
        total = total + term[...].astype(jnp.float32)
    width = query_ref.shape[1]
    cosine, sine = cos_ref[...], sin_ref[...]
    low, high = total[:, :HALF], total[:, HALF:HD]
    low_ref[:, :width] = query_ref[...]
    low_ref[:, width : width + HALF] = (low * cosine + high * sine).astype(jnp.bfloat16)
    low_ref[:, width + HALF : width + HD] = (high * cosine - low * sine).astype(jnp.bfloat16)
    low_ref[:, width + HD :] = total[:, HD:].astype(jnp.bfloat16)
    for n in range(0, part_ref.shape[1], 256):
        part = matmul_nt(low_ref[...], full_ref[n : n + 256, : low_ref.shape[1]])
        part_ref[:, n : n + 256] = part.astype(jnp.bfloat16)


def join(cosine, sine, query_low, full_qkv, terms):
    rows = query_low.shape[0]
    depth, width = full_qkv.shape[0], query_low.shape[1] + 2 * HD
    low = lambda n: jax.ShapeDtypeStruct((rows, n), jnp.bfloat16)
    return call(
        join_kernel, (low(width), low(depth)), (cosine, sine, query_low, full_qkv, *terms), "join",
        flops=2 * rows * depth * width,
    )


GROUP = 16


def rms_of(values):
    return lax.rsqrt(jnp.mean(values * values, axis=-1, keepdims=True) + epsilon)


def norm_back(normed, scale, weighted):
    return scale * (weighted - normed * jnp.mean(weighted * normed, axis=-1, keepdims=True))


def fold(values):
    total = values[:8]
    for row in range(8, values.shape[0], 8):
        total = total + values[row : row + 8]
    return total


def wide(ref, rows):
    return ref[rows, :].astype(jnp.float32)


def walk(count, step):
    def run(index, carry):
        step(pl.ds(pl.multiple_of(index * GROUP, GROUP), GROUP))
        return carry

    lax.fori_loop(0, count // GROUP, run, 0, unroll=2)


def mid_kernel(tok_ref, branch_ref, gains_ref, out_ref):
    def step(rows):
        branch = wide(branch_ref, rows)
        residual = wide(tok_ref, rows) + branch * rms_of(branch) * gains_ref[1:2, :]
        out_ref[rows, :] = (residual * rms_of(residual) * gains_ref[2:3, :]).astype(jnp.bfloat16)

    walk(tok_ref.shape[0], step)


def top_kernel(tok_ref, branch_ref, mlp_ref, cot_ref, gains_ref, out_ref, grad_ref, sum_ref, acc_ref):
    @pl.when(pl.program_id(0) == 0)
    def _():
        acc_ref[...] = jnp.zeros_like(acc_ref)

    def step(rows):
        branch = wide(branch_ref, rows)
        residual = wide(tok_ref, rows) + branch * rms_of(branch) * gains_ref[1:2, :]
        mlp = wide(mlp_ref, rows)
        scale = rms_of(mlp)
        normed = mlp * scale
        out_ref[rows, :] = (residual + normed * gains_ref[3:4, :]).astype(jnp.bfloat16)
        out_grad = wide(cot_ref, rows)
        acc_ref[...] += fold(out_grad * normed)
        grad_ref[rows, :] = norm_back(normed, scale, out_grad * gains_ref[3:4, :]).astype(jnp.bfloat16)

    walk(tok_ref.shape[0], step)

    @pl.when(pl.program_id(0) == pl.num_programs(0) - 1)
    def _():
        sum_ref[...] = jnp.sum(acc_ref[...], axis=0, keepdims=True)


def low_kernel(
    tok_ref, branch_ref, mid_ref, cot_ref, gains_ref, resid_ref, grad_ref, sum_ref, acc_ref
):
    @pl.when(pl.program_id(0) == 0)
    def _():
        acc_ref[...] = jnp.zeros_like(acc_ref)

    def step(rows):
        branch = wide(branch_ref, rows)
        branch_scale = rms_of(branch)
        branch_normed = branch * branch_scale
        residual = wide(tok_ref, rows) + branch_normed * gains_ref[1:2, :]
        scale = rms_of(residual)
        normed = residual * scale
        mid_grad = wide(mid_ref, rows)
        acc_ref[:8, :] += fold(mid_grad * normed)
        grad = wide(cot_ref, rows) + norm_back(normed, scale, mid_grad * gains_ref[2:3, :])
        resid_ref[rows, :] = grad
        acc_ref[8:, :] += fold(grad * branch_normed)
        grad_ref[rows, :] = norm_back(
            branch_normed, branch_scale, grad * gains_ref[1:2, :]
        ).astype(jnp.bfloat16)

    walk(tok_ref.shape[0], step)

    @pl.when(pl.program_id(0) == pl.num_programs(0) - 1)
    def _():
        sum_ref[0:1, :] = jnp.sum(acc_ref[:8, :], axis=0, keepdims=True)
        sum_ref[1:2, :] = jnp.sum(acc_ref[8:, :], axis=0, keepdims=True)


def end_kernel(tok_ref, sum_ref, resid_ref, gains_ref, out_ref):
    def step(rows):
        values = wide(tok_ref, rows)
        scale = rms_of(values)
        weighted = wide(sum_ref, rows) * gains_ref[0:1, :]
        out_ref[rows, :] = resid_ref[rows, :] + norm_back(values * scale, scale, weighted)

    walk(tok_ref.shape[0], step)


def by_rows(kernel, args, gains, kinds, sums, name, block=128):
    rows, depth = args[0].shape
    tile = pl.BlockSpec((block, depth), lambda i: (i, 0))
    ahead = pl.BlockSpec((block, depth), lambda i: (i, 0))
    whole = lambda n: pl.BlockSpec((n, depth), lambda i: (0, 0))
    shapes = [jax.ShapeDtypeStruct((rows, depth), kind) for kind in kinds]
    out_specs = [tile] * len(kinds)
    scratch = []
    if sums:
        shapes.append(jax.ShapeDtypeStruct((sums, depth), jnp.float32))
        out_specs.append(whole(sums))
        scratch.append(pltpu.VMEM((8 * sums, depth), jnp.float32))
    size = sum(a.size * a.dtype.itemsize for a in (*args, *shapes))
    found = pl.pallas_call(
        kernel,
        out_shape=tuple(shapes),
        grid=(rows // block,),
        in_specs=[ahead] * len(args) + [whole(gains.shape[0])],
        out_specs=out_specs,
        scratch_shapes=scratch,
        compiler_params=pltpu.CompilerParams(vmem_limit_bytes=MOST),
        cost_estimate=pl.CostEstimate(flops=0, bytes_accessed=size, transcendentals=0),
        name=name,
    )(*args, gains)
    return found if len(found) > 1 else found[0]


UNITS = 768
STEP = 256


def units_kernel(in_ref, gate_ref, up_ref, hidden_ref, active_ref, slope_ref):
    for n in range(0, UNITS, STEP):
        at = slice(n, n + STEP)
        gate = matmul(in_ref[...], gate_ref[:, at])
        up = matmul(in_ref[...], up_ref[:, at])
        root = (2.0 / jnp.pi) ** 0.5
        square = gate * gate
        bend = jnp.tanh(root * gate * (1.0 + 0.044715 * square))
        half = 0.5 * (1.0 + bend)
        active = gate * half
        slope = half + 0.5 * gate * (1.0 - bend * bend) * (root * (1.0 + 3 * 0.044715 * square))
        hidden_ref[:, at] = (active * up).astype(jnp.bfloat16)
        active_ref[:, at] = active.astype(jnp.bfloat16)
        slope_ref[:, at] = (slope * up).astype(jnp.bfloat16)


def units(normed, full_gate, full_up):
    rows, depth = normed.shape
    count = full_gate.shape[1]
    column = lambda n: pl.BlockSpec((n, UNITS), lambda i: (0, i))
    ahead = pl.BlockSpec((depth, UNITS), lambda i: (0, i))
    return pl.pallas_call(
        units_kernel,
        out_shape=tuple(jax.ShapeDtypeStruct((rows, count), jnp.bfloat16) for _ in range(3)),
        grid=(count // UNITS,),
        in_specs=[pl.BlockSpec((rows, depth), lambda i: (0, 0)), ahead, ahead],
        out_specs=[column(rows)] * 3,
        compiler_params=pltpu.CompilerParams(vmem_limit_bytes=MOST),
        cost_estimate=pl.CostEstimate(
            flops=4 * rows * depth * count, bytes_accessed=4 * depth * count,
            transcendentals=rows * count,
        ),
        name="units",
    )(normed, full_gate, full_up)


def down_kernel(hidden_ref, down_ref, out_ref):
    for n in range(0, UNITS, STEP):
        part = matmul_nt(hidden_ref[...], down_ref[n : n + STEP, :])
        out_ref[:, n : n + STEP] = part.astype(jnp.bfloat16)


def project_down(hidden, full_down_t):
    rows, count = hidden.shape
    depth = full_down_t.shape[0]
    return pl.pallas_call(
        down_kernel,
        out_shape=jax.ShapeDtypeStruct((rows, depth), jnp.bfloat16),
        grid=(depth // UNITS,),
        in_specs=[
            pl.BlockSpec((rows, count), lambda i: (0, 0)),
            pl.BlockSpec((UNITS, count), lambda i: (i, 0)),
        ],
        out_specs=pl.BlockSpec((rows, UNITS), lambda i: (0, i)),
        compiler_params=pltpu.CompilerParams(vmem_limit_bytes=MOST),
        cost_estimate=pl.CostEstimate(
            flops=2 * rows * depth * count, bytes_accessed=2 * depth * count, transcendentals=0
        ),
        name="project_down",
    )(hidden, full_down_t)


def units_back_kernel(grad_ref, down_ref, active_ref, slope_ref, dg_ref, du_ref):
    for n in range(0, UNITS, STEP):
        at = slice(n, n + STEP)
        hidden_grad = matmul(grad_ref[...], down_ref[:, at])
        dg_ref[:, at] = (hidden_grad * slope_ref[:, at].astype(jnp.float32)).astype(jnp.bfloat16)
        du_ref[:, at] = (hidden_grad * active_ref[:, at].astype(jnp.float32)).astype(jnp.bfloat16)


def units_back(mlp_low, full_down_t, active, slope):
    rows, depth = mlp_low.shape
    count = active.shape[1]
    column = lambda n: pl.BlockSpec((n, UNITS), lambda i: (0, i))
    ahead = pl.BlockSpec((depth, UNITS), lambda i: (0, i))
    return pl.pallas_call(
        units_back_kernel,
        out_shape=tuple(jax.ShapeDtypeStruct((rows, count), jnp.bfloat16) for _ in range(2)),
        grid=(count // UNITS,),
        in_specs=[pl.BlockSpec((rows, depth), lambda i: (0, 0)), ahead, column(rows), column(rows)],
        out_specs=[column(rows)] * 2,
        compiler_params=pltpu.CompilerParams(vmem_limit_bytes=MOST),
        cost_estimate=pl.CostEstimate(
            flops=2 * rows * depth * count, bytes_accessed=2 * depth * count, transcendentals=0
        ),
        name="units_back",
    )(mlp_low, full_down_t, active, slope)


def features_back_kernel(dg_ref, du_ref, gate_ref, up_ref, out_ref):
    for n in range(0, UNITS, STEP):
        at = slice(n, n + STEP)
        part = matmul_nt(dg_ref[...], gate_ref[at, :]) + matmul_nt(du_ref[...], up_ref[at, :])
        out_ref[:, at] = part.astype(jnp.bfloat16)


def features_back(gate_low, up_low, full_gate, full_up):
    rows, count = gate_low.shape
    depth = full_gate.shape[0]
    whole = pl.BlockSpec((rows, count), lambda i: (0, 0))
    tile = pl.BlockSpec((UNITS, count), lambda i: (i, 0))
    return pl.pallas_call(
        features_back_kernel,
        out_shape=jax.ShapeDtypeStruct((rows, depth), jnp.bfloat16),
        grid=(depth // UNITS,),
        in_specs=[whole, whole, tile, tile],
        out_specs=pl.BlockSpec((rows, UNITS), lambda i: (0, i)),
        compiler_params=pltpu.CompilerParams(vmem_limit_bytes=MOST),
        cost_estimate=pl.CostEstimate(
            flops=4 * rows * depth * count, bytes_accessed=4 * depth * count, transcendentals=0
        ),
        name="features_back",
    )(gate_low, up_low, full_gate, full_up)


def slot_block(map_ref, me, slot, swapped):
    device = slot >> 1
    if swapped:
        device = me ^ (((device & 3) << 1) | (device >> 2))
    return map_ref[device * 2 + (slot & 1)]


def block_list(lookup, key_blocks, own, seq_blocks, reach, list_ref):
    def look(slot, count):
        other = lookup(slot)
        gap = own - other
        whole = (gap > 0) & (gap < reach) & (own // seq_blocks == other // seq_blocks)
        list_ref[count] = slot
        return count + whole.astype(jnp.int32)

    return lax.fori_loop(0, key_blocks, look, jnp.int32(0))


def find_block(lookup, key_blocks, wanted):
    def look(slot, found):
        return jnp.where(lookup(slot) == wanted, slot, found)

    return lax.fori_loop(0, key_blocks, look, jnp.int32(-1))


def visit_blocks(map_ref, me, chunk, q_blocks, key_blocks, seq_blocks, reach, swapped, list_ref, tile, blk, keys_first):
    first = chunk * key_blocks
    lookup = lambda slot: slot_block(map_ref, me, first + slot, swapped)
    row_no = lax.broadcasted_iota(jnp.int32, (blk, blk), 0)
    col_no = lax.broadcasted_iota(jnp.int32, (blk, blk), 1)
    query_no, key_no = (col_no, row_no) if keys_first else (row_no, col_no)
    for b in range(q_blocks):
        own = map_ref[me * q_blocks + b]
        count = block_list(lookup, key_blocks, own, seq_blocks, reach, list_ref)

        def pair(step, carry):
            tile(b, (list_ref[2 * step], list_ref[2 * step + 1]), None)
            return carry

        lax.fori_loop(0, count // 2, pair, 0)

        @pl.when(count % 2 == 1)
        def _():
            tile(b, (list_ref[count - 1],), None)

        diagonal = find_block(lookup, key_blocks, own)

        @pl.when(diagonal >= 0)
        def _():
            tile(b, (diagonal,), query_no >= key_no)

        if reach < seq_blocks:
            edge = find_block(lookup, key_blocks, own - reach)

            @pl.when((edge >= 0) & (own % seq_blocks >= reach))
            def _():
                tile(b, (edge,), query_no < key_no)


def turn_kernel(*refs):
    *pieces, whole_ref, turned_ref = refs
    row = 0
    for piece in pieces:
        count = piece.shape[0]
        whole_ref[row : row + count, :] = piece[...]
        turned_ref[:, row : row + count] = piece[:, :HD].T
        row += count


def turn(pieces):
    if len(pieces) == 1:
        return pieces[0], pieces[0][:, :HD].T
    total = sum(piece.shape[0] for piece in pieces)
    low = lambda a, b: jax.ShapeDtypeStruct((a, b), jnp.bfloat16)
    return call(turn_kernel, (low(total, 2 * HD), low(HD, total)), pieces, "turn")


def attend_kernel(
    map_ref, me_ref, q_ref, *refs, blk, heads, parts, key_blocks, seq_blocks, reach
):
    pieces = refs[:parts]
    o_ref, low_ref, l_ref = refs[parts : parts + 3]
    chunk = pl.program_id(0)
    if parts > 1:
        kv_ref = refs[parts + 3]
        row = 0
        for piece in pieces:
            kv_ref[row : row + piece.shape[0], :] = piece[...]
            row += piece.shape[0]
    else:
        kv_ref = pieces[0]
    acc_ref, sum_ref, list_ref = refs[-3:]
    q_blocks = q_ref.shape[0] // blk

    @pl.when(chunk == 0)
    def _():
        acc_ref[...] = jnp.zeros_like(acc_ref)
        sum_ref[...] = jnp.zeros_like(sum_ref)

    def tile(b, slots, mask):
        rows = [pl.ds(pl.multiple_of(slot * blk, blk), blk) for slot in slots]
        cols = slice(b * blk, (b + 1) * blk)
        for h in range(heads):
            query = q_ref[cols, h * HD : (h + 1) * HD]
            part = result = None
            for row in rows:
                capped = jnp.tanh(matmul_nt(query, kv_ref[row, :HD]) * (1.0 / soft_cap))
                weights = jnp.exp2(capped * (soft_cap * LOG2E))
                if mask is not None:
                    weights = jnp.where(mask, weights, 0.0)
                for piece in range(0, blk, 128):
                    term = weights[:, piece : piece + 128]
                    part = term if part is None else part + term
                term = matmul(weights.astype(jnp.bfloat16), kv_ref[row, HD:])
                result = term if result is None else result + term
            sum_ref[cols, h * 128 : (h + 1) * 128] += part
            acc_ref[cols, h * HD : (h + 1) * HD] += result

    visit_blocks(
        map_ref, me_ref[0], chunk, q_blocks, key_blocks, seq_blocks, reach, parts > 1, list_ref,
        tile, blk, False,
    )

    @pl.when(chunk == pl.num_programs(0) - 1)
    def _():
        for b in range(q_blocks):
            for h in range(heads):
                at = (slice(b * blk, (b + 1) * blk), slice(h * HD, (h + 1) * HD))
                lanes = (slice(b * blk, (b + 1) * blk), slice(h * 128, (h + 1) * 128))
                total = jnp.sum(sum_ref[lanes], axis=-1, keepdims=True)
                result = acc_ref[at] / total
                o_ref[at] = result
                low_ref[at] = result.astype(jnp.bfloat16)
                l_ref[lanes] = jnp.broadcast_to(total, (blk, 128))


def attend(block_map, me, queries, pieces, blk, seq_blocks):
    rows, width = queries.shape
    heads = width // HD
    total = sum(piece.shape[0] for piece in pieces)
    joined = len(pieces) > 1
    chunk_rows = total if joined else min(total, KEY_CHUNK)
    kernel = partial(
        attend_kernel, blk=blk, heads=heads, parts=len(pieces), key_blocks=chunk_rows // blk,
        seq_blocks=seq_blocks, reach=WINDOW // blk,
    )
    whole = lambda i, *_: (0, 0)
    if joined:
        kv_specs = [pl.BlockSpec(piece.shape, whole) for piece in pieces]
    else:
        kv_specs = [pl.BlockSpec((chunk_rows, 2 * HD), lambda i, *_: (i, 0))]
    out_shape = [
        jax.ShapeDtypeStruct((rows, width), jnp.float32),
        jax.ShapeDtypeStruct((rows, width), jnp.bfloat16),
        jax.ShapeDtypeStruct((rows, heads * 128), jnp.float32),
    ]
    held = [pltpu.VMEM((total, 2 * HD), jnp.bfloat16)] if joined else []
    return pl.pallas_call(
        kernel,
        out_shape=tuple(out_shape),
        grid_spec=pltpu.PrefetchScalarGridSpec(
            num_scalar_prefetch=2,
            grid=(total // chunk_rows,),
            in_specs=[pl.BlockSpec((rows, width), whole), *kv_specs],
            out_specs=[pl.BlockSpec(shape.shape, whole) for shape in out_shape],
            scratch_shapes=[
                *held,
                pltpu.VMEM((rows, width), jnp.float32),
                pltpu.VMEM((rows, heads * 128), jnp.float32),
                pltpu.SMEM((chunk_rows // blk + 1,), jnp.int32),
            ],
        ),
        compiler_params=pltpu.CompilerParams(vmem_limit_bytes=MOST),
        cost_estimate=pl.CostEstimate(
            flops=4 * rows * width * total, bytes_accessed=8 * rows * width + 8 * total * HD,
            transcendentals=2 * rows * heads * total,
        ),
        name="attend",
    )(block_map, me, queries, *pieces)


def attend_back_kernel(
    map_ref, me_ref, da_ref, out_ref, o_ref, l_ref, q_ref, kv_ref, kt_ref, cos_ref, sin_ref, *refs,
    blk, heads, swapped, key_blocks, seq_blocks, reach
):
    dq_ref, *dkv_refs = refs[: 5 if swapped else 2]
    do_ref, stat_ref, dqt_ref, dk_ref, dv_ref, list_ref = refs[5 if swapped else 2 :]
    chunk = pl.program_id(0)
    q_blocks = q_ref.shape[0] // blk

    @pl.when(chunk == 0)
    def _():
        dqt_ref[...] = jnp.zeros_like(dqt_ref)
        for h in range(heads):
            at = slice(h * HD, (h + 1) * HD)
            out_grad = matmul(da_ref[...], out_ref[:, at]).astype(jnp.bfloat16)
            do_ref[:, at] = out_grad
            delta = jnp.sum(out_grad.astype(jnp.float32) * o_ref[:, at], axis=-1, keepdims=True)
            stat_ref[heads + h : heads + h + 1, :] = jnp.broadcast_to(
                delta, (delta.shape[0], 128)
            ).T[:1, :]
            stat_ref[h : h + 1, :] = jnp.log2(l_ref[:, h * 128 : (h + 1) * 128]).T[:1, :]

    dk_ref[...] = jnp.zeros_like(dk_ref)
    dv_ref[...] = jnp.zeros_like(dv_ref)

    def tile(b, slots, mask):
        rows = [pl.ds(pl.multiple_of(slot * blk, blk), blk) for slot in slots]
        cols = slice(b * blk, (b + 1) * blk)
        dk_parts, dv_parts = [None] * len(rows), [None] * len(rows)
        dq_parts = [None] * heads
        add = lambda total, term: term if total is None else total + term
        for h in range(heads):
            query = q_ref[cols, h * HD : (h + 1) * HD]
            out_grad = do_ref[cols, h * HD : (h + 1) * HD]
            log_total = stat_ref[h : h + 1, cols]
            delta = stat_ref[heads + h : heads + h + 1, cols]
            for k, row in enumerate(rows):
                tangent = jnp.tanh(matmul_nt(kv_ref[row, :HD], query) * (1.0 / soft_cap))
                probs = jnp.exp2(tangent * (soft_cap * LOG2E) - log_total)
                if mask is not None:
                    probs = jnp.where(mask, probs, 0.0)
                prob_grad = matmul_nt(kv_ref[row, HD:], out_grad)
                score = (probs * (prob_grad - delta) * (1.0 - tangent * tangent)).astype(jnp.bfloat16)
                dk_parts[k] = add(dk_parts[k], matmul(score, query))
                dv_parts[k] = add(dv_parts[k], matmul(probs.astype(jnp.bfloat16), out_grad))
                dq_parts[h] = add(dq_parts[h], matmul(kt_ref[:, row], score))
        for h in range(heads):
            dqt_ref[h * HD : (h + 1) * HD, cols] += dq_parts[h]
        for k, row in enumerate(rows):
            dk_ref[row, :] += dk_parts[k]
            dv_ref[row, :] += dv_parts[k]

    visit_blocks(
        map_ref, me_ref[0], chunk, q_blocks, key_blocks, seq_blocks, reach, swapped, list_ref,
        tile, blk, True,
    )

    row = 0
    for dkv_ref in dkv_refs:
        count = dkv_ref.shape[0]
        dkv_ref[:, :HD] = dk_ref[row : row + count, :].astype(jnp.bfloat16)
        dkv_ref[:, HD:] = dv_ref[row : row + count, :].astype(jnp.bfloat16)
        row += count

    @pl.when(chunk == pl.num_programs(0) - 1)
    def _():
        cosine, sine = cos_ref[...], sin_ref[...]
        for h in range(heads):
            low = dqt_ref[h * HD : h * HD + HALF, :].T * HD ** (-0.5)
            high = dqt_ref[h * HD + HALF : (h + 1) * HD, :].T * HD ** (-0.5)
            dq_ref[:, h * HD : h * HD + HALF] = (low * cosine + high * sine).astype(jnp.bfloat16)
            dq_ref[:, h * HD + HALF : (h + 1) * HD] = (high * cosine - low * sine).astype(
                jnp.bfloat16
            )


def attend_back(
    block_map, me, branch_low, full_out_t, attended, totals, queries, kv_all, key_turned, cosine,
    sine, blk, seq_blocks, swapped
):
    rows, width = queries.shape
    heads = width // HD
    depth = branch_low.shape[1]
    total = kv_all.shape[0]
    chunk_rows = total if swapped else min(total, KEY_CHUNK)
    kernel = partial(
        attend_back_kernel, blk=blk, heads=heads, swapped=swapped, key_blocks=chunk_rows // blk,
        seq_blocks=seq_blocks, reach=WINDOW // blk,
    )
    whole = lambda i, *_: (0, 0)
    parts = [3 * rows, rows, 3 * rows, rows] if swapped else [total]
    dkv_shapes = [jax.ShapeDtypeStruct((part, 2 * HD), jnp.bfloat16) for part in parts]
    dkv_specs = [
        pl.BlockSpec((min(part, chunk_rows), 2 * HD), lambda i, *_: (i, 0)) for part in parts
    ]
    return pl.pallas_call(
        kernel,
        out_shape=(jax.ShapeDtypeStruct((rows, width), jnp.bfloat16), *dkv_shapes),
        grid_spec=pltpu.PrefetchScalarGridSpec(
            num_scalar_prefetch=2,
            grid=(total // chunk_rows,),
            in_specs=[
                pl.BlockSpec((rows, depth), whole),
                pl.BlockSpec((depth, width), whole),
                pl.BlockSpec((rows, width), whole),
                pl.BlockSpec((rows, heads * 128), whole),
                pl.BlockSpec((rows, width), whole),
                pl.BlockSpec((chunk_rows, 2 * HD), lambda i, *_: (i, 0)),
                pl.BlockSpec((HD, chunk_rows), lambda i, *_: (0, i)),
                pl.BlockSpec((rows, HALF), whole),
                pl.BlockSpec((rows, HALF), whole),
            ],
            out_specs=[pl.BlockSpec((rows, width), whole), *dkv_specs],
            scratch_shapes=[
                pltpu.VMEM((rows, width), jnp.bfloat16),
                pltpu.VMEM((2 * heads, rows), jnp.float32),
                pltpu.VMEM((width, rows), jnp.float32),
                pltpu.VMEM((chunk_rows, HD), jnp.float32),
                pltpu.VMEM((chunk_rows, HD), jnp.float32),
                pltpu.SMEM((chunk_rows // blk + 1,), jnp.int32),
            ],
        ),
        compiler_params=pltpu.CompilerParams(vmem_limit_bytes=MOST),
        cost_estimate=pl.CostEstimate(
            flops=10 * rows * width * total, bytes_accessed=16 * rows * width + 10 * total * HD,
            transcendentals=2 * rows * heads * total,
        ),
        name="attend_back",
    )(
        block_map, me, branch_low, full_out_t, attended, totals, queries, kv_all, key_turned,
        cosine, sine,
    )


def body(
    tokens, block_map, w_query, w_key, w_value, w_out, w_gate, w_up, w_down, norm_gains, cotangent
):
    ctx_count = lax.axis_size("ctx")
    tok_dev, depth = tokens.shape
    block_rows = tok_dev // 2
    seq_count = max(1, ctx_count // 16)
    seq_len = tok_dev * ctx_count // seq_count
    seq_blocks = seq_len // block_rows
    me = lax.axis_index("ctx")
    me_list = me.reshape(1).astype(jnp.int32)
    heads_dev = w_query.shape[1] // HD
    q_width = heads_dev * HD
    flat_map = block_map.reshape(-1).astype(jnp.int32)
    pairs = paired()

    qkv_shard = pack(w_query, w_key, w_value, norm_gains.T)
    if pairs:
        qkv_pieces = gather_pieces(qkv_shard)
        out_shard = tie(w_out, qkv_pieces[3], qkv_pieces[4]).T
        out_near = nearby(out_shard)
    else:
        qkv_pieces = (lax.all_gather(qkv_shard, "ctx", axis=0, tiled=True),)
        out_pieces = (lax.all_gather(w_out.T, "ctx", axis=0, tiled=True),)
    own_ids = lax.dynamic_index_in_dim(block_map, me, 0, keepdims=False)
    offsets = jnp.arange(block_rows, dtype=jnp.int32)
    own_index = (own_ids[:, None] * block_rows + offsets[None, :]).reshape(-1)
    cosine, sine = angle_tables(own_index % seq_len)
    inputs = tokens.astype(jnp.float32)
    in_scale = rms_scale(inputs)
    unit_in = (inputs * in_scale).astype(jnp.bfloat16)
    queries, kv_local = project(unit_in, cosine, sine, qkv_pieces, heads_dev)
    if pairs:
        kv_local, *out_near = lax.optimization_barrier((kv_local, *out_near))
        kv_pieces = gather_pieces(kv_local)
        out_pieces = gather_pieces(tie(out_shard, *kv_pieces[1:3]), out_near)
        late = (*kv_pieces[3:5], *out_pieces[3:5])
    else:
        kv_pieces = (lax.all_gather(kv_local, "ctx", axis=0, tiled=True),)
        late = kv_pieces
    w_gate, w_up, w_down, *_ = lax.optimization_barrier((w_gate, w_up, w_down, *late))
    if pairs:
        gate_near = nearby(w_gate)
    attended, attn_flat, totals = attend(
        flat_map, me_list, queries, kv_pieces, block_rows, seq_blocks
    )
    branch_part = out_project(attn_flat, out_pieces, depth)
    if pairs:
        branch_part, *gate_near = lax.optimization_barrier((branch_part, *gate_near))
        gate_pieces = gather_pieces(w_gate, gate_near)
        qkv_pieces = tie_all(qkv_pieces, branch_part)
    branch = lax.psum(branch_part, "tp")
    full_up = lax.all_gather(w_up, "ctx", axis=0, tiled=True)
    full_qkv = assemble(qkv_pieces)
    gains = full_qkv[:, q_width + 2 * HD : q_width + 2 * HD + 4].T.astype(jnp.float32)
    normed_in = (inputs * in_scale * gains[0]).astype(jnp.bfloat16)
    if pairs:
        down_shard, gains, normed_in, *far = lax.optimization_barrier(
            (w_down.T, gains, normed_in, *gate_pieces[3:5])
        )
        gate_pieces = (*gate_pieces[:3], *far, *gate_pieces[5:])
        down_near = nearby(down_shard)
        full_gate = assemble(gate_pieces, 3)
        full_gate, *down_near = lax.optimization_barrier((full_gate, *down_near))
        down_pieces = gather_pieces(down_shard, down_near)
    else:
        full_gate = lax.all_gather(w_gate, "ctx", axis=0, tiled=True)
        down_pieces = (lax.all_gather(w_down.T, "ctx", axis=0, tiled=True),)
    branch, full_gate, full_up, *mine = lax.optimization_barrier(
        (branch, full_gate, full_up, *down_pieces[:5])
    )
    down_pieces = (*mine, *down_pieces[5:])
    normed_mid = by_rows(mid_kernel, (tokens, branch), gains, (jnp.bfloat16,), 0, "mid_norms")
    hidden, active, slope = units(normed_mid, full_gate, full_up)
    full_down_t = assemble(down_pieces, 3)
    mlp_part = project_down(hidden, full_down_t)
    mlp_part, out_pieces, kv_pieces = lax.optimization_barrier((mlp_part, out_pieces, kv_pieces))
    full_out_t = assemble(out_pieces)
    kv_all, key_turned = turn(kv_pieces)
    mlp_out = lax.psum(mlp_part, "tp")
    mlp_out, full_out_t, kv_all, key_turned = lax.optimization_barrier(
        (mlp_out, full_out_t, kv_all, key_turned)
    )
    result, mlp_low, gain_four = by_rows(
        top_kernel, (tokens, branch, mlp_out, cotangent), gains, (jnp.bfloat16, jnp.bfloat16), 1,
        "top_norms",
    )
    gate_low, up_low = units_back(mlp_low, full_down_t, active, slope)
    mid_part = features_back(gate_low, up_low, full_gate, full_up)
    mid_part, hidden_t, mlp_t, gate_t, up_t = lax.optimization_barrier(
        (mid_part, hidden, mlp_low, gate_low, up_low)
    )
    mid_sum = lax.psum(mid_part, "tp")
    down_grad = matmul(hidden_t.T, mlp_t).astype(jnp.bfloat16)
    down_shard = lax.psum_scatter(down_grad, "ctx", scatter_dimension=1, tiled=True)
    gate_grad = matmul(normed_mid.T, gate_t).astype(jnp.bfloat16)
    gate_blocks = scatter_start(gate_grad)
    up_grad = matmul(normed_mid.T, up_t).astype(jnp.bfloat16)
    up_grad, gate_blocks = lax.optimization_barrier((up_grad, gate_blocks))
    gate_terms = scatter_finish(gate_blocks)
    mid_sum, up_grad = lax.optimization_barrier((mid_sum, up_grad))
    resid_grad, branch_low, gain_mid = by_rows(
        low_kernel, (tokens, branch, mid_sum, cotangent), gains, (jnp.float32, jnp.bfloat16), 2,
        "low_norms",
    )
    query_low, *kv_terms = attend_back(
        flat_map, me_list, branch_low, full_out_t, attended, totals, queries, kv_all, key_turned,
        cosine, sine, block_rows, seq_blocks, pairs,
    )
    *kv_terms, down_shard, gate_terms = lax.optimization_barrier((*kv_terms, down_shard, gate_terms))
    gate_shard = add_terms(gate_terms)
    if pairs:
        far = kv_terms[1] + swap(kv_terms[3], 1)
        near = kv_terms[0] + swap(kv_terms[2], 1)
        blocks = (near[k * tok_dev : (k + 1) * tok_dev] for k in range(3))
        kv_sums = scatter_finish(scatter_corner(*blocks, far))
    else:
        kv_sums = (lax.psum_scatter(kv_terms[0], "ctx", scatter_dimension=0, tiled=True),)
    qkv_low, in_part = join(cosine, sine, query_low, full_qkv, kv_sums)
    in_part, qkv_low, branch_t, up_grad = lax.optimization_barrier(
        (in_part, qkv_low, branch_low, up_grad)
    )
    in_sum = lax.psum(in_part, "tp")
    up_shard = lax.psum_scatter(up_grad, "ctx", scatter_dimension=0, tiled=True)
    gain_one = jnp.sum(in_part.astype(jnp.float32) * (inputs * in_scale), axis=0)
    gain_one = sum_small_tp(gain_one)
    gains_shard = scatter_gains(jnp.concatenate([gain_one[None], gain_mid[1:], gain_mid[:1], gain_four]))
    qkv_grad = matmul(normed_in.T, qkv_low).astype(jnp.bfloat16)
    qkv_shard = add_terms(scatter_finish(scatter_start(qkv_grad)))
    out_weight_grad = matmul(branch_t.T, attn_flat).astype(jnp.bfloat16)
    out_grad_t = add_terms(scatter_finish(scatter_start(out_weight_grad)))
    shards = (
        qkv_shard[:, :q_width],
        qkv_shard[:, q_width : q_width + HD],
        qkv_shard[:, q_width + HD :],
        out_grad_t.T,
        gate_shard,
        up_shard.astype(jnp.float32),
        down_shard.astype(jnp.float32),
        gains_shard,
    )
    in_sum, shards = lax.optimization_barrier((in_sum, shards))
    input_grad = by_rows(
        end_kernel, (tokens, in_sum, resid_grad), gains, (jnp.float32,), 0, "end_norms"
    )
    return (result, input_grad, *shards)


def solution(mesh):
    in_specs = (
        P("ctx", None),
        P(),
        P("ctx", "tp"),
        P("ctx", "tp"),
        P("ctx", "tp"),
        P("tp", "ctx"),
        P("ctx", "tp"),
        P("ctx", "tp"),
        P("tp", "ctx"),
        P(None, "ctx"),
        P("ctx", None),
    )
    out_specs = (
        P("ctx", None),
        P("ctx", None),
        P("ctx", "tp"),
        P("ctx", "tp"),
        P("ctx", "tp"),
        P("tp", "ctx"),
        P("ctx", "tp"),
        P("ctx", "tp"),
        P("tp", "ctx"),
        P(None, "ctx"),
    )
    return jax.shard_map(body, mesh=mesh, in_specs=in_specs, out_specs=out_specs, check_vma=False)
```

```python
from functools import partial

import jax
import jax.numpy as jnp
from jax import lax
from jax.experimental import pallas as pl
from jax.experimental.pallas import tpu as pltpu
from jax.sharding import PartitionSpec as P

HD = 256
HALF = 128
WINDOW = 4096
KEY_CHUNK = 4096
MOST = 60 * 2**20


epsilon = 1e-06
soft_cap = 50.0
LOG2E = 1.4426950408889634


def rms_scale(values):
    return lax.rsqrt(jnp.mean(values * values, axis=-1, keepdims=True) + epsilon)


def angle_tables(positions):
    frequency = jnp.power(10000.0, -2.0 * jnp.arange(HALF, dtype=jnp.float32) / HD)
    phases = positions.astype(jnp.float32)[:, None] * frequency[None, :]
    return (jnp.cos(phases), jnp.sin(phases))


def matmul(left, right):
    return jnp.dot(left, right, preferred_element_type=jnp.float32)


def matmul_nt(left, right):
    return lax.dot_general(left, right, (((1,), (1,)), ((), ())), preferred_element_type=jnp.float32)


def tie(value, *others):
    return lax.optimization_barrier((value,) + others)[0]


def tie_all(values, *others):
    return lax.optimization_barrier((*values, *others))[: len(values)]


def call(kernel, out_shape, args, name, scalars=0, scratch=(), flops=0, mem=32, space=None):
    spec = pl.BlockSpec(memory_space=pltpu.VMEM if space is None else space)
    outs = jax.tree.map(lambda _: spec, out_shape)
    size = sum(a.size * a.dtype.itemsize for a in args)
    size += sum(a.size * a.dtype.itemsize for a in jax.tree.leaves(out_shape))
    return pl.pallas_call(
        kernel,
        out_shape=out_shape,
        in_specs=[pl.BlockSpec(memory_space=pltpu.SMEM)] * scalars + [spec] * (len(args) - scalars),
        out_specs=outs,
        scratch_shapes=list(scratch),
        compiler_params=pltpu.CompilerParams(vmem_limit_bytes=mem * 2**20),
        cost_estimate=pl.CostEstimate(flops=flops, bytes_accessed=size, transcendentals=0),
        name=name,
    )(*args)


def swap(value, bit):
    pairs = [(i, i ^ bit) for i in range(lax.axis_size("ctx"))]
    return lax.ppermute(value, "ctx", pairs)


def paired():
    return lax.axis_size("ctx") == 8


def nearby(piece):
    return swap(piece, 2), swap(piece, 4)


def gather_pieces(piece, near=None):
    half = piece.shape[0] // 2
    by_x, by_y = nearby(piece) if near is None else near
    mine = (piece, by_x, by_y, swap(by_x[:half], 4), swap(by_y[half:], 2))
    return mine + tuple(swap(part, 1) for part in mine)


def nearby_halves(low, high):
    first = (swap(low, 2), swap(high, 4))
    return first[0], swap(high, 2), swap(low, 4), first[1]


def gather_halves(low, high, near=None):
    near = nearby_halves(low, high) if near is None else near
    mine = (low, high, *near, swap(near[0], 4), swap(near[3], 2))
    return mine + tuple(swap(part, 1) for part in mine)


def piece_rows(rows, halves):
    me = lax.axis_index("ctx")
    if halves:
        bits = [bit for core in (0, 1) for bit in (0, 2, 4, 6) for _ in range(2)]
        shift = [0, rows // 2] * 8
        places = [(me ^ (bit + k // 8)) * rows for k, bit in enumerate(bits)]
    else:
        places = [(me ^ bit) * rows for bit in (0, 2, 4, 6, 6, 1, 3, 5, 7, 7)]
        shift = [0, 0, 0, 0, rows // 2] * 2
    return jnp.stack(places).astype(jnp.int32) + jnp.array(shift, jnp.int32)


def places_of(pieces):
    if len(pieces) == 1:
        return jnp.zeros((1,), jnp.int32)
    rows = sum(piece.shape[0] for piece in pieces) // 8
    return piece_rows(rows, len(pieces) == 16)


def place(rows_ref, pieces, whole_ref):
    for k, piece in enumerate(pieces):
        whole_ref[pl.ds(pl.multiple_of(rows_ref[k], 16), piece.shape[0]), :] = piece[...]


def assemble_kernel(rows_ref, *refs):
    place(rows_ref, refs[:-1], refs[-1])


def assemble(pieces, grid=1):
    if len(pieces) == 1:
        return pieces[0]
    rows, width = sum(piece.shape[0] for piece in pieces) // 8, pieces[0].shape[1]
    column = lambda n: pl.BlockSpec((n, width // grid), lambda i: (0, i))
    return pl.pallas_call(
        assemble_kernel,
        out_shape=jax.ShapeDtypeStruct((8 * rows, width), pieces[0].dtype),
        grid=(grid,),
        in_specs=[pl.BlockSpec(memory_space=pltpu.SMEM)] + [column(p.shape[0]) for p in pieces],
        out_specs=column(8 * rows),
        compiler_params=pltpu.CompilerParams(vmem_limit_bytes=MOST),
        cost_estimate=pl.CostEstimate(flops=0, bytes_accessed=32 * rows * width, transcendentals=0),
        name="assemble",
    )(places_of(pieces), *pieces)


def scatter_corner(own, by_x, by_y, corner):
    half = own.shape[0] // 2
    from_x = swap(corner[:half], 2)
    from_y = swap(corner[half:], 4)
    by_y = jnp.concatenate([by_y[:half] + from_x, by_y[half:]], axis=0)
    by_x = jnp.concatenate([by_x[:half], by_x[half:] + from_y], axis=0)
    return own, by_x, by_y


def scatter_start(whole):
    if not paired():
        return (lax.psum_scatter(whole, "ctx", scatter_dimension=0, tiled=True),)
    me = lax.axis_index("ctx")
    chip, core = me // 2, me % 2
    rows = whole.shape[0] // 8
    blocks = whole.reshape(4, 2, rows, whole.shape[1])
    theirs = lax.dynamic_index_in_dim(blocks, 1 - core, 1, keepdims=False)
    mine = lax.dynamic_index_in_dim(blocks, core, 1, keepdims=False)
    mine = mine + swap(theirs, 1)
    pick = lambda bits: lax.dynamic_index_in_dim(mine, chip ^ bits, 0, keepdims=False)
    return scatter_corner(pick(0), pick(1), pick(2), pick(3))


def scatter_finish(blocks):
    if len(blocks) == 1:
        return blocks
    own, by_x, by_y = blocks
    return own, swap(by_x, 2), swap(by_y, 4)


def add_terms(terms):
    total = terms[0].astype(jnp.float32)
    for term in terms[1:]:
        total = total + term.astype(jnp.float32)
    return total


def scatter_gains(whole):
    if not paired():
        return lax.psum_scatter(whole, "ctx", scatter_dimension=1, tiled=True)
    me = lax.axis_index("ctx")
    columns = whole.shape[1] // 8
    stack = whole.reshape(whole.shape[0], 8, columns).transpose(1, 0, 2)
    for bit in (4, 2, 1):
        half = stack.shape[0] // 2
        low = (me & bit) == 0
        theirs = jnp.where(low, stack[half:], stack[:half])
        mine = jnp.where(low, stack[:half], stack[half:])
        stack = mine + swap(theirs, bit)
    return stack[0]


def sum_small_tp(value):
    count = lax.axis_size("tp")
    bit = 1
    while bit < count:
        value = value + lax.ppermute(value, "tp", [(i, i ^ bit) for i in range(count)])
        bit *= 2
    return value


def pack_kernel(a_ref, b_ref, c_ref, gains_ref, out_ref):
    one, two = a_ref.shape[1], a_ref.shape[1] + b_ref.shape[1]
    three = two + c_ref.shape[1]
    out_ref[:, :one] = a_ref[...]
    out_ref[:, one:two] = b_ref[...]
    out_ref[:, two:three] = c_ref[...]
    lane = lax.broadcasted_iota(jnp.int32, (gains_ref.shape[0], HALF), 1)
    columns = jnp.broadcast_to(gains_ref[:, :1], lane.shape)
    for k in range(1, gains_ref.shape[1]):
        columns = jnp.where(lane == k, jnp.broadcast_to(gains_ref[:, k : k + 1], lane.shape), columns)
    out_ref[:, three:] = columns


def pack(first, second, third, gains):
    width = first.shape[1] + second.shape[1] + third.shape[1] + HALF
    shape = jax.ShapeDtypeStruct((first.shape[0], width), first.dtype)
    return call(pack_kernel, shape, (first, second, third, gains), "pack")


def project_kernel(rows_ref, in_ref, cos_ref, sin_ref, *refs, heads, parts):
    pieces, q_ref, kv_refs = refs[:parts], refs[parts], refs[parts + 1 : parts + 3]
    block = kv_refs[0].shape[0]
    if parts > 1:
        full_ref = refs[parts + 3]
        place(rows_ref, pieces, full_ref)
    else:
        full_ref = pieces[0]
    gain = full_ref[:, (heads + 2) * HD : (heads + 2) * HD + 1].astype(jnp.float32)
    for n in range(heads + 2):
        weight = (full_ref[:, n * HD : (n + 1) * HD].astype(jnp.float32) * gain).astype(jnp.bfloat16)
        raw = matmul(in_ref[...], weight)
        if n <= heads:
            low, high = raw[:, :HALF], raw[:, HALF:]
            cosine, sine = cos_ref[...], sin_ref[...]
            low, high = low * cosine - high * sine, high * cosine + low * sine
            if n < heads:
                q_ref[:, n * HD : n * HD + HALF] = (low * HD ** (-0.5)).astype(jnp.bfloat16)
                q_ref[:, n * HD + HALF : (n + 1) * HD] = (high * HD ** (-0.5)).astype(jnp.bfloat16)
            else:
                for k, kv_ref in enumerate(kv_refs):
                    rows = slice(k * block, (k + 1) * block)
                    kv_ref[:, :HALF] = low[rows].astype(jnp.bfloat16)
                    kv_ref[:, HALF:HD] = high[rows].astype(jnp.bfloat16)
        else:
            for k, kv_ref in enumerate(kv_refs):
                kv_ref[:, HD:] = raw[k * block : (k + 1) * block].astype(jnp.bfloat16)


def project(normed, cosine, sine, pieces, heads):
    rows, depth = normed.shape
    width = pieces[0].shape[1]
    low = lambda m, n: jax.ShapeDtypeStruct((m, n), jnp.bfloat16)
    scratch = [pltpu.VMEM((depth, width), jnp.bfloat16)] if len(pieces) > 1 else []
    return call(
        partial(project_kernel, heads=heads, parts=len(pieces)),
        (low(rows, heads * HD), low(rows // 2, 2 * HD), low(rows // 2, 2 * HD)),
        (places_of(pieces), normed, cosine, sine, *pieces), "project", scalars=1, scratch=scratch,
        flops=2 * rows * depth * width,
    )


def out_project_kernel(rows_ref, attn_ref, *refs, parts):
    pieces, branch_ref = refs[:parts], refs[parts]
    if parts > 1:
        full_ref = refs[parts + 1]
        place(rows_ref, pieces, full_ref)
    else:
        full_ref = pieces[0]
    for n in range(0, branch_ref.shape[1], 256):
        part = matmul_nt(attn_ref[...], full_ref[n : n + 256, :])
        branch_ref[:, n : n + 256] = part.astype(jnp.bfloat16)


def out_project(attn, pieces, depth, name="out_project"):
    rows, width = attn.shape
    scratch = [pltpu.VMEM((depth, width), jnp.bfloat16)] if len(pieces) > 1 else []
    return call(
        partial(out_project_kernel, parts=len(pieces)),
        jax.ShapeDtypeStruct((rows, depth), jnp.bfloat16), (places_of(pieces), attn, *pieces),
        name, scalars=1, scratch=scratch, flops=2 * rows * depth * width,
    )


def join_kernel(cos_ref, sin_ref, query_ref, full_ref, *refs):
    *terms, low_ref, part_ref = refs
    total = terms[0][...].astype(jnp.float32)
    for term in terms[1:]:
        total = total + term[...].astype(jnp.float32)
    width = query_ref.shape[1]
    cosine, sine = cos_ref[...], sin_ref[...]
    low, high = total[:, :HALF], total[:, HALF:HD]
    low_ref[:, :width] = query_ref[...]
    low_ref[:, width : width + HALF] = (low * cosine + high * sine).astype(jnp.bfloat16)
    low_ref[:, width + HALF : width + HD] = (high * cosine - low * sine).astype(jnp.bfloat16)
    low_ref[:, width + HD :] = total[:, HD:].astype(jnp.bfloat16)
    for n in range(0, part_ref.shape[1], 256):
        part = matmul_nt(low_ref[...], full_ref[n : n + 256, : low_ref.shape[1]])
        part_ref[:, n : n + 256] = part.astype(jnp.bfloat16)


def join(cosine, sine, query_low, full_qkv, terms):
    rows = query_low.shape[0]
    depth, width = full_qkv.shape[0], query_low.shape[1] + 2 * HD
    low = lambda n: jax.ShapeDtypeStruct((rows, n), jnp.bfloat16)
    return call(
        join_kernel, (low(width), low(depth)), (cosine, sine, query_low, full_qkv, *terms), "join",
        flops=2 * rows * depth * width,
    )


GROUP = 16


def rms_of(values):
    return lax.rsqrt(jnp.mean(values * values, axis=-1, keepdims=True) + epsilon)


def norm_back(normed, scale, weighted):
    return scale * (weighted - normed * jnp.mean(weighted * normed, axis=-1, keepdims=True))


def fold(values):
    total = values[:8]
    for row in range(8, values.shape[0], 8):
        total = total + values[row : row + 8]
    return total


def wide(ref, rows):
    return ref[rows, :].astype(jnp.float32)


def walk(count, step):
    def run(index, carry):
        step(pl.ds(pl.multiple_of(index * GROUP, GROUP), GROUP))
        return carry

    lax.fori_loop(0, count // GROUP, run, 0, unroll=2)


def mid_kernel(tok_ref, branch_ref, gains_ref, out_ref):
    def step(rows):
        branch = wide(branch_ref, rows)
        residual = wide(tok_ref, rows) + branch * rms_of(branch) * gains_ref[1:2, :]
        out_ref[rows, :] = (residual * rms_of(residual) * gains_ref[2:3, :]).astype(jnp.bfloat16)

    walk(tok_ref.shape[0], step)


def top_kernel(tok_ref, branch_ref, mlp_ref, cot_ref, gains_ref, out_ref, grad_ref, sum_ref, acc_ref):
    @pl.when(pl.program_id(0) == 0)
    def _():
        acc_ref[...] = jnp.zeros_like(acc_ref)

    def step(rows):
        branch = wide(branch_ref, rows)
        residual = wide(tok_ref, rows) + branch * rms_of(branch) * gains_ref[1:2, :]
        mlp = wide(mlp_ref, rows)
        scale = rms_of(mlp)
        normed = mlp * scale
        out_ref[rows, :] = (residual + normed * gains_ref[3:4, :]).astype(jnp.bfloat16)
        out_grad = wide(cot_ref, rows)
        acc_ref[...] += fold(out_grad * normed)
        grad_ref[rows, :] = norm_back(normed, scale, out_grad * gains_ref[3:4, :]).astype(jnp.bfloat16)

    walk(tok_ref.shape[0], step)

    @pl.when(pl.program_id(0) == pl.num_programs(0) - 1)
    def _():
        sum_ref[...] = jnp.sum(acc_ref[...], axis=0, keepdims=True)


def low_kernel(
    tok_ref, branch_ref, mid_ref, cot_ref, gains_ref, resid_ref, grad_ref, sum_ref, acc_ref
):
    @pl.when(pl.program_id(0) == 0)
    def _():
        acc_ref[...] = jnp.zeros_like(acc_ref)

    def step(rows):
        branch = wide(branch_ref, rows)
        branch_scale = rms_of(branch)
        branch_normed = branch * branch_scale
        residual = wide(tok_ref, rows) + branch_normed * gains_ref[1:2, :]
        scale = rms_of(residual)
        normed = residual * scale
        mid_grad = wide(mid_ref, rows)
        acc_ref[:8, :] += fold(mid_grad * normed)
        grad = wide(cot_ref, rows) + norm_back(normed, scale, mid_grad * gains_ref[2:3, :])
        resid_ref[rows, :] = grad
        acc_ref[8:, :] += fold(grad * branch_normed)
        grad_ref[rows, :] = norm_back(
            branch_normed, branch_scale, grad * gains_ref[1:2, :]
        ).astype(jnp.bfloat16)

    walk(tok_ref.shape[0], step)

    @pl.when(pl.program_id(0) == pl.num_programs(0) - 1)
    def _():
        sum_ref[0:1, :] = jnp.sum(acc_ref[:8, :], axis=0, keepdims=True)
        sum_ref[1:2, :] = jnp.sum(acc_ref[8:, :], axis=0, keepdims=True)


def end_kernel(tok_ref, sum_ref, resid_ref, gains_ref, out_ref):
    def step(rows):
        values = wide(tok_ref, rows)
        scale = rms_of(values)
        weighted = wide(sum_ref, rows) * gains_ref[0:1, :]
        out_ref[rows, :] = resid_ref[rows, :] + norm_back(values * scale, scale, weighted)

    walk(tok_ref.shape[0], step)


def by_rows(kernel, args, gains, kinds, sums, name, block=128):
    rows, depth = args[0].shape
    tile = pl.BlockSpec((block, depth), lambda i: (i, 0))
    ahead = pl.BlockSpec((block, depth), lambda i: (i, 0))
    whole = lambda n: pl.BlockSpec((n, depth), lambda i: (0, 0))
    shapes = [jax.ShapeDtypeStruct((rows, depth), kind) for kind in kinds]
    out_specs = [tile] * len(kinds)
    scratch = []
    if sums:
        shapes.append(jax.ShapeDtypeStruct((sums, depth), jnp.float32))
        out_specs.append(whole(sums))
        scratch.append(pltpu.VMEM((8 * sums, depth), jnp.float32))
    size = sum(a.size * a.dtype.itemsize for a in (*args, *shapes))
    found = pl.pallas_call(
        kernel,
        out_shape=tuple(shapes),
        grid=(rows // block,),
        in_specs=[ahead] * len(args) + [whole(gains.shape[0])],
        out_specs=out_specs,
        scratch_shapes=scratch,
        compiler_params=pltpu.CompilerParams(vmem_limit_bytes=MOST),
        cost_estimate=pl.CostEstimate(flops=0, bytes_accessed=size, transcendentals=0),
        name=name,
    )(*args, gains)
    return found if len(found) > 1 else found[0]


UNITS = 768
STEP = 256


def units_kernel(in_ref, gate_ref, up_ref, hidden_ref, active_ref, slope_ref):
    for n in range(0, UNITS, STEP):
        at = slice(n, n + STEP)
        gate = matmul(in_ref[...], gate_ref[:, at])
        up = matmul(in_ref[...], up_ref[:, at])
        root = (2.0 / jnp.pi) ** 0.5
        square = gate * gate
        bend = jnp.tanh(root * gate * (1.0 + 0.044715 * square))
        half = 0.5 * (1.0 + bend)
        active = gate * half
        slope = half + 0.5 * gate * (1.0 - bend * bend) * (root * (1.0 + 3 * 0.044715 * square))
        hidden_ref[:, at] = (active * up).astype(jnp.bfloat16)
        active_ref[:, at] = active.astype(jnp.bfloat16)
        slope_ref[:, at] = (slope * up).astype(jnp.bfloat16)


def units(normed, full_gate, full_up):
    rows, depth = normed.shape
    count = full_gate.shape[1]
    column = lambda n: pl.BlockSpec((n, UNITS), lambda i: (0, i))
    ahead = pl.BlockSpec((depth, UNITS), lambda i: (0, i))
    return pl.pallas_call(
        units_kernel,
        out_shape=tuple(jax.ShapeDtypeStruct((rows, count), jnp.bfloat16) for _ in range(3)),
        grid=(count // UNITS,),
        in_specs=[pl.BlockSpec((rows, depth), lambda i: (0, 0)), ahead, ahead],
        out_specs=[column(rows)] * 3,
        compiler_params=pltpu.CompilerParams(vmem_limit_bytes=MOST),
        cost_estimate=pl.CostEstimate(
            flops=4 * rows * depth * count, bytes_accessed=4 * depth * count,
            transcendentals=rows * count,
        ),
        name="units",
    )(normed, full_gate, full_up)


def units_back_kernel(grad_ref, down_ref, active_ref, slope_ref, dg_ref, du_ref):
    for n in range(0, UNITS, STEP):
        at = slice(n, n + STEP)
        hidden_grad = matmul(grad_ref[...], down_ref[:, at])
        dg_ref[:, at] = (hidden_grad * slope_ref[:, at].astype(jnp.float32)).astype(jnp.bfloat16)
        du_ref[:, at] = (hidden_grad * active_ref[:, at].astype(jnp.float32)).astype(jnp.bfloat16)


def units_back(mlp_low, full_down_t, active, slope):
    rows, depth = mlp_low.shape
    count = active.shape[1]
    column = lambda n: pl.BlockSpec((n, UNITS), lambda i: (0, i))
    ahead = pl.BlockSpec((depth, UNITS), lambda i: (0, i))
    return pl.pallas_call(
        units_back_kernel,
        out_shape=tuple(jax.ShapeDtypeStruct((rows, count), jnp.bfloat16) for _ in range(2)),
        grid=(count // UNITS,),
        in_specs=[pl.BlockSpec((rows, depth), lambda i: (0, 0)), ahead, column(rows), column(rows)],
        out_specs=[column(rows)] * 2,
        compiler_params=pltpu.CompilerParams(vmem_limit_bytes=MOST),
        cost_estimate=pl.CostEstimate(
            flops=2 * rows * depth * count, bytes_accessed=2 * depth * count, transcendentals=0
        ),
        name="units_back",
    )(mlp_low, full_down_t, active, slope)


def features_back_kernel(dg_ref, du_ref, gate_ref, up_ref, out_ref):
    for n in range(0, UNITS, STEP):
        at = slice(n, n + STEP)
        part = matmul_nt(dg_ref[...], gate_ref[at, :]) + matmul_nt(du_ref[...], up_ref[at, :])
        out_ref[:, at] = part.astype(jnp.bfloat16)


def features_back(gate_low, up_low, full_gate, full_up):
    rows, count = gate_low.shape
    depth = full_gate.shape[0]
    whole = pl.BlockSpec((rows, count), lambda i: (0, 0))
    tile = pl.BlockSpec((UNITS, count), lambda i: (i, 0))
    return pl.pallas_call(
        features_back_kernel,
        out_shape=jax.ShapeDtypeStruct((rows, depth), jnp.bfloat16),
        grid=(depth // UNITS,),
        in_specs=[whole, whole, tile, tile],
        out_specs=pl.BlockSpec((rows, UNITS), lambda i: (0, i)),
        compiler_params=pltpu.CompilerParams(vmem_limit_bytes=MOST),
        cost_estimate=pl.CostEstimate(
            flops=4 * rows * depth * count, bytes_accessed=4 * depth * count, transcendentals=0
        ),
        name="features_back",
    )(gate_low, up_low, full_gate, full_up)


def slot_block(map_ref, me, slot, swapped):
    device = slot >> 1
    if swapped:
        device = me ^ (((device & 3) << 1) | (device >> 2))
    return map_ref[device * 2 + (slot & 1)]


def block_list(lookup, key_blocks, own, seq_blocks, reach, list_ref):
    def look(slot, count):
        other = lookup(slot)
        gap = own - other
        whole = (gap > 0) & (gap < reach) & (own // seq_blocks == other // seq_blocks)
        list_ref[count] = slot
        return count + whole.astype(jnp.int32)

    return lax.fori_loop(0, key_blocks, look, jnp.int32(0))


def find_block(lookup, key_blocks, wanted):
    def look(slot, found):
        return jnp.where(lookup(slot) == wanted, slot, found)

    return lax.fori_loop(0, key_blocks, look, jnp.int32(-1))


def visit_blocks(map_ref, me, chunk, q_blocks, key_blocks, seq_blocks, reach, swapped, list_ref, tile, blk, keys_first):
    first = chunk * key_blocks
    lookup = lambda slot: slot_block(map_ref, me, first + slot, swapped)
    row_no = lax.broadcasted_iota(jnp.int32, (blk, blk), 0)
    col_no = lax.broadcasted_iota(jnp.int32, (blk, blk), 1)
    query_no, key_no = (col_no, row_no) if keys_first else (row_no, col_no)
    for b in range(q_blocks):
        own = map_ref[me * q_blocks + b]
        count = block_list(lookup, key_blocks, own, seq_blocks, reach, list_ref)

        def pair(step, carry):
            tile(b, (list_ref[2 * step], list_ref[2 * step + 1]), None)
            return carry

        lax.fori_loop(0, count // 2, pair, 0)

        @pl.when(count % 2 == 1)
        def _():
            tile(b, (list_ref[count - 1],), None)

        diagonal = find_block(lookup, key_blocks, own)

        @pl.when(diagonal >= 0)
        def _():
            tile(b, (diagonal,), query_no >= key_no)

        if reach < seq_blocks:
            edge = find_block(lookup, key_blocks, own - reach)

            @pl.when((edge >= 0) & (own % seq_blocks >= reach))
            def _():
                tile(b, (edge,), query_no < key_no)


def turn_kernel(*refs):
    *pieces, whole_ref, turned_ref = refs
    row = 0
    for piece in pieces:
        count = piece.shape[0]
        whole_ref[row : row + count, :] = piece[...]
        turned_ref[:, row : row + count] = piece[:, :HD].T
        row += count


def turn(pieces):
    if len(pieces) == 1:
        return pieces[0], pieces[0][:, :HD].T
    total = sum(piece.shape[0] for piece in pieces)
    low = lambda a, b: jax.ShapeDtypeStruct((a, b), jnp.bfloat16)
    return call(turn_kernel, (low(total, 2 * HD), low(HD, total)), pieces, "turn")


def attend_kernel(
    map_ref, me_ref, q_ref, *refs, blk, heads, parts, key_blocks, seq_blocks, reach
):
    pieces = refs[:parts]
    o_ref, low_ref, l_ref = refs[parts : parts + 3]
    chunk = pl.program_id(0)
    if parts > 1:
        kv_ref = refs[parts + 3]
        row = 0
        for piece in pieces:
            kv_ref[row : row + piece.shape[0], :] = piece[...]
            row += piece.shape[0]
    else:
        kv_ref = pieces[0]
    acc_ref, sum_ref, list_ref = refs[-3:]
    q_blocks = q_ref.shape[0] // blk

    @pl.when(chunk == 0)
    def _():
        acc_ref[...] = jnp.zeros_like(acc_ref)
        sum_ref[...] = jnp.zeros_like(sum_ref)

    def tile(b, slots, mask):
        rows = [pl.ds(pl.multiple_of(slot * blk, blk), blk) for slot in slots]
        cols = slice(b * blk, (b + 1) * blk)
        for h in range(heads):
            query = q_ref[cols, h * HD : (h + 1) * HD]
            part = result = None
            for row in rows:
                capped = jnp.tanh(matmul_nt(query, kv_ref[row, :HD]) * (1.0 / soft_cap))
                weights = jnp.exp2(capped * (soft_cap * LOG2E))
                if mask is not None:
                    weights = jnp.where(mask, weights, 0.0)
                for piece in range(0, blk, 128):
                    term = weights[:, piece : piece + 128]
                    part = term if part is None else part + term
                term = matmul(weights.astype(jnp.bfloat16), kv_ref[row, HD:])
                result = term if result is None else result + term
            sum_ref[cols, h * 128 : (h + 1) * 128] += part
            acc_ref[cols, h * HD : (h + 1) * HD] += result

    visit_blocks(
        map_ref, me_ref[0], chunk, q_blocks, key_blocks, seq_blocks, reach, parts > 1, list_ref,
        tile, blk, False,
    )

    @pl.when(chunk == pl.num_programs(0) - 1)
    def _():
        for b in range(q_blocks):
            for h in range(heads):
                at = (slice(b * blk, (b + 1) * blk), slice(h * HD, (h + 1) * HD))
                lanes = (slice(b * blk, (b + 1) * blk), slice(h * 128, (h + 1) * 128))
                total = jnp.sum(sum_ref[lanes], axis=-1, keepdims=True)
                result = acc_ref[at] / total
                o_ref[at] = result
                low_ref[at] = result.astype(jnp.bfloat16)
                l_ref[lanes] = jnp.broadcast_to(total, (blk, 128))


def attend(block_map, me, queries, pieces, blk, seq_blocks):
    rows, width = queries.shape
    heads = width // HD
    total = sum(piece.shape[0] for piece in pieces)
    joined = len(pieces) > 1
    chunk_rows = total if joined else min(total, KEY_CHUNK)
    kernel = partial(
        attend_kernel, blk=blk, heads=heads, parts=len(pieces), key_blocks=chunk_rows // blk,
        seq_blocks=seq_blocks, reach=WINDOW // blk,
    )
    whole = lambda i, *_: (0, 0)
    if joined:
        kv_specs = [pl.BlockSpec(piece.shape, whole) for piece in pieces]
    else:
        kv_specs = [pl.BlockSpec((chunk_rows, 2 * HD), lambda i, *_: (i, 0))]
    out_shape = [
        jax.ShapeDtypeStruct((rows, width), jnp.float32),
        jax.ShapeDtypeStruct((rows, width), jnp.bfloat16),
        jax.ShapeDtypeStruct((rows, heads * 128), jnp.float32),
    ]
    held = [pltpu.VMEM((total, 2 * HD), jnp.bfloat16)] if joined else []
    return pl.pallas_call(
        kernel,
        out_shape=tuple(out_shape),
        grid_spec=pltpu.PrefetchScalarGridSpec(
            num_scalar_prefetch=2,
            grid=(total // chunk_rows,),
            in_specs=[pl.BlockSpec((rows, width), whole), *kv_specs],
            out_specs=[pl.BlockSpec(shape.shape, whole) for shape in out_shape],
            scratch_shapes=[
                *held,
                pltpu.VMEM((rows, width), jnp.float32),
                pltpu.VMEM((rows, heads * 128), jnp.float32),
                pltpu.SMEM((chunk_rows // blk + 1,), jnp.int32),
            ],
        ),
        compiler_params=pltpu.CompilerParams(vmem_limit_bytes=MOST),
        cost_estimate=pl.CostEstimate(
            flops=4 * rows * width * total, bytes_accessed=8 * rows * width + 8 * total * HD,
            transcendentals=2 * rows * heads * total,
        ),
        name="attend",
    )(block_map, me, queries, *pieces)


def attend_back_kernel(
    map_ref, me_ref, da_ref, out_ref, o_ref, l_ref, q_ref, kv_ref, kt_ref, cos_ref, sin_ref, *refs,
    blk, heads, swapped, key_blocks, seq_blocks, reach
):
    dq_ref, *dkv_refs = refs[: 5 if swapped else 2]
    do_ref, stat_ref, dqt_ref, dk_ref, dv_ref, list_ref = refs[5 if swapped else 2 :]
    chunk = pl.program_id(0)
    q_blocks = q_ref.shape[0] // blk

    @pl.when(chunk == 0)
    def _():
        dqt_ref[...] = jnp.zeros_like(dqt_ref)
        for h in range(heads):
            at = slice(h * HD, (h + 1) * HD)
            out_grad = matmul(da_ref[...], out_ref[:, at]).astype(jnp.bfloat16)
            do_ref[:, at] = out_grad
            delta = jnp.sum(out_grad.astype(jnp.float32) * o_ref[:, at], axis=-1, keepdims=True)
            stat_ref[heads + h : heads + h + 1, :] = jnp.broadcast_to(
                delta, (delta.shape[0], 128)
            ).T[:1, :]
            stat_ref[h : h + 1, :] = jnp.log2(l_ref[:, h * 128 : (h + 1) * 128]).T[:1, :]

    dk_ref[...] = jnp.zeros_like(dk_ref)
    dv_ref[...] = jnp.zeros_like(dv_ref)

    def tile(b, slots, mask):
        rows = [pl.ds(pl.multiple_of(slot * blk, blk), blk) for slot in slots]
        cols = slice(b * blk, (b + 1) * blk)
        dk_parts, dv_parts = [None] * len(rows), [None] * len(rows)
        dq_parts = [None] * heads
        add = lambda total, term: term if total is None else total + term
        for h in range(heads):
            query = q_ref[cols, h * HD : (h + 1) * HD]
            out_grad = do_ref[cols, h * HD : (h + 1) * HD]
            log_total = stat_ref[h : h + 1, cols]
            delta = stat_ref[heads + h : heads + h + 1, cols]
            for k, row in enumerate(rows):
                tangent = jnp.tanh(matmul_nt(kv_ref[row, :HD], query) * (1.0 / soft_cap))
                probs = jnp.exp2(tangent * (soft_cap * LOG2E) - log_total)
                if mask is not None:
                    probs = jnp.where(mask, probs, 0.0)
                prob_grad = matmul_nt(kv_ref[row, HD:], out_grad)
                score = (probs * (prob_grad - delta) * (1.0 - tangent * tangent)).astype(jnp.bfloat16)
                dk_parts[k] = add(dk_parts[k], matmul(score, query))
                dv_parts[k] = add(dv_parts[k], matmul(probs.astype(jnp.bfloat16), out_grad))
                dq_parts[h] = add(dq_parts[h], matmul(kt_ref[:, row], score))
        for h in range(heads):
            dqt_ref[h * HD : (h + 1) * HD, cols] += dq_parts[h]
        for k, row in enumerate(rows):
            dk_ref[row, :] += dk_parts[k]
            dv_ref[row, :] += dv_parts[k]

    visit_blocks(
        map_ref, me_ref[0], chunk, q_blocks, key_blocks, seq_blocks, reach, swapped, list_ref,
        tile, blk, True,
    )

    row = 0
    for dkv_ref in dkv_refs:
        count = dkv_ref.shape[0]
        dkv_ref[:, :HD] = dk_ref[row : row + count, :].astype(jnp.bfloat16)
        dkv_ref[:, HD:] = dv_ref[row : row + count, :].astype(jnp.bfloat16)
        row += count

    @pl.when(chunk == pl.num_programs(0) - 1)
    def _():
        cosine, sine = cos_ref[...], sin_ref[...]
        for h in range(heads):
            low = dqt_ref[h * HD : h * HD + HALF, :].T * HD ** (-0.5)
            high = dqt_ref[h * HD + HALF : (h + 1) * HD, :].T * HD ** (-0.5)
            dq_ref[:, h * HD : h * HD + HALF] = (low * cosine + high * sine).astype(jnp.bfloat16)
            dq_ref[:, h * HD + HALF : (h + 1) * HD] = (high * cosine - low * sine).astype(
                jnp.bfloat16
            )


def attend_back(
    block_map, me, branch_low, full_out_t, attended, totals, queries, kv_all, key_turned, cosine,
    sine, blk, seq_blocks, swapped
):
    rows, width = queries.shape
    heads = width // HD
    depth = branch_low.shape[1]
    total = kv_all.shape[0]
    chunk_rows = total if swapped else min(total, KEY_CHUNK)
    kernel = partial(
        attend_back_kernel, blk=blk, heads=heads, swapped=swapped, key_blocks=chunk_rows // blk,
        seq_blocks=seq_blocks, reach=WINDOW // blk,
    )
    whole = lambda i, *_: (0, 0)
    parts = [3 * rows, rows, 3 * rows, rows] if swapped else [total]
    dkv_shapes = [jax.ShapeDtypeStruct((part, 2 * HD), jnp.bfloat16) for part in parts]
    dkv_specs = [
        pl.BlockSpec((min(part, chunk_rows), 2 * HD), lambda i, *_: (i, 0)) for part in parts
    ]
    return pl.pallas_call(
        kernel,
        out_shape=(jax.ShapeDtypeStruct((rows, width), jnp.bfloat16), *dkv_shapes),
        grid_spec=pltpu.PrefetchScalarGridSpec(
            num_scalar_prefetch=2,
            grid=(total // chunk_rows,),
            in_specs=[
                pl.BlockSpec((rows, depth), whole),
                pl.BlockSpec((depth, width), whole),
                pl.BlockSpec((rows, width), whole),
                pl.BlockSpec((rows, heads * 128), whole),
                pl.BlockSpec((rows, width), whole),
                pl.BlockSpec((chunk_rows, 2 * HD), lambda i, *_: (i, 0)),
                pl.BlockSpec((HD, chunk_rows), lambda i, *_: (0, i)),
                pl.BlockSpec((rows, HALF), whole),
                pl.BlockSpec((rows, HALF), whole),
            ],
            out_specs=[pl.BlockSpec((rows, width), whole), *dkv_specs],
            scratch_shapes=[
                pltpu.VMEM((rows, width), jnp.bfloat16),
                pltpu.VMEM((2 * heads, rows), jnp.float32),
                pltpu.VMEM((width, rows), jnp.float32),
                pltpu.VMEM((chunk_rows, HD), jnp.float32),
                pltpu.VMEM((chunk_rows, HD), jnp.float32),
                pltpu.SMEM((chunk_rows // blk + 1,), jnp.int32),
            ],
        ),
        compiler_params=pltpu.CompilerParams(vmem_limit_bytes=MOST),
        cost_estimate=pl.CostEstimate(
            flops=10 * rows * width * total, bytes_accessed=16 * rows * width + 10 * total * HD,
            transcendentals=2 * rows * heads * total,
        ),
        name="attend_back",
    )(
        block_map, me, branch_low, full_out_t, attended, totals, queries, kv_all, key_turned,
        cosine, sine,
    )


def body(
    tokens, block_map, w_query, w_key, w_value, w_out, w_gate, w_up, w_down, norm_gains, cotangent
):
    ctx_count = lax.axis_size("ctx")
    tok_dev, depth = tokens.shape
    block_rows = tok_dev // 2
    seq_count = max(1, ctx_count // 16)
    seq_len = tok_dev * ctx_count // seq_count
    seq_blocks = seq_len // block_rows
    me = lax.axis_index("ctx")
    me_list = me.reshape(1).astype(jnp.int32)
    heads_dev = w_query.shape[1] // HD
    q_width = heads_dev * HD
    flat_map = block_map.reshape(-1).astype(jnp.int32)
    pairs = paired()

    qkv_shard = pack(w_query, w_key, w_value, norm_gains.T)
    if pairs:
        qkv_pieces = gather_pieces(qkv_shard)
        out_shard = tie(w_out, qkv_pieces[3], qkv_pieces[4]).T
        out_near = nearby(out_shard)
    else:
        qkv_pieces = (lax.all_gather(qkv_shard, "ctx", axis=0, tiled=True),)
        out_pieces = (lax.all_gather(w_out.T, "ctx", axis=0, tiled=True),)
    own_ids = lax.dynamic_index_in_dim(block_map, me, 0, keepdims=False)
    offsets = jnp.arange(block_rows, dtype=jnp.int32)
    own_index = (own_ids[:, None] * block_rows + offsets[None, :]).reshape(-1)
    cosine, sine = angle_tables(own_index % seq_len)
    inputs = tokens.astype(jnp.float32)
    in_scale = rms_scale(inputs)
    unit_in = (inputs * in_scale).astype(jnp.bfloat16)
    queries, *kv_local = project(unit_in, cosine, sine, qkv_pieces, heads_dev)
    if pairs:
        kv_local, out_near = lax.optimization_barrier((kv_local, out_near))
        kv_near = nearby_halves(*kv_local)
        kv_pieces = gather_halves(*kv_local, kv_near)
        out_pieces = gather_pieces(tie(out_shard, *kv_near), out_near)
        late = (*kv_pieces[2:8], *out_pieces[3:5])
    else:
        kv_pieces = (lax.all_gather(jnp.concatenate(kv_local), "ctx", axis=0, tiled=True),)
        late = kv_pieces
    w_gate, w_up, w_down, *_ = lax.optimization_barrier((w_gate, w_up, w_down, *late))
    if pairs:
        gate_near = nearby(w_gate)
    attended, attn_flat, totals = attend(
        flat_map, me_list, queries, kv_pieces, block_rows, seq_blocks
    )
    branch_part = out_project(attn_flat, out_pieces, depth)
    if pairs:
        branch_part, *gate_near = lax.optimization_barrier((branch_part, *gate_near))
        gate_pieces = gather_pieces(w_gate, gate_near)
        qkv_pieces = tie_all(qkv_pieces, branch_part)
    branch = lax.psum(branch_part, "tp")
    full_up = lax.all_gather(w_up, "ctx", axis=0, tiled=True)
    full_qkv = assemble(qkv_pieces)
    gains = full_qkv[:, q_width + 2 * HD : q_width + 2 * HD + 4].T.astype(jnp.float32)
    normed_in = (inputs * in_scale * gains[0]).astype(jnp.bfloat16)
    if pairs:
        down_shard, gains, normed_in, *far = lax.optimization_barrier(
            (w_down.T, gains, normed_in, *gate_pieces[3:5])
        )
        gate_pieces = (*gate_pieces[:3], *far, *gate_pieces[5:])
        down_near = nearby(down_shard)
        full_gate = assemble(gate_pieces, 3)
        full_gate, *down_near = lax.optimization_barrier((full_gate, *down_near))
        down_pieces = gather_pieces(down_shard, down_near)
    else:
        full_gate = lax.all_gather(w_gate, "ctx", axis=0, tiled=True)
        down_pieces = (lax.all_gather(w_down.T, "ctx", axis=0, tiled=True),)
    branch, full_gate, full_up, *near = lax.optimization_barrier(
        (branch, full_gate, full_up, *down_pieces[:3])
    )
    normed_mid = by_rows(mid_kernel, (tokens, branch), gains, (jnp.bfloat16,), 0, "mid_norms")
    if pairs:
        normed_mid, *far = lax.optimization_barrier((normed_mid, *down_pieces[3:5]))
        mine = (*near, *far)
        down_pieces = (*mine, *(swap(part, 1) for part in mine))
    hidden, active, slope = units(normed_mid, full_gate, full_up)
    mlp_part = out_project(hidden, down_pieces, depth, "project_down")
    mlp_part, out_pieces, kv_pieces, down_pieces = lax.optimization_barrier(
        (mlp_part, out_pieces, kv_pieces, down_pieces)
    )
    full_down_t = assemble(down_pieces, 3)
    full_out_t = assemble(out_pieces)
    kv_all, key_turned = turn(kv_pieces)
    mlp_out = lax.psum(mlp_part, "tp")
    mlp_out, full_out_t, kv_all, key_turned, full_down_t = lax.optimization_barrier(
        (mlp_out, full_out_t, kv_all, key_turned, full_down_t)
    )
    result, mlp_low, gain_four = by_rows(
        top_kernel, (tokens, branch, mlp_out, cotangent), gains, (jnp.bfloat16, jnp.bfloat16), 1,
        "top_norms",
    )
    gate_low, up_low = units_back(mlp_low, full_down_t, active, slope)
    mid_part = features_back(gate_low, up_low, full_gate, full_up)
    mid_part, hidden_t, mlp_t, gate_t, up_t = lax.optimization_barrier(
        (mid_part, hidden, mlp_low, gate_low, up_low)
    )
    mid_sum = lax.psum(mid_part, "tp")
    down_grad = matmul(hidden_t.T, mlp_t).astype(jnp.bfloat16)
    down_shard = lax.psum_scatter(down_grad, "ctx", scatter_dimension=1, tiled=True)
    gate_grad = matmul(normed_mid.T, gate_t).astype(jnp.bfloat16)
    gate_blocks = scatter_start(gate_grad)
    up_grad = matmul(normed_mid.T, up_t).astype(jnp.bfloat16)
    up_grad, gate_blocks = lax.optimization_barrier((up_grad, gate_blocks))
    gate_terms = scatter_finish(gate_blocks)
    mid_sum, up_grad = lax.optimization_barrier((mid_sum, up_grad))
    resid_grad, branch_low, gain_mid = by_rows(
        low_kernel, (tokens, branch, mid_sum, cotangent), gains, (jnp.float32, jnp.bfloat16), 2,
        "low_norms",
    )
    query_low, *kv_terms = attend_back(
        flat_map, me_list, branch_low, full_out_t, attended, totals, queries, kv_all, key_turned,
        cosine, sine, block_rows, seq_blocks, pairs,
    )
    *kv_terms, down_shard, gate_terms = lax.optimization_barrier((*kv_terms, down_shard, gate_terms))
    gate_shard = add_terms(gate_terms)
    if pairs:
        far = kv_terms[1] + swap(kv_terms[3], 1)
        near = kv_terms[0] + swap(kv_terms[2], 1)
        blocks = (near[k * tok_dev : (k + 1) * tok_dev] for k in range(3))
        kv_sums = scatter_finish(scatter_corner(*blocks, far))
    else:
        kv_sums = (lax.psum_scatter(kv_terms[0], "ctx", scatter_dimension=0, tiled=True),)
    qkv_low, in_part = join(cosine, sine, query_low, full_qkv, kv_sums)
    in_part, qkv_low, branch_t, up_grad = lax.optimization_barrier(
        (in_part, qkv_low, branch_low, up_grad)
    )
    in_sum = lax.psum(in_part, "tp")
    up_shard = lax.psum_scatter(up_grad, "ctx", scatter_dimension=0, tiled=True)
    gain_one = jnp.sum(in_part.astype(jnp.float32) * (inputs * in_scale), axis=0)
    gain_one = sum_small_tp(gain_one)
    gains_shard = scatter_gains(jnp.concatenate([gain_one[None], gain_mid[1:], gain_mid[:1], gain_four]))
    qkv_grad = matmul(normed_in.T, qkv_low).astype(jnp.bfloat16)
    qkv_shard = add_terms(scatter_finish(scatter_start(qkv_grad)))
    out_weight_grad = matmul(branch_t.T, attn_flat).astype(jnp.bfloat16)
    out_grad_t = add_terms(scatter_finish(scatter_start(out_weight_grad)))
    shards = (
        qkv_shard[:, :q_width],
        qkv_shard[:, q_width : q_width + HD],
        qkv_shard[:, q_width + HD :],
        out_grad_t.T,
        gate_shard,
        up_shard.astype(jnp.float32),
        down_shard.astype(jnp.float32),
        gains_shard,
    )
    in_sum, shards = lax.optimization_barrier((in_sum, shards))
    input_grad = by_rows(
        end_kernel, (tokens, in_sum, resid_grad), gains, (jnp.float32,), 0, "end_norms"
    )
    return (result, input_grad, *shards)


def solution(mesh):
    in_specs = (
        P("ctx", None),
        P(),
        P("ctx", "tp"),
        P("ctx", "tp"),
        P("ctx", "tp"),
        P("tp", "ctx"),
        P("ctx", "tp"),
        P("ctx", "tp"),
        P("tp", "ctx"),
        P(None, "ctx"),
        P("ctx", None),
    )
    out_specs = (
        P("ctx", None),
        P("ctx", None),
        P("ctx", "tp"),
        P("ctx", "tp"),
        P("ctx", "tp"),
        P("tp", "ctx"),
        P("ctx", "tp"),
        P("ctx", "tp"),
        P("tp", "ctx"),
        P(None, "ctx"),
    )
    return jax.shard_map(body, mesh=mesh, in_specs=in_specs, out_specs=out_specs, check_vma=False)
```

```python
from functools import partial

import jax
import jax.numpy as jnp
from jax import lax
from jax.experimental import pallas as pl
from jax.experimental.pallas import tpu as pltpu
from jax.sharding import PartitionSpec as P

HD = 256
HALF = 128
WINDOW = 4096
KEY_CHUNK = 4096
MOST = 60 * 2**20


epsilon = 1e-06
soft_cap = 50.0
LOG2E = 1.4426950408889634


def rms_scale(values):
    return lax.rsqrt(jnp.mean(values * values, axis=-1, keepdims=True) + epsilon)


def angle_tables(positions):
    frequency = jnp.power(10000.0, -2.0 * jnp.arange(HALF, dtype=jnp.float32) / HD)
    phases = positions.astype(jnp.float32)[:, None] * frequency[None, :]
    return (jnp.cos(phases), jnp.sin(phases))


def matmul(left, right):
    return jnp.dot(left, right, preferred_element_type=jnp.float32)


def matmul_nt(left, right):
    return lax.dot_general(left, right, (((1,), (1,)), ((), ())), preferred_element_type=jnp.float32)


def tie(value, *others):
    return lax.optimization_barrier((value,) + others)[0]


def tie_all(values, *others):
    return lax.optimization_barrier((*values, *others))[: len(values)]


def call(kernel, out_shape, args, name, scalars=0, scratch=(), flops=0, mem=32, space=None):
    spec = pl.BlockSpec(memory_space=pltpu.VMEM if space is None else space)
    outs = jax.tree.map(lambda _: spec, out_shape)
    size = sum(a.size * a.dtype.itemsize for a in args)
    size += sum(a.size * a.dtype.itemsize for a in jax.tree.leaves(out_shape))
    return pl.pallas_call(
        kernel,
        out_shape=out_shape,
        in_specs=[pl.BlockSpec(memory_space=pltpu.SMEM)] * scalars + [spec] * (len(args) - scalars),
        out_specs=outs,
        scratch_shapes=list(scratch),
        compiler_params=pltpu.CompilerParams(vmem_limit_bytes=mem * 2**20),
        cost_estimate=pl.CostEstimate(flops=flops, bytes_accessed=size, transcendentals=0),
        name=name,
    )(*args)


def swap(value, bit):
    pairs = [(i, i ^ bit) for i in range(lax.axis_size("ctx"))]
    return lax.ppermute(value, "ctx", pairs)


def paired():
    return lax.axis_size("ctx") == 8


def nearby(piece):
    return swap(piece, 2), swap(piece, 4)


def gather_pieces(piece, near=None):
    half = piece.shape[0] // 2
    by_x, by_y = nearby(piece) if near is None else near
    mine = (piece, by_x, by_y, swap(by_x[:half], 4), swap(by_y[half:], 2))
    return mine + tuple(swap(part, 1) for part in mine)


def nearby_halves(low, high):
    first = (swap(low, 2), swap(high, 4))
    return first[0], swap(high, 2), swap(low, 4), first[1]


def gather_halves(low, high, near=None):
    near = nearby_halves(low, high) if near is None else near
    mine = (low, high, *near, swap(near[0], 4), swap(near[3], 2))
    return mine + tuple(swap(part, 1) for part in mine)


def piece_rows(rows, halves):
    me = lax.axis_index("ctx")
    if halves:
        bits = [bit for core in (0, 1) for bit in (0, 2, 4, 6) for _ in range(2)]
        shift = [0, rows // 2] * 8
        places = [(me ^ (bit + k // 8)) * rows for k, bit in enumerate(bits)]
    else:
        places = [(me ^ bit) * rows for bit in (0, 2, 4, 6, 6, 1, 3, 5, 7, 7)]
        shift = [0, 0, 0, 0, rows // 2] * 2
    return jnp.stack(places).astype(jnp.int32) + jnp.array(shift, jnp.int32)


def places_of(pieces):
    if len(pieces) == 1:
        return jnp.zeros((1,), jnp.int32)
    rows = sum(piece.shape[0] for piece in pieces) // 8
    return piece_rows(rows, len(pieces) == 16)


def place(rows_ref, pieces, whole_ref):
    for k, piece in enumerate(pieces):
        whole_ref[pl.ds(pl.multiple_of(rows_ref[k], 16), piece.shape[0]), :] = piece[...]


def assemble_kernel(rows_ref, *refs):
    place(rows_ref, refs[:-1], refs[-1])


def assemble(pieces, grid=1):
    if len(pieces) == 1:
        return pieces[0]
    rows, width = sum(piece.shape[0] for piece in pieces) // 8, pieces[0].shape[1]
    column = lambda n: pl.BlockSpec((n, width // grid), lambda i: (0, i))
    return pl.pallas_call(
        assemble_kernel,
        out_shape=jax.ShapeDtypeStruct((8 * rows, width), pieces[0].dtype),
        grid=(grid,),
        in_specs=[pl.BlockSpec(memory_space=pltpu.SMEM)] + [column(p.shape[0]) for p in pieces],
        out_specs=column(8 * rows),
        compiler_params=pltpu.CompilerParams(vmem_limit_bytes=MOST),
        cost_estimate=pl.CostEstimate(flops=0, bytes_accessed=32 * rows * width, transcendentals=0),
        name="assemble",
    )(places_of(pieces), *pieces)


def scatter_corner(own, by_x, by_y, corner):
    half = own.shape[0] // 2
    from_x = swap(corner[:half], 2)
    from_y = swap(corner[half:], 4)
    by_y = jnp.concatenate([by_y[:half] + from_x, by_y[half:]], axis=0)
    by_x = jnp.concatenate([by_x[:half], by_x[half:] + from_y], axis=0)
    return own, by_x, by_y


def scatter_chips(whole):
    if not paired():
        return lax.psum_scatter(whole, "ctx", scatter_dimension=0, tiled=True)
    core = lax.axis_index("ctx") % 2
    blocks = whole.reshape(4, 2, whole.shape[0] // 8, whole.shape[1])
    theirs = lax.dynamic_index_in_dim(blocks, 1 - core, 1, keepdims=False)
    mine = lax.dynamic_index_in_dim(blocks, core, 1, keepdims=False)
    return mine + swap(theirs, 1)


def scatter_blocks(chips):
    if not paired():
        return (chips,)
    chip = lax.axis_index("ctx") // 2
    pick = lambda bits: lax.dynamic_index_in_dim(chips, chip ^ bits, 0, keepdims=False)
    return scatter_corner(pick(0), pick(1), pick(2), pick(3))


def scatter_start(whole):
    return scatter_blocks(scatter_chips(whole))


def scatter_finish(blocks):
    if len(blocks) == 1:
        return blocks
    own, by_x, by_y = blocks
    return own, swap(by_x, 2), swap(by_y, 4)


def add_terms(terms):
    total = terms[0].astype(jnp.float32)
    for term in terms[1:]:
        total = total + term.astype(jnp.float32)
    return total


def scatter_gains(whole):
    if not paired():
        return lax.psum_scatter(whole, "ctx", scatter_dimension=1, tiled=True)
    me = lax.axis_index("ctx")
    columns = whole.shape[1] // 8
    stack = whole.reshape(whole.shape[0], 8, columns).transpose(1, 0, 2)
    for bit in (4, 2, 1):
        half = stack.shape[0] // 2
        low = (me & bit) == 0
        theirs = jnp.where(low, stack[half:], stack[:half])
        mine = jnp.where(low, stack[:half], stack[half:])
        stack = mine + swap(theirs, bit)
    return stack[0]


def sum_small_tp(value):
    count = lax.axis_size("tp")
    bit = 1
    while bit < count:
        value = value + lax.ppermute(value, "tp", [(i, i ^ bit) for i in range(count)])
        bit *= 2
    return value


def pack_kernel(a_ref, b_ref, c_ref, gains_ref, out_ref):
    one, two = a_ref.shape[1], a_ref.shape[1] + b_ref.shape[1]
    three = two + c_ref.shape[1]
    out_ref[:, :one] = a_ref[...]
    out_ref[:, one:two] = b_ref[...]
    out_ref[:, two:three] = c_ref[...]
    lane = lax.broadcasted_iota(jnp.int32, (gains_ref.shape[0], HALF), 1)
    columns = jnp.broadcast_to(gains_ref[:, :1], lane.shape)
    for k in range(1, gains_ref.shape[1]):
        columns = jnp.where(lane == k, jnp.broadcast_to(gains_ref[:, k : k + 1], lane.shape), columns)
    out_ref[:, three:] = columns


def pack(first, second, third, gains):
    width = first.shape[1] + second.shape[1] + third.shape[1] + HALF
    shape = jax.ShapeDtypeStruct((first.shape[0], width), first.dtype)
    return call(pack_kernel, shape, (first, second, third, gains), "pack")


def project_kernel(rows_ref, in_ref, cos_ref, sin_ref, *refs, heads, parts):
    pieces, q_ref, kv_refs = refs[:parts], refs[parts], refs[parts + 1 : parts + 3]
    block = kv_refs[0].shape[0]
    if parts > 1:
        full_ref = refs[parts + 3]
        place(rows_ref, pieces, full_ref)
    else:
        full_ref = pieces[0]
    gain = full_ref[:, (heads + 2) * HD : (heads + 2) * HD + 1].astype(jnp.float32)
    for n in range(heads + 2):
        weight = (full_ref[:, n * HD : (n + 1) * HD].astype(jnp.float32) * gain).astype(jnp.bfloat16)
        raw = matmul(in_ref[...], weight)
        if n <= heads:
            low, high = raw[:, :HALF], raw[:, HALF:]
            cosine, sine = cos_ref[...], sin_ref[...]
            low, high = low * cosine - high * sine, high * cosine + low * sine
            if n < heads:
                q_ref[:, n * HD : n * HD + HALF] = (low * HD ** (-0.5)).astype(jnp.bfloat16)
                q_ref[:, n * HD + HALF : (n + 1) * HD] = (high * HD ** (-0.5)).astype(jnp.bfloat16)
            else:
                for k, kv_ref in enumerate(kv_refs):
                    rows = slice(k * block, (k + 1) * block)
                    kv_ref[:, :HALF] = low[rows].astype(jnp.bfloat16)
                    kv_ref[:, HALF:HD] = high[rows].astype(jnp.bfloat16)
        else:
            for k, kv_ref in enumerate(kv_refs):
                kv_ref[:, HD:] = raw[k * block : (k + 1) * block].astype(jnp.bfloat16)


def project(normed, cosine, sine, pieces, heads):
    rows, depth = normed.shape
    width = pieces[0].shape[1]
    low = lambda m, n: jax.ShapeDtypeStruct((m, n), jnp.bfloat16)
    scratch = [pltpu.VMEM((depth, width), jnp.bfloat16)] if len(pieces) > 1 else []
    return call(
        partial(project_kernel, heads=heads, parts=len(pieces)),
        (low(rows, heads * HD), low(rows // 2, 2 * HD), low(rows // 2, 2 * HD)),
        (places_of(pieces), normed, cosine, sine, *pieces), "project", scalars=1, scratch=scratch,
        flops=2 * rows * depth * width,
    )


def out_project_kernel(rows_ref, attn_ref, *refs, parts):
    pieces, branch_ref = refs[:parts], refs[parts]
    if parts > 1:
        full_ref = refs[parts + 1]
        place(rows_ref, pieces, full_ref)
    else:
        full_ref = pieces[0]
    for n in range(0, branch_ref.shape[1], 256):
        part = matmul_nt(attn_ref[...], full_ref[n : n + 256, :])
        branch_ref[:, n : n + 256] = part.astype(jnp.bfloat16)


def out_project(attn, pieces, depth, name="out_project"):
    rows, width = attn.shape
    scratch = [pltpu.VMEM((depth, width), jnp.bfloat16)] if len(pieces) > 1 else []
    return call(
        partial(out_project_kernel, parts=len(pieces)),
        jax.ShapeDtypeStruct((rows, depth), jnp.bfloat16), (places_of(pieces), attn, *pieces),
        name, scalars=1, scratch=scratch, flops=2 * rows * depth * width,
    )


def join_kernel(cos_ref, sin_ref, query_ref, full_ref, *refs):
    *terms, low_ref, part_ref = refs
    total = terms[0][...].astype(jnp.float32)
    for term in terms[1:]:
        total = total + term[...].astype(jnp.float32)
    width = query_ref.shape[1]
    cosine, sine = cos_ref[...], sin_ref[...]
    low, high = total[:, :HALF], total[:, HALF:HD]
    low_ref[:, :width] = query_ref[...]
    low_ref[:, width : width + HALF] = (low * cosine + high * sine).astype(jnp.bfloat16)
    low_ref[:, width + HALF : width + HD] = (high * cosine - low * sine).astype(jnp.bfloat16)
    low_ref[:, width + HD :] = total[:, HD:].astype(jnp.bfloat16)
    for n in range(0, part_ref.shape[1], 256):
        part = matmul_nt(low_ref[...], full_ref[n : n + 256, : low_ref.shape[1]])
        part_ref[:, n : n + 256] = part.astype(jnp.bfloat16)


def join(cosine, sine, query_low, full_qkv, terms):
    rows = query_low.shape[0]
    depth, width = full_qkv.shape[0], query_low.shape[1] + 2 * HD
    low = lambda n: jax.ShapeDtypeStruct((rows, n), jnp.bfloat16)
    return call(
        join_kernel, (low(width), low(depth)), (cosine, sine, query_low, full_qkv, *terms), "join",
        flops=2 * rows * depth * width,
    )


GROUP = 16


def rms_of(values):
    return lax.rsqrt(jnp.mean(values * values, axis=-1, keepdims=True) + epsilon)


def norm_back(normed, scale, weighted):
    return scale * (weighted - normed * jnp.mean(weighted * normed, axis=-1, keepdims=True))


def fold(values):
    total = values[:8]
    for row in range(8, values.shape[0], 8):
        total = total + values[row : row + 8]
    return total


def wide(ref, rows):
    return ref[rows, :].astype(jnp.float32)


def walk(count, step):
    def run(index, carry):
        step(pl.ds(pl.multiple_of(index * GROUP, GROUP), GROUP))
        return carry

    lax.fori_loop(0, count // GROUP, run, 0, unroll=2)


def mid_kernel(tok_ref, branch_ref, gains_ref, out_ref):
    def step(rows):
        branch = wide(branch_ref, rows)
        residual = wide(tok_ref, rows) + branch * rms_of(branch) * gains_ref[1:2, :]
        out_ref[rows, :] = (residual * rms_of(residual) * gains_ref[2:3, :]).astype(jnp.bfloat16)

    walk(tok_ref.shape[0], step)


def top_kernel(tok_ref, branch_ref, mlp_ref, cot_ref, gains_ref, out_ref, grad_ref, sum_ref, acc_ref):
    @pl.when(pl.program_id(0) == 0)
    def _():
        acc_ref[...] = jnp.zeros_like(acc_ref)

    def step(rows):
        branch = wide(branch_ref, rows)
        residual = wide(tok_ref, rows) + branch * rms_of(branch) * gains_ref[1:2, :]
        mlp = wide(mlp_ref, rows)
        scale = rms_of(mlp)
        normed = mlp * scale
        out_ref[rows, :] = (residual + normed * gains_ref[3:4, :]).astype(jnp.bfloat16)
        out_grad = wide(cot_ref, rows)
        acc_ref[...] += fold(out_grad * normed)
        grad_ref[rows, :] = norm_back(normed, scale, out_grad * gains_ref[3:4, :]).astype(jnp.bfloat16)

    walk(tok_ref.shape[0], step)

    @pl.when(pl.program_id(0) == pl.num_programs(0) - 1)
    def _():
        sum_ref[...] = jnp.sum(acc_ref[...], axis=0, keepdims=True)


def low_kernel(
    tok_ref, branch_ref, mid_ref, cot_ref, gains_ref, resid_ref, grad_ref, sum_ref, acc_ref
):
    @pl.when(pl.program_id(0) == 0)
    def _():
        acc_ref[...] = jnp.zeros_like(acc_ref)

    def step(rows):
        branch = wide(branch_ref, rows)
        branch_scale = rms_of(branch)
        branch_normed = branch * branch_scale
        residual = wide(tok_ref, rows) + branch_normed * gains_ref[1:2, :]
        scale = rms_of(residual)
        normed = residual * scale
        mid_grad = wide(mid_ref, rows)
        acc_ref[:8, :] += fold(mid_grad * normed)
        grad = wide(cot_ref, rows) + norm_back(normed, scale, mid_grad * gains_ref[2:3, :])
        resid_ref[rows, :] = grad
        acc_ref[8:, :] += fold(grad * branch_normed)
        grad_ref[rows, :] = norm_back(
            branch_normed, branch_scale, grad * gains_ref[1:2, :]
        ).astype(jnp.bfloat16)

    walk(tok_ref.shape[0], step)

    @pl.when(pl.program_id(0) == pl.num_programs(0) - 1)
    def _():
        sum_ref[0:1, :] = jnp.sum(acc_ref[:8, :], axis=0, keepdims=True)
        sum_ref[1:2, :] = jnp.sum(acc_ref[8:, :], axis=0, keepdims=True)


def end_kernel(tok_ref, sum_ref, resid_ref, gains_ref, out_ref):
    def step(rows):
        values = wide(tok_ref, rows)
        scale = rms_of(values)
        weighted = wide(sum_ref, rows) * gains_ref[0:1, :]
        out_ref[rows, :] = resid_ref[rows, :] + norm_back(values * scale, scale, weighted)

    walk(tok_ref.shape[0], step)


def by_rows(kernel, args, gains, kinds, sums, name, block=128):
    rows, depth = args[0].shape
    tile = pl.BlockSpec((block, depth), lambda i: (i, 0))
    ahead = pl.BlockSpec((block, depth), lambda i: (i, 0))
    whole = lambda n: pl.BlockSpec((n, depth), lambda i: (0, 0))
    shapes = [jax.ShapeDtypeStruct((rows, depth), kind) for kind in kinds]
    out_specs = [tile] * len(kinds)
    scratch = []
    if sums:
        shapes.append(jax.ShapeDtypeStruct((sums, depth), jnp.float32))
        out_specs.append(whole(sums))
        scratch.append(pltpu.VMEM((8 * sums, depth), jnp.float32))
    size = sum(a.size * a.dtype.itemsize for a in (*args, *shapes))
    found = pl.pallas_call(
        kernel,
        out_shape=tuple(shapes),
        grid=(rows // block,),
        in_specs=[ahead] * len(args) + [whole(gains.shape[0])],
        out_specs=out_specs,
        scratch_shapes=scratch,
        compiler_params=pltpu.CompilerParams(vmem_limit_bytes=MOST),
        cost_estimate=pl.CostEstimate(flops=0, bytes_accessed=size, transcendentals=0),
        name=name,
    )(*args, gains)
    return found if len(found) > 1 else found[0]


UNITS = 768
STEP = 256


def units_kernel(in_ref, gate_ref, up_ref, hidden_ref, active_ref, slope_ref):
    for n in range(0, UNITS, STEP):
        at = slice(n, n + STEP)
        gate = matmul(in_ref[...], gate_ref[:, at])
        up = matmul(in_ref[...], up_ref[:, at])
        root = (2.0 / jnp.pi) ** 0.5
        square = gate * gate
        bend = jnp.tanh(root * gate * (1.0 + 0.044715 * square))
        half = 0.5 * (1.0 + bend)
        active = gate * half
        slope = half + 0.5 * gate * (1.0 - bend * bend) * (root * (1.0 + 3 * 0.044715 * square))
        hidden_ref[:, at] = (active * up).astype(jnp.bfloat16)
        active_ref[:, at] = active.astype(jnp.bfloat16)
        slope_ref[:, at] = (slope * up).astype(jnp.bfloat16)


def units(normed, full_gate, full_up):
    rows, depth = normed.shape
    count = full_gate.shape[1]
    column = lambda n: pl.BlockSpec((n, UNITS), lambda i: (0, i))
    ahead = pl.BlockSpec((depth, UNITS), lambda i: (0, i))
    return pl.pallas_call(
        units_kernel,
        out_shape=tuple(jax.ShapeDtypeStruct((rows, count), jnp.bfloat16) for _ in range(3)),
        grid=(count // UNITS,),
        in_specs=[pl.BlockSpec((rows, depth), lambda i: (0, 0)), ahead, ahead],
        out_specs=[column(rows)] * 3,
        compiler_params=pltpu.CompilerParams(vmem_limit_bytes=MOST),
        cost_estimate=pl.CostEstimate(
            flops=4 * rows * depth * count, bytes_accessed=4 * depth * count,
            transcendentals=rows * count,
        ),
        name="units",
    )(normed, full_gate, full_up)


def units_back_kernel(grad_ref, down_ref, active_ref, slope_ref, dg_ref, du_ref):
    for n in range(0, UNITS, STEP):
        at = slice(n, n + STEP)
        hidden_grad = matmul(grad_ref[...], down_ref[:, at])
        dg_ref[:, at] = (hidden_grad * slope_ref[:, at].astype(jnp.float32)).astype(jnp.bfloat16)
        du_ref[:, at] = (hidden_grad * active_ref[:, at].astype(jnp.float32)).astype(jnp.bfloat16)


def units_back(mlp_low, full_down_t, active, slope):
    rows, depth = mlp_low.shape
    count = active.shape[1]
    column = lambda n: pl.BlockSpec((n, UNITS), lambda i: (0, i))
    ahead = pl.BlockSpec((depth, UNITS), lambda i: (0, i))
    return pl.pallas_call(
        units_back_kernel,
        out_shape=tuple(jax.ShapeDtypeStruct((rows, count), jnp.bfloat16) for _ in range(2)),
        grid=(count // UNITS,),
        in_specs=[pl.BlockSpec((rows, depth), lambda i: (0, 0)), ahead, column(rows), column(rows)],
        out_specs=[column(rows)] * 2,
        compiler_params=pltpu.CompilerParams(vmem_limit_bytes=MOST),
        cost_estimate=pl.CostEstimate(
            flops=2 * rows * depth * count, bytes_accessed=2 * depth * count, transcendentals=0
        ),
        name="units_back",
    )(mlp_low, full_down_t, active, slope)


def features_back_kernel(dg_ref, du_ref, gate_ref, up_ref, out_ref):
    for n in range(0, UNITS, STEP):
        at = slice(n, n + STEP)
        part = matmul_nt(dg_ref[...], gate_ref[at, :]) + matmul_nt(du_ref[...], up_ref[at, :])
        out_ref[:, at] = part.astype(jnp.bfloat16)


def features_back(gate_low, up_low, full_gate, full_up):
    rows, count = gate_low.shape
    depth = full_gate.shape[0]
    whole = pl.BlockSpec((rows, count), lambda i: (0, 0))
    tile = pl.BlockSpec((UNITS, count), lambda i: (i, 0))
    return pl.pallas_call(
        features_back_kernel,
        out_shape=jax.ShapeDtypeStruct((rows, depth), jnp.bfloat16),
        grid=(depth // UNITS,),
        in_specs=[whole, whole, tile, tile],
        out_specs=pl.BlockSpec((rows, UNITS), lambda i: (0, i)),
        compiler_params=pltpu.CompilerParams(vmem_limit_bytes=MOST),
        cost_estimate=pl.CostEstimate(
            flops=4 * rows * depth * count, bytes_accessed=4 * depth * count, transcendentals=0
        ),
        name="features_back",
    )(gate_low, up_low, full_gate, full_up)


def slot_block(map_ref, me, slot, swapped):
    device = slot >> 1
    if swapped:
        device = me ^ (((device & 3) << 1) | (device >> 2))
    return map_ref[device * 2 + (slot & 1)]


def block_list(lookup, key_blocks, own, seq_blocks, reach, list_ref):
    def look(slot, count):
        other = lookup(slot)
        gap = own - other
        whole = (gap > 0) & (gap < reach) & (own // seq_blocks == other // seq_blocks)
        list_ref[count] = slot
        return count + whole.astype(jnp.int32)

    return lax.fori_loop(0, key_blocks, look, jnp.int32(0))


def find_block(lookup, key_blocks, wanted):
    def look(slot, found):
        return jnp.where(lookup(slot) == wanted, slot, found)

    return lax.fori_loop(0, key_blocks, look, jnp.int32(-1))


def visit_blocks(map_ref, me, chunk, q_blocks, key_blocks, seq_blocks, reach, swapped, list_ref, tile, blk, keys_first):
    first = chunk * key_blocks
    lookup = lambda slot: slot_block(map_ref, me, first + slot, swapped)
    row_no = lax.broadcasted_iota(jnp.int32, (blk, blk), 0)
    col_no = lax.broadcasted_iota(jnp.int32, (blk, blk), 1)
    query_no, key_no = (col_no, row_no) if keys_first else (row_no, col_no)
    for b in range(q_blocks):
        own = map_ref[me * q_blocks + b]
        count = block_list(lookup, key_blocks, own, seq_blocks, reach, list_ref)

        def pair(step, carry):
            tile(b, (list_ref[2 * step], list_ref[2 * step + 1]), None)
            return carry

        lax.fori_loop(0, count // 2, pair, 0)

        @pl.when(count % 2 == 1)
        def _():
            tile(b, (list_ref[count - 1],), None)

        diagonal = find_block(lookup, key_blocks, own)

        @pl.when(diagonal >= 0)
        def _():
            tile(b, (diagonal,), query_no >= key_no)

        if reach < seq_blocks:
            edge = find_block(lookup, key_blocks, own - reach)

            @pl.when((edge >= 0) & (own % seq_blocks >= reach))
            def _():
                tile(b, (edge,), query_no < key_no)


def turn_kernel(*refs):
    *pieces, whole_ref, turned_ref = refs
    row = 0
    for piece in pieces:
        count = piece.shape[0]
        whole_ref[row : row + count, :] = piece[...]
        turned_ref[:, row : row + count] = piece[:, :HD].T
        row += count


def turn(pieces):
    if len(pieces) == 1:
        return pieces[0], pieces[0][:, :HD].T
    total = sum(piece.shape[0] for piece in pieces)
    low = lambda a, b: jax.ShapeDtypeStruct((a, b), jnp.bfloat16)
    return call(turn_kernel, (low(total, 2 * HD), low(HD, total)), pieces, "turn")


def attend_kernel(
    map_ref, me_ref, q_ref, *refs, blk, heads, parts, key_blocks, seq_blocks, reach
):
    pieces = refs[:parts]
    o_ref, low_ref, l_ref = refs[parts : parts + 3]
    chunk = pl.program_id(0)
    if parts > 1:
        kv_ref = refs[parts + 3]
        row = 0
        for piece in pieces:
            kv_ref[row : row + piece.shape[0], :] = piece[...]
            row += piece.shape[0]
    else:
        kv_ref = pieces[0]
    acc_ref, sum_ref, list_ref = refs[-3:]
    q_blocks = q_ref.shape[0] // blk

    @pl.when(chunk == 0)
    def _():
        acc_ref[...] = jnp.zeros_like(acc_ref)
        sum_ref[...] = jnp.zeros_like(sum_ref)

    def tile(b, slots, mask):
        rows = [pl.ds(pl.multiple_of(slot * blk, blk), blk) for slot in slots]
        cols = slice(b * blk, (b + 1) * blk)
        for h in range(heads):
            query = q_ref[cols, h * HD : (h + 1) * HD]
            part = result = None
            for row in rows:
                capped = jnp.tanh(matmul_nt(query, kv_ref[row, :HD]) * (1.0 / soft_cap))
                weights = jnp.exp2(capped * (soft_cap * LOG2E))
                if mask is not None:
                    weights = jnp.where(mask, weights, 0.0)
                for piece in range(0, blk, 128):
                    term = weights[:, piece : piece + 128]
                    part = term if part is None else part + term
                term = matmul(weights.astype(jnp.bfloat16), kv_ref[row, HD:])
                result = term if result is None else result + term
            sum_ref[cols, h * 128 : (h + 1) * 128] += part
            acc_ref[cols, h * HD : (h + 1) * HD] += result

    visit_blocks(
        map_ref, me_ref[0], chunk, q_blocks, key_blocks, seq_blocks, reach, parts > 1, list_ref,
        tile, blk, False,
    )

    @pl.when(chunk == pl.num_programs(0) - 1)
    def _():
        for b in range(q_blocks):
            for h in range(heads):
                at = (slice(b * blk, (b + 1) * blk), slice(h * HD, (h + 1) * HD))
                lanes = (slice(b * blk, (b + 1) * blk), slice(h * 128, (h + 1) * 128))
                total = jnp.sum(sum_ref[lanes], axis=-1, keepdims=True)
                result = acc_ref[at] / total
                o_ref[at] = result
                low_ref[at] = result.astype(jnp.bfloat16)
                l_ref[lanes] = jnp.broadcast_to(total, (blk, 128))


def attend(block_map, me, queries, pieces, blk, seq_blocks):
    rows, width = queries.shape
    heads = width // HD
    total = sum(piece.shape[0] for piece in pieces)
    joined = len(pieces) > 1
    chunk_rows = total if joined else min(total, KEY_CHUNK)
    kernel = partial(
        attend_kernel, blk=blk, heads=heads, parts=len(pieces), key_blocks=chunk_rows // blk,
        seq_blocks=seq_blocks, reach=WINDOW // blk,
    )
    whole = lambda i, *_: (0, 0)
    if joined:
        kv_specs = [pl.BlockSpec(piece.shape, whole) for piece in pieces]
    else:
        kv_specs = [pl.BlockSpec((chunk_rows, 2 * HD), lambda i, *_: (i, 0))]
    out_shape = [
        jax.ShapeDtypeStruct((rows, width), jnp.float32),
        jax.ShapeDtypeStruct((rows, width), jnp.bfloat16),
        jax.ShapeDtypeStruct((rows, heads * 128), jnp.float32),
    ]
    held = [pltpu.VMEM((total, 2 * HD), jnp.bfloat16)] if joined else []
    return pl.pallas_call(
        kernel,
        out_shape=tuple(out_shape),
        grid_spec=pltpu.PrefetchScalarGridSpec(
            num_scalar_prefetch=2,
            grid=(total // chunk_rows,),
            in_specs=[pl.BlockSpec((rows, width), whole), *kv_specs],
            out_specs=[pl.BlockSpec(shape.shape, whole) for shape in out_shape],
            scratch_shapes=[
                *held,
                pltpu.VMEM((rows, width), jnp.float32),
                pltpu.VMEM((rows, heads * 128), jnp.float32),
                pltpu.SMEM((chunk_rows // blk + 1,), jnp.int32),
            ],
        ),
        compiler_params=pltpu.CompilerParams(vmem_limit_bytes=MOST),
        cost_estimate=pl.CostEstimate(
            flops=4 * rows * width * total, bytes_accessed=8 * rows * width + 8 * total * HD,
            transcendentals=2 * rows * heads * total,
        ),
        name="attend",
    )(block_map, me, queries, *pieces)


def attend_back_kernel(
    map_ref, me_ref, da_ref, out_ref, o_ref, l_ref, q_ref, kv_ref, kt_ref, cos_ref, sin_ref, *refs,
    blk, heads, swapped, key_blocks, seq_blocks, reach
):
    dq_ref, *dkv_refs = refs[: 5 if swapped else 2]
    do_ref, stat_ref, dqt_ref, dk_ref, dv_ref, list_ref = refs[5 if swapped else 2 :]
    chunk = pl.program_id(0)
    q_blocks = q_ref.shape[0] // blk

    @pl.when(chunk == 0)
    def _():
        dqt_ref[...] = jnp.zeros_like(dqt_ref)
        for h in range(heads):
            at = slice(h * HD, (h + 1) * HD)
            out_grad = matmul(da_ref[...], out_ref[:, at]).astype(jnp.bfloat16)
            do_ref[:, at] = out_grad
            delta = jnp.sum(out_grad.astype(jnp.float32) * o_ref[:, at], axis=-1, keepdims=True)
            stat_ref[heads + h : heads + h + 1, :] = jnp.broadcast_to(
                delta, (delta.shape[0], 128)
            ).T[:1, :]
            stat_ref[h : h + 1, :] = jnp.log2(l_ref[:, h * 128 : (h + 1) * 128]).T[:1, :]

    dk_ref[...] = jnp.zeros_like(dk_ref)
    dv_ref[...] = jnp.zeros_like(dv_ref)

    def tile(b, slots, mask):
        rows = [pl.ds(pl.multiple_of(slot * blk, blk), blk) for slot in slots]
        cols = slice(b * blk, (b + 1) * blk)
        dk_parts, dv_parts = [None] * len(rows), [None] * len(rows)
        dq_parts = [None] * heads
        add = lambda total, term: term if total is None else total + term
        for h in range(heads):
            query = q_ref[cols, h * HD : (h + 1) * HD]
            out_grad = do_ref[cols, h * HD : (h + 1) * HD]
            log_total = stat_ref[h : h + 1, cols]
            delta = stat_ref[heads + h : heads + h + 1, cols]
            for k, row in enumerate(rows):
                tangent = jnp.tanh(matmul_nt(kv_ref[row, :HD], query) * (1.0 / soft_cap))
                probs = jnp.exp2(tangent * (soft_cap * LOG2E) - log_total)
                if mask is not None:
                    probs = jnp.where(mask, probs, 0.0)
                prob_grad = matmul_nt(kv_ref[row, HD:], out_grad)
                score = (probs * (prob_grad - delta) * (1.0 - tangent * tangent)).astype(jnp.bfloat16)
                dk_parts[k] = add(dk_parts[k], matmul(score, query))
                dv_parts[k] = add(dv_parts[k], matmul(probs.astype(jnp.bfloat16), out_grad))
                dq_parts[h] = add(dq_parts[h], matmul(kt_ref[:, row], score))
        for h in range(heads):
            dqt_ref[h * HD : (h + 1) * HD, cols] += dq_parts[h]
        for k, row in enumerate(rows):
            dk_ref[row, :] += dk_parts[k]
            dv_ref[row, :] += dv_parts[k]

    visit_blocks(
        map_ref, me_ref[0], chunk, q_blocks, key_blocks, seq_blocks, reach, swapped, list_ref,
        tile, blk, True,
    )

    row = 0
    for dkv_ref in dkv_refs:
        count = dkv_ref.shape[0]
        dkv_ref[:, :HD] = dk_ref[row : row + count, :].astype(jnp.bfloat16)
        dkv_ref[:, HD:] = dv_ref[row : row + count, :].astype(jnp.bfloat16)
        row += count

    @pl.when(chunk == pl.num_programs(0) - 1)
    def _():
        cosine, sine = cos_ref[...], sin_ref[...]
        for h in range(heads):
            low = dqt_ref[h * HD : h * HD + HALF, :].T * HD ** (-0.5)
            high = dqt_ref[h * HD + HALF : (h + 1) * HD, :].T * HD ** (-0.5)
            dq_ref[:, h * HD : h * HD + HALF] = (low * cosine + high * sine).astype(jnp.bfloat16)
            dq_ref[:, h * HD + HALF : (h + 1) * HD] = (high * cosine - low * sine).astype(
                jnp.bfloat16
            )


def attend_back(
    block_map, me, branch_low, full_out_t, attended, totals, queries, kv_all, key_turned, cosine,
    sine, blk, seq_blocks, swapped
):
    rows, width = queries.shape
    heads = width // HD
    depth = branch_low.shape[1]
    total = kv_all.shape[0]
    chunk_rows = total if swapped else min(total, KEY_CHUNK)
    kernel = partial(
        attend_back_kernel, blk=blk, heads=heads, swapped=swapped, key_blocks=chunk_rows // blk,
        seq_blocks=seq_blocks, reach=WINDOW // blk,
    )
    whole = lambda i, *_: (0, 0)
    parts = [3 * rows, rows, 3 * rows, rows] if swapped else [total]
    dkv_shapes = [jax.ShapeDtypeStruct((part, 2 * HD), jnp.bfloat16) for part in parts]
    dkv_specs = [
        pl.BlockSpec((min(part, chunk_rows), 2 * HD), lambda i, *_: (i, 0)) for part in parts
    ]
    return pl.pallas_call(
        kernel,
        out_shape=(jax.ShapeDtypeStruct((rows, width), jnp.bfloat16), *dkv_shapes),
        grid_spec=pltpu.PrefetchScalarGridSpec(
            num_scalar_prefetch=2,
            grid=(total // chunk_rows,),
            in_specs=[
                pl.BlockSpec((rows, depth), whole),
                pl.BlockSpec((depth, width), whole),
                pl.BlockSpec((rows, width), whole),
                pl.BlockSpec((rows, heads * 128), whole),
                pl.BlockSpec((rows, width), whole),
                pl.BlockSpec((chunk_rows, 2 * HD), lambda i, *_: (i, 0)),
                pl.BlockSpec((HD, chunk_rows), lambda i, *_: (0, i)),
                pl.BlockSpec((rows, HALF), whole),
                pl.BlockSpec((rows, HALF), whole),
            ],
            out_specs=[pl.BlockSpec((rows, width), whole), *dkv_specs],
            scratch_shapes=[
                pltpu.VMEM((rows, width), jnp.bfloat16),
                pltpu.VMEM((2 * heads, rows), jnp.float32),
                pltpu.VMEM((width, rows), jnp.float32),
                pltpu.VMEM((chunk_rows, HD), jnp.float32),
                pltpu.VMEM((chunk_rows, HD), jnp.float32),
                pltpu.SMEM((chunk_rows // blk + 1,), jnp.int32),
            ],
        ),
        compiler_params=pltpu.CompilerParams(vmem_limit_bytes=MOST),
        cost_estimate=pl.CostEstimate(
            flops=10 * rows * width * total, bytes_accessed=16 * rows * width + 10 * total * HD,
            transcendentals=2 * rows * heads * total,
        ),
        name="attend_back",
    )(
        block_map, me, branch_low, full_out_t, attended, totals, queries, kv_all, key_turned,
        cosine, sine,
    )


def body(
    tokens, block_map, w_query, w_key, w_value, w_out, w_gate, w_up, w_down, norm_gains, cotangent
):
    ctx_count = lax.axis_size("ctx")
    tok_dev, depth = tokens.shape
    block_rows = tok_dev // 2
    seq_count = max(1, ctx_count // 16)
    seq_len = tok_dev * ctx_count // seq_count
    seq_blocks = seq_len // block_rows
    me = lax.axis_index("ctx")
    me_list = me.reshape(1).astype(jnp.int32)
    heads_dev = w_query.shape[1] // HD
    q_width = heads_dev * HD
    flat_map = block_map.reshape(-1).astype(jnp.int32)
    pairs = paired()

    qkv_shard = pack(w_query, w_key, w_value, norm_gains.T)
    if pairs:
        qkv_pieces = gather_pieces(qkv_shard)
        out_shard = tie(w_out, qkv_pieces[3], qkv_pieces[4]).T
        out_near = nearby(out_shard)
    else:
        qkv_pieces = (lax.all_gather(qkv_shard, "ctx", axis=0, tiled=True),)
        out_pieces = (lax.all_gather(w_out.T, "ctx", axis=0, tiled=True),)
    own_ids = lax.dynamic_index_in_dim(block_map, me, 0, keepdims=False)
    offsets = jnp.arange(block_rows, dtype=jnp.int32)
    own_index = (own_ids[:, None] * block_rows + offsets[None, :]).reshape(-1)
    cosine, sine = angle_tables(own_index % seq_len)
    inputs = tokens.astype(jnp.float32)
    in_scale = rms_scale(inputs)
    unit_in = (inputs * in_scale).astype(jnp.bfloat16)
    queries, *kv_local = project(unit_in, cosine, sine, qkv_pieces, heads_dev)
    if pairs:
        kv_local, out_near = lax.optimization_barrier((kv_local, out_near))
        kv_near = nearby_halves(*kv_local)
        kv_pieces = gather_halves(*kv_local, kv_near)
        half = out_shard.shape[0] // 2
        out_far = (swap(out_near[0][:half], 4), swap(out_near[1][half:], 2))
        out_mine = tie_all((out_shard, *out_near, *out_far), *kv_pieces[6:8])
        out_pieces = out_mine + tuple(swap(part, 1) for part in out_mine)
        late = (*kv_pieces[2:8], *out_far)
    else:
        kv_pieces = (lax.all_gather(jnp.concatenate(kv_local), "ctx", axis=0, tiled=True),)
        late = kv_pieces
    w_gate, w_up, w_down, *_ = lax.optimization_barrier((w_gate, w_up, w_down, *late))
    if pairs:
        gate_near = nearby(w_gate)
    attended, attn_flat, totals = attend(
        flat_map, me_list, queries, kv_pieces, block_rows, seq_blocks
    )
    branch_part = out_project(attn_flat, out_pieces, depth)
    if pairs:
        branch_part, *gate_near = lax.optimization_barrier((branch_part, *gate_near))
        gate_pieces = gather_pieces(w_gate, gate_near)
        qkv_pieces = tie_all(qkv_pieces, branch_part)
    branch = lax.psum(branch_part, "tp")
    full_up = lax.all_gather(w_up, "ctx", axis=0, tiled=True)
    full_qkv = assemble(qkv_pieces)
    gains = full_qkv[:, q_width + 2 * HD : q_width + 2 * HD + 4].T.astype(jnp.float32)
    normed_in = (inputs * in_scale * gains[0]).astype(jnp.bfloat16)
    if pairs:
        down_shard, gains, normed_in, *far = lax.optimization_barrier(
            (w_down.T, gains, normed_in, *gate_pieces[3:5])
        )
        gate_pieces = (*gate_pieces[:3], *far, *gate_pieces[5:])
        down_near = nearby(down_shard)
        full_gate = assemble(gate_pieces, 3)
        full_gate, *down_near = lax.optimization_barrier((full_gate, *down_near))
        down_pieces = gather_pieces(down_shard, down_near)
    else:
        full_gate = lax.all_gather(w_gate, "ctx", axis=0, tiled=True)
        down_pieces = (lax.all_gather(w_down.T, "ctx", axis=0, tiled=True),)
    branch, full_gate, full_up, *near = lax.optimization_barrier(
        (branch, full_gate, full_up, *down_pieces[:3])
    )
    normed_mid = by_rows(mid_kernel, (tokens, branch), gains, (jnp.bfloat16,), 0, "mid_norms")
    if pairs:
        normed_mid, *far = lax.optimization_barrier((normed_mid, *down_pieces[3:5]))
        mine = (*near, *far)
        down_pieces = (*mine, *(swap(part, 1) for part in mine))
    hidden, active, slope = units(normed_mid, full_gate, full_up)
    mlp_part = out_project(hidden, down_pieces, depth, "project_down")
    mlp_part, out_pieces, kv_pieces, down_pieces = lax.optimization_barrier(
        (mlp_part, out_pieces, kv_pieces, down_pieces)
    )
    full_down_t = assemble(down_pieces, 3)
    full_out_t = assemble(out_pieces)
    kv_all, key_turned = turn(kv_pieces)
    mlp_out = lax.psum(mlp_part, "tp")
    mlp_out, full_out_t, kv_all, key_turned, full_down_t = lax.optimization_barrier(
        (mlp_out, full_out_t, kv_all, key_turned, full_down_t)
    )
    result, mlp_low, gain_four = by_rows(
        top_kernel, (tokens, branch, mlp_out, cotangent), gains, (jnp.bfloat16, jnp.bfloat16), 1,
        "top_norms",
    )
    gate_low, up_low = units_back(mlp_low, full_down_t, active, slope)
    mid_part = features_back(gate_low, up_low, full_gate, full_up)
    mid_part, hidden_t, mlp_t, gate_t, up_t = lax.optimization_barrier(
        (mid_part, hidden, mlp_low, gate_low, up_low)
    )
    mid_sum = lax.psum(mid_part, "tp")
    down_grad = matmul(hidden_t.T, mlp_t).astype(jnp.bfloat16)
    down_shard = lax.psum_scatter(down_grad, "ctx", scatter_dimension=1, tiled=True)
    gate_grad = matmul(normed_mid.T, gate_t).astype(jnp.bfloat16)
    gate_blocks = scatter_start(gate_grad)
    up_grad = matmul(normed_mid.T, up_t).astype(jnp.bfloat16)
    up_grad, gate_blocks = lax.optimization_barrier((up_grad, gate_blocks))
    gate_terms = scatter_finish(gate_blocks)
    up_chips = scatter_chips(up_grad)
    mid_sum, up_chips = lax.optimization_barrier((mid_sum, up_chips))
    resid_grad, branch_low, gain_mid = by_rows(
        low_kernel, (tokens, branch, mid_sum, cotangent), gains, (jnp.float32, jnp.bfloat16), 2,
        "low_norms",
    )
    query_low, *kv_terms = attend_back(
        flat_map, me_list, branch_low, full_out_t, attended, totals, queries, kv_all, key_turned,
        cosine, sine, block_rows, seq_blocks, pairs,
    )
    *kv_terms, down_shard, gate_terms = lax.optimization_barrier((*kv_terms, down_shard, gate_terms))
    gate_shard = add_terms(gate_terms)
    if pairs:
        far = kv_terms[1] + swap(kv_terms[3], 1)
        near = kv_terms[0] + swap(kv_terms[2], 1)
        blocks = (near[k * tok_dev : (k + 1) * tok_dev] for k in range(3))
        kv_sums = scatter_finish(scatter_corner(*blocks, far))
    else:
        kv_sums = (lax.psum_scatter(kv_terms[0], "ctx", scatter_dimension=0, tiled=True),)
    qkv_low, in_part = join(cosine, sine, query_low, full_qkv, kv_sums)
    in_part, qkv_low, branch_t, up_chips = lax.optimization_barrier(
        (in_part, qkv_low, branch_low, up_chips)
    )
    in_sum = lax.psum(in_part, "tp")
    up_shard = add_terms(scatter_finish(scatter_blocks(up_chips)))
    gain_one = jnp.sum(in_part.astype(jnp.float32) * (inputs * in_scale), axis=0)
    gain_one = sum_small_tp(gain_one)
    gains_shard = scatter_gains(jnp.concatenate([gain_one[None], gain_mid[1:], gain_mid[:1], gain_four]))
    qkv_grad = matmul(normed_in.T, qkv_low).astype(jnp.bfloat16)
    qkv_shard = add_terms(scatter_finish(scatter_start(qkv_grad)))
    out_weight_grad = matmul(branch_t.T, attn_flat).astype(jnp.bfloat16)
    out_grad_t = add_terms(scatter_finish(scatter_start(out_weight_grad)))
    shards = (
        qkv_shard[:, :q_width],
        qkv_shard[:, q_width : q_width + HD],
        qkv_shard[:, q_width + HD :],
        out_grad_t.T,
        gate_shard,
        up_shard,
        down_shard.astype(jnp.float32),
        gains_shard,
    )
    input_grad = by_rows(
        end_kernel, (tokens, in_sum, resid_grad), gains, (jnp.float32,), 0, "end_norms"
    )
    return (result, input_grad, *shards)


def solution(mesh):
    in_specs = (
        P("ctx", None),
        P(),
        P("ctx", "tp"),
        P("ctx", "tp"),
        P("ctx", "tp"),
        P("tp", "ctx"),
        P("ctx", "tp"),
        P("ctx", "tp"),
        P("tp", "ctx"),
        P(None, "ctx"),
        P("ctx", None),
    )
    out_specs = (
        P("ctx", None),
        P("ctx", None),
        P("ctx", "tp"),
        P("ctx", "tp"),
        P("ctx", "tp"),
        P("tp", "ctx"),
        P("ctx", "tp"),
        P("ctx", "tp"),
        P("tp", "ctx"),
        P(None, "ctx"),
    )
    return jax.shard_map(body, mesh=mesh, in_specs=in_specs, out_specs=out_specs, check_vma=False)
```

```python
from functools import partial

import jax
import jax.numpy as jnp
from jax import lax
from jax.experimental import pallas as pl
from jax.experimental.pallas import tpu as pltpu
from jax.sharding import PartitionSpec as P

HD = 256
HALF = 128
WINDOW = 4096
KEY_CHUNK = 4096
MOST = 60 * 2**20


epsilon = 1e-06
soft_cap = 50.0
LOG2E = 1.4426950408889634


def rms_scale(values):
    return lax.rsqrt(jnp.mean(values * values, axis=-1, keepdims=True) + epsilon)


def angle_tables(positions):
    frequency = jnp.power(10000.0, -2.0 * jnp.arange(HALF, dtype=jnp.float32) / HD)
    phases = positions.astype(jnp.float32)[:, None] * frequency[None, :]
    return (jnp.cos(phases), jnp.sin(phases))


def matmul(left, right):
    return jnp.dot(left, right, preferred_element_type=jnp.float32)


def matmul_nt(left, right):
    return lax.dot_general(left, right, (((1,), (1,)), ((), ())), preferred_element_type=jnp.float32)


def tie(value, *others):
    return lax.optimization_barrier((value,) + others)[0]


def tie_all(values, *others):
    return lax.optimization_barrier((*values, *others))[: len(values)]


def call(kernel, out_shape, args, name, scalars=0, scratch=(), flops=0, mem=32, space=None):
    spec = pl.BlockSpec(memory_space=pltpu.VMEM if space is None else space)
    outs = jax.tree.map(lambda _: spec, out_shape)
    size = sum(a.size * a.dtype.itemsize for a in args)
    size += sum(a.size * a.dtype.itemsize for a in jax.tree.leaves(out_shape))
    return pl.pallas_call(
        kernel,
        out_shape=out_shape,
        in_specs=[pl.BlockSpec(memory_space=pltpu.SMEM)] * scalars + [spec] * (len(args) - scalars),
        out_specs=outs,
        scratch_shapes=list(scratch),
        compiler_params=pltpu.CompilerParams(vmem_limit_bytes=mem * 2**20),
        cost_estimate=pl.CostEstimate(flops=flops, bytes_accessed=size, transcendentals=0),
        name=name,
    )(*args)


def swap(value, bit):
    pairs = [(i, i ^ bit) for i in range(lax.axis_size("ctx"))]
    return lax.ppermute(value, "ctx", pairs)


def paired():
    return lax.axis_size("ctx") == 8


def nearby(piece):
    return swap(piece, 2), swap(piece, 4)


def gather_pieces(piece, near=None):
    half = piece.shape[0] // 2
    by_x, by_y = nearby(piece) if near is None else near
    mine = (piece, by_x, by_y, swap(by_x[:half], 4), swap(by_y[half:], 2))
    return mine + tuple(swap(part, 1) for part in mine)


def nearby_halves(low, high):
    first = (swap(low, 2), swap(high, 4))
    return first[0], swap(high, 2), swap(low, 4), first[1]


def gather_halves(low, high, near=None):
    near = nearby_halves(low, high) if near is None else near
    mine = (low, high, *near, swap(near[0], 4), swap(near[3], 2))
    return mine + tuple(swap(part, 1) for part in mine)


def piece_rows(rows, halves):
    me = lax.axis_index("ctx")
    if halves:
        bits = [bit for core in (0, 1) for bit in (0, 2, 4, 6) for _ in range(2)]
        shift = [0, rows // 2] * 8
        places = [(me ^ (bit + k // 8)) * rows for k, bit in enumerate(bits)]
    else:
        places = [(me ^ bit) * rows for bit in (0, 2, 4, 6, 6, 1, 3, 5, 7, 7)]
        shift = [0, 0, 0, 0, rows // 2] * 2
    return jnp.stack(places).astype(jnp.int32) + jnp.array(shift, jnp.int32)


def places_of(pieces):
    if len(pieces) == 1:
        return jnp.zeros((1,), jnp.int32)
    rows = sum(piece.shape[0] for piece in pieces) // 8
    return piece_rows(rows, len(pieces) == 16)


def place(rows_ref, pieces, whole_ref):
    for k, piece in enumerate(pieces):
        whole_ref[pl.ds(pl.multiple_of(rows_ref[k], 16), piece.shape[0]), :] = piece[...]


def assemble_kernel(rows_ref, *refs):
    place(rows_ref, refs[:-1], refs[-1])


def assemble(pieces, grid=1):
    if len(pieces) == 1:
        return pieces[0]
    rows, width = sum(piece.shape[0] for piece in pieces) // 8, pieces[0].shape[1]
    column = lambda n: pl.BlockSpec((n, width // grid), lambda i: (0, i))
    return pl.pallas_call(
        assemble_kernel,
        out_shape=jax.ShapeDtypeStruct((8 * rows, width), pieces[0].dtype),
        grid=(grid,),
        in_specs=[pl.BlockSpec(memory_space=pltpu.SMEM)] + [column(p.shape[0]) for p in pieces],
        out_specs=column(8 * rows),
        compiler_params=pltpu.CompilerParams(vmem_limit_bytes=MOST),
        cost_estimate=pl.CostEstimate(flops=0, bytes_accessed=32 * rows * width, transcendentals=0),
        name="assemble",
    )(places_of(pieces), *pieces)


def scatter_corner(own, by_x, by_y, corner):
    half = own.shape[0] // 2
    from_x = swap(corner[:half], 2)
    from_y = swap(corner[half:], 4)
    by_y = jnp.concatenate([by_y[:half] + from_x, by_y[half:]], axis=0)
    by_x = jnp.concatenate([by_x[:half], by_x[half:] + from_y], axis=0)
    return own, by_x, by_y


def scatter_chips(whole):
    if not paired():
        return lax.psum_scatter(whole, "ctx", scatter_dimension=0, tiled=True)
    core = lax.axis_index("ctx") % 2
    blocks = whole.reshape(4, 2, whole.shape[0] // 8, whole.shape[1])
    theirs = lax.dynamic_index_in_dim(blocks, 1 - core, 1, keepdims=False)
    mine = lax.dynamic_index_in_dim(blocks, core, 1, keepdims=False)
    return mine + swap(theirs, 1)


def scatter_blocks(chips):
    if not paired():
        return (chips,)
    chip = lax.axis_index("ctx") // 2
    pick = lambda bits: lax.dynamic_index_in_dim(chips, chip ^ bits, 0, keepdims=False)
    return scatter_corner(pick(0), pick(1), pick(2), pick(3))


def scatter_start(whole):
    return scatter_blocks(scatter_chips(whole))


def scatter_finish(blocks):
    if len(blocks) == 1:
        return blocks
    own, by_x, by_y = blocks
    return own, swap(by_x, 2), swap(by_y, 4)


def add_terms(terms):
    total = terms[0].astype(jnp.float32)
    for term in terms[1:]:
        total = total + term.astype(jnp.float32)
    return total


def scatter_gains(whole):
    if not paired():
        return lax.psum_scatter(whole, "ctx", scatter_dimension=1, tiled=True)
    me = lax.axis_index("ctx")
    columns = whole.shape[1] // 8
    stack = whole.reshape(whole.shape[0], 8, columns).transpose(1, 0, 2)
    for bit in (4, 2, 1):
        half = stack.shape[0] // 2
        low = (me & bit) == 0
        theirs = jnp.where(low, stack[half:], stack[:half])
        mine = jnp.where(low, stack[:half], stack[half:])
        stack = mine + swap(theirs, bit)
    return stack[0]


def sum_small_tp(value):
    count = lax.axis_size("tp")
    bit = 1
    while bit < count:
        value = value + lax.ppermute(value, "tp", [(i, i ^ bit) for i in range(count)])
        bit *= 2
    return value


def pack_kernel(a_ref, b_ref, c_ref, gains_ref, out_ref):
    one, two = a_ref.shape[1], a_ref.shape[1] + b_ref.shape[1]
    three = two + c_ref.shape[1]
    out_ref[:, :one] = a_ref[...]
    out_ref[:, one:two] = b_ref[...]
    out_ref[:, two:three] = c_ref[...]
    lane = lax.broadcasted_iota(jnp.int32, (gains_ref.shape[0], HALF), 1)
    columns = jnp.broadcast_to(gains_ref[:, :1], lane.shape)
    for k in range(1, gains_ref.shape[1]):
        columns = jnp.where(lane == k, jnp.broadcast_to(gains_ref[:, k : k + 1], lane.shape), columns)
    out_ref[:, three:] = columns


def pack(first, second, third, gains):
    width = first.shape[1] + second.shape[1] + third.shape[1] + HALF
    shape = jax.ShapeDtypeStruct((first.shape[0], width), first.dtype)
    return call(pack_kernel, shape, (first, second, third, gains), "pack")


def project_kernel(rows_ref, in_ref, cos_ref, sin_ref, *refs, heads, parts):
    pieces, q_ref, kv_refs = refs[:parts], refs[parts], refs[parts + 1 : parts + 3]
    block = kv_refs[0].shape[0]
    if parts > 1:
        full_ref = refs[parts + 3]
        place(rows_ref, pieces, full_ref)
    else:
        full_ref = pieces[0]
    gain = full_ref[:, (heads + 2) * HD : (heads + 2) * HD + 1].astype(jnp.float32)
    for n in range(heads + 2):
        weight = (full_ref[:, n * HD : (n + 1) * HD].astype(jnp.float32) * gain).astype(jnp.bfloat16)
        raw = matmul(in_ref[...], weight)
        if n <= heads:
            low, high = raw[:, :HALF], raw[:, HALF:]
            cosine, sine = cos_ref[...], sin_ref[...]
            low, high = low * cosine - high * sine, high * cosine + low * sine
            if n < heads:
                q_ref[:, n * HD : n * HD + HALF] = (low * HD ** (-0.5)).astype(jnp.bfloat16)
                q_ref[:, n * HD + HALF : (n + 1) * HD] = (high * HD ** (-0.5)).astype(jnp.bfloat16)
            else:
                for k, kv_ref in enumerate(kv_refs):
                    rows = slice(k * block, (k + 1) * block)
                    kv_ref[:, :HALF] = low[rows].astype(jnp.bfloat16)
                    kv_ref[:, HALF:HD] = high[rows].astype(jnp.bfloat16)
        else:
            for k, kv_ref in enumerate(kv_refs):
                kv_ref[:, HD:] = raw[k * block : (k + 1) * block].astype(jnp.bfloat16)


def project(normed, cosine, sine, pieces, heads):
    rows, depth = normed.shape
    width = pieces[0].shape[1]
    low = lambda m, n: jax.ShapeDtypeStruct((m, n), jnp.bfloat16)
    scratch = [pltpu.VMEM((depth, width), jnp.bfloat16)] if len(pieces) > 1 else []
    return call(
        partial(project_kernel, heads=heads, parts=len(pieces)),
        (low(rows, heads * HD), low(rows // 2, 2 * HD), low(rows // 2, 2 * HD)),
        (places_of(pieces), normed, cosine, sine, *pieces), "project", scalars=1, scratch=scratch,
        flops=2 * rows * depth * width,
    )


def out_project_kernel(rows_ref, attn_ref, *refs, parts):
    pieces, branch_ref = refs[:parts], refs[parts]
    if parts > 1:
        full_ref = refs[parts + 1]
        place(rows_ref, pieces, full_ref)
    else:
        full_ref = pieces[0]
    for n in range(0, branch_ref.shape[1], 256):
        part = matmul_nt(attn_ref[...], full_ref[n : n + 256, :])
        branch_ref[:, n : n + 256] = part.astype(jnp.bfloat16)


def out_project(attn, pieces, depth, name="out_project"):
    rows, width = attn.shape
    scratch = [pltpu.VMEM((depth, width), jnp.bfloat16)] if len(pieces) > 1 else []
    return call(
        partial(out_project_kernel, parts=len(pieces)),
        jax.ShapeDtypeStruct((rows, depth), jnp.bfloat16), (places_of(pieces), attn, *pieces),
        name, scalars=1, scratch=scratch, flops=2 * rows * depth * width,
    )


def join_kernel(cos_ref, sin_ref, query_ref, full_ref, *refs):
    *terms, low_ref, part_ref = refs
    total = terms[0][...].astype(jnp.float32)
    for term in terms[1:]:
        total = total + term[...].astype(jnp.float32)
    width = query_ref.shape[1]
    cosine, sine = cos_ref[...], sin_ref[...]
    low, high = total[:, :HALF], total[:, HALF:HD]
    low_ref[:, :width] = query_ref[...]
    low_ref[:, width : width + HALF] = (low * cosine + high * sine).astype(jnp.bfloat16)
    low_ref[:, width + HALF : width + HD] = (high * cosine - low * sine).astype(jnp.bfloat16)
    low_ref[:, width + HD :] = total[:, HD:].astype(jnp.bfloat16)
    for n in range(0, part_ref.shape[1], 256):
        part = matmul_nt(low_ref[...], full_ref[n : n + 256, : low_ref.shape[1]])
        part_ref[:, n : n + 256] = part.astype(jnp.bfloat16)


def join(cosine, sine, query_low, full_qkv, terms):
    rows = query_low.shape[0]
    depth, width = full_qkv.shape[0], query_low.shape[1] + 2 * HD
    low = lambda n: jax.ShapeDtypeStruct((rows, n), jnp.bfloat16)
    return call(
        join_kernel, (low(width), low(depth)), (cosine, sine, query_low, full_qkv, *terms), "join",
        flops=2 * rows * depth * width,
    )


GROUP = 16


def rms_of(values):
    return lax.rsqrt(jnp.mean(values * values, axis=-1, keepdims=True) + epsilon)


def norm_back(normed, scale, weighted):
    return scale * (weighted - normed * jnp.mean(weighted * normed, axis=-1, keepdims=True))


def fold(values):
    total = values[:8]
    for row in range(8, values.shape[0], 8):
        total = total + values[row : row + 8]
    return total


def wide(ref, rows):
    return ref[rows, :].astype(jnp.float32)


def walk(count, step):
    def run(index, carry):
        step(pl.ds(pl.multiple_of(index * GROUP, GROUP), GROUP))
        return carry

    lax.fori_loop(0, count // GROUP, run, 0, unroll=8)


def mid_kernel(tok_ref, branch_ref, gains_ref, out_ref):
    def step(rows):
        branch = wide(branch_ref, rows)
        residual = wide(tok_ref, rows) + branch * rms_of(branch) * gains_ref[1:2, :]
        out_ref[rows, :] = (residual * rms_of(residual) * gains_ref[2:3, :]).astype(jnp.bfloat16)

    walk(tok_ref.shape[0], step)


def top_kernel(tok_ref, branch_ref, mlp_ref, cot_ref, gains_ref, out_ref, grad_ref, sum_ref, acc_ref):
    @pl.when(pl.program_id(0) == 0)
    def _():
        acc_ref[...] = jnp.zeros_like(acc_ref)

    def step(rows):
        branch = wide(branch_ref, rows)
        residual = wide(tok_ref, rows) + branch * rms_of(branch) * gains_ref[1:2, :]
        mlp = wide(mlp_ref, rows)
        scale = rms_of(mlp)
        normed = mlp * scale
        out_ref[rows, :] = (residual + normed * gains_ref[3:4, :]).astype(jnp.bfloat16)
        out_grad = wide(cot_ref, rows)
        acc_ref[...] += fold(out_grad * normed)
        grad_ref[rows, :] = norm_back(normed, scale, out_grad * gains_ref[3:4, :]).astype(jnp.bfloat16)

    walk(tok_ref.shape[0], step)

    @pl.when(pl.program_id(0) == pl.num_programs(0) - 1)
    def _():
        sum_ref[...] = jnp.sum(acc_ref[...], axis=0, keepdims=True)


def low_kernel(
    tok_ref, branch_ref, mid_ref, cot_ref, gains_ref, resid_ref, grad_ref, sum_ref, acc_ref
):
    @pl.when(pl.program_id(0) == 0)
    def _():
        acc_ref[...] = jnp.zeros_like(acc_ref)

    def step(rows):
        branch = wide(branch_ref, rows)
        branch_scale = rms_of(branch)
        branch_normed = branch * branch_scale
        residual = wide(tok_ref, rows) + branch_normed * gains_ref[1:2, :]
        scale = rms_of(residual)
        normed = residual * scale
        mid_grad = wide(mid_ref, rows)
        acc_ref[:8, :] += fold(mid_grad * normed)
        grad = wide(cot_ref, rows) + norm_back(normed, scale, mid_grad * gains_ref[2:3, :])
        resid_ref[rows, :] = grad
        acc_ref[8:, :] += fold(grad * branch_normed)
        grad_ref[rows, :] = norm_back(
            branch_normed, branch_scale, grad * gains_ref[1:2, :]
        ).astype(jnp.bfloat16)

    walk(tok_ref.shape[0], step)

    @pl.when(pl.program_id(0) == pl.num_programs(0) - 1)
    def _():
        sum_ref[0:1, :] = jnp.sum(acc_ref[:8, :], axis=0, keepdims=True)
        sum_ref[1:2, :] = jnp.sum(acc_ref[8:, :], axis=0, keepdims=True)


def end_kernel(tok_ref, sum_ref, resid_ref, gains_ref, out_ref):
    def step(rows):
        values = wide(tok_ref, rows)
        scale = rms_of(values)
        weighted = wide(sum_ref, rows) * gains_ref[0:1, :]
        out_ref[rows, :] = resid_ref[rows, :] + norm_back(values * scale, scale, weighted)

    walk(tok_ref.shape[0], step)


def by_rows(kernel, args, gains, kinds, sums, name, block=128):
    rows, depth = args[0].shape
    tile = pl.BlockSpec((block, depth), lambda i: (i, 0))
    ahead = pl.BlockSpec((block, depth), lambda i: (i, 0))
    whole = lambda n: pl.BlockSpec((n, depth), lambda i: (0, 0))
    shapes = [jax.ShapeDtypeStruct((rows, depth), kind) for kind in kinds]
    out_specs = [tile] * len(kinds)
    scratch = []
    if sums:
        shapes.append(jax.ShapeDtypeStruct((sums, depth), jnp.float32))
        out_specs.append(whole(sums))
        scratch.append(pltpu.VMEM((8 * sums, depth), jnp.float32))
    size = sum(a.size * a.dtype.itemsize for a in (*args, *shapes))
    found = pl.pallas_call(
        kernel,
        out_shape=tuple(shapes),
        grid=(rows // block,),
        in_specs=[ahead] * len(args) + [whole(gains.shape[0])],
        out_specs=out_specs,
        scratch_shapes=scratch,
        compiler_params=pltpu.CompilerParams(vmem_limit_bytes=MOST),
        cost_estimate=pl.CostEstimate(flops=0, bytes_accessed=size, transcendentals=0),
        name=name,
    )(*args, gains)
    return found if len(found) > 1 else found[0]


UNITS = 768
STEP = 256


def units_kernel(in_ref, gate_ref, up_ref, hidden_ref, active_ref, slope_ref):
    for n in range(0, UNITS, UNITS):
        at = slice(n, n + UNITS)
        gate = matmul(in_ref[...], gate_ref[:, at])
        up = matmul(in_ref[...], up_ref[:, at])
        root = (2.0 / jnp.pi) ** 0.5
        square = gate * gate
        bend = jnp.tanh(root * gate * (1.0 + 0.044715 * square))
        half = 0.5 * (1.0 + bend)
        active = gate * half
        slope = half + 0.5 * gate * (1.0 - bend * bend) * (root * (1.0 + 3 * 0.044715 * square))
        hidden_ref[:, at] = (active * up).astype(jnp.bfloat16)
        active_ref[:, at] = active.astype(jnp.bfloat16)
        slope_ref[:, at] = (slope * up).astype(jnp.bfloat16)


def units(normed, full_gate, full_up):
    rows, depth = normed.shape
    count = full_gate.shape[1]
    column = lambda n: pl.BlockSpec((n, UNITS), lambda i: (0, i))
    ahead = pl.BlockSpec((depth, UNITS), lambda i: (0, i))
    return pl.pallas_call(
        units_kernel,
        out_shape=tuple(jax.ShapeDtypeStruct((rows, count), jnp.bfloat16) for _ in range(3)),
        grid=(count // UNITS,),
        in_specs=[pl.BlockSpec((rows, depth), lambda i: (0, 0)), ahead, ahead],
        out_specs=[column(rows)] * 3,
        compiler_params=pltpu.CompilerParams(vmem_limit_bytes=MOST),
        cost_estimate=pl.CostEstimate(
            flops=4 * rows * depth * count, bytes_accessed=4 * depth * count,
            transcendentals=rows * count,
        ),
        name="units",
    )(normed, full_gate, full_up)


def units_back_kernel(grad_ref, down_ref, active_ref, slope_ref, dg_ref, du_ref):
    for n in range(0, UNITS, STEP):
        at = slice(n, n + STEP)
        hidden_grad = matmul(grad_ref[...], down_ref[:, at])
        dg_ref[:, at] = (hidden_grad * slope_ref[:, at].astype(jnp.float32)).astype(jnp.bfloat16)
        du_ref[:, at] = (hidden_grad * active_ref[:, at].astype(jnp.float32)).astype(jnp.bfloat16)


def units_back(mlp_low, full_down_t, active, slope):
    rows, depth = mlp_low.shape
    count = active.shape[1]
    column = lambda n: pl.BlockSpec((n, UNITS), lambda i: (0, i))
    ahead = pl.BlockSpec((depth, UNITS), lambda i: (0, i))
    return pl.pallas_call(
        units_back_kernel,
        out_shape=tuple(jax.ShapeDtypeStruct((rows, count), jnp.bfloat16) for _ in range(2)),
        grid=(count // UNITS,),
        in_specs=[pl.BlockSpec((rows, depth), lambda i: (0, 0)), ahead, column(rows), column(rows)],
        out_specs=[column(rows)] * 2,
        compiler_params=pltpu.CompilerParams(vmem_limit_bytes=MOST),
        cost_estimate=pl.CostEstimate(
            flops=2 * rows * depth * count, bytes_accessed=2 * depth * count, transcendentals=0
        ),
        name="units_back",
    )(mlp_low, full_down_t, active, slope)


def features_back_kernel(dg_ref, du_ref, gate_ref, up_ref, out_ref):
    for n in range(0, UNITS, STEP):
        at = slice(n, n + STEP)
        part = matmul_nt(dg_ref[...], gate_ref[at, :]) + matmul_nt(du_ref[...], up_ref[at, :])
        out_ref[:, at] = part.astype(jnp.bfloat16)


def features_back(gate_low, up_low, full_gate, full_up):
    rows, count = gate_low.shape
    depth = full_gate.shape[0]
    whole = pl.BlockSpec((rows, count), lambda i: (0, 0))
    tile = pl.BlockSpec((UNITS, count), lambda i: (i, 0))
    return pl.pallas_call(
        features_back_kernel,
        out_shape=jax.ShapeDtypeStruct((rows, depth), jnp.bfloat16),
        grid=(depth // UNITS,),
        in_specs=[whole, whole, tile, tile],
        out_specs=pl.BlockSpec((rows, UNITS), lambda i: (0, i)),
        compiler_params=pltpu.CompilerParams(vmem_limit_bytes=MOST),
        cost_estimate=pl.CostEstimate(
            flops=4 * rows * depth * count, bytes_accessed=4 * depth * count, transcendentals=0
        ),
        name="features_back",
    )(gate_low, up_low, full_gate, full_up)


def slot_block(map_ref, me, slot, swapped):
    device = slot >> 1
    if swapped:
        device = me ^ (((device & 3) << 1) | (device >> 2))
    return map_ref[device * 2 + (slot & 1)]


def block_list(lookup, key_blocks, own, seq_blocks, reach, list_ref):
    def look(slot, count):
        other = lookup(slot)
        gap = own - other
        whole = (gap > 0) & (gap < reach) & (own // seq_blocks == other // seq_blocks)
        list_ref[count] = slot
        return count + whole.astype(jnp.int32)

    return lax.fori_loop(0, key_blocks, look, jnp.int32(0))


def find_block(lookup, key_blocks, wanted):
    def look(slot, found):
        return jnp.where(lookup(slot) == wanted, slot, found)

    return lax.fori_loop(0, key_blocks, look, jnp.int32(-1))


def visit_blocks(map_ref, me, chunk, q_blocks, key_blocks, seq_blocks, reach, swapped, list_ref, tile, blk, keys_first):
    first = chunk * key_blocks
    lookup = lambda slot: slot_block(map_ref, me, first + slot, swapped)
    row_no = lax.broadcasted_iota(jnp.int32, (blk, blk), 0)
    col_no = lax.broadcasted_iota(jnp.int32, (blk, blk), 1)
    query_no, key_no = (col_no, row_no) if keys_first else (row_no, col_no)
    for b in range(q_blocks):
        own = map_ref[me * q_blocks + b]
        count = block_list(lookup, key_blocks, own, seq_blocks, reach, list_ref)

        def four(step, carry):
            tile(b, tuple(list_ref[4 * step + k] for k in range(4)), None)
            return carry

        lax.fori_loop(0, count // 4, four, 0)

        @pl.when(count % 4 >= 2)
        def _():
            first = (count // 4) * 4
            tile(b, (list_ref[first], list_ref[first + 1]), None)

        @pl.when(count % 2 == 1)
        def _():
            tile(b, (list_ref[count - 1],), None)

        diagonal = find_block(lookup, key_blocks, own)

        @pl.when(diagonal >= 0)
        def _():
            tile(b, (diagonal,), query_no >= key_no)

        if reach < seq_blocks:
            edge = find_block(lookup, key_blocks, own - reach)

            @pl.when((edge >= 0) & (own % seq_blocks >= reach))
            def _():
                tile(b, (edge,), query_no < key_no)


def turn_kernel(*refs):
    *pieces, whole_ref, turned_ref = refs
    row = 0
    for piece in pieces:
        count = piece.shape[0]
        whole_ref[row : row + count, :] = piece[...]
        turned_ref[:, row : row + count] = piece[:, :HD].T
        row += count


def turn(pieces):
    if len(pieces) == 1:
        return pieces[0], pieces[0][:, :HD].T
    total = sum(piece.shape[0] for piece in pieces)
    low = lambda a, b: jax.ShapeDtypeStruct((a, b), jnp.bfloat16)
    return call(turn_kernel, (low(total, 2 * HD), low(HD, total)), pieces, "turn")


def attend_kernel(
    map_ref, me_ref, q_ref, *refs, blk, heads, parts, key_blocks, seq_blocks, reach
):
    pieces = refs[:parts]
    o_ref, low_ref, l_ref = refs[parts : parts + 3]
    chunk = pl.program_id(0)
    if parts > 1:
        kv_ref = refs[parts + 3]
        row = 0
        for piece in pieces:
            kv_ref[row : row + piece.shape[0], :] = piece[...]
            row += piece.shape[0]
    else:
        kv_ref = pieces[0]
    acc_ref, sum_ref, list_ref = refs[-3:]
    q_blocks = q_ref.shape[0] // blk

    @pl.when(chunk == 0)
    def _():
        acc_ref[...] = jnp.zeros_like(acc_ref)
        sum_ref[...] = jnp.zeros_like(sum_ref)

    def tile(b, slots, mask):
        rows = [pl.ds(pl.multiple_of(slot * blk, blk), blk) for slot in slots]
        cols = slice(b * blk, (b + 1) * blk)
        if mask is None:
            query = jnp.concatenate([q_ref[cols, h * HD : (h + 1) * HD] for h in range(heads)], axis=0)
            part, held = None, []
            for row in rows:
                capped = jnp.tanh(matmul_nt(query, kv_ref[row, :HD]) * (1.0 / soft_cap))
                weights = jnp.exp2(capped * (soft_cap * LOG2E))
                for piece in range(0, blk, 128):
                    term = weights[:, piece : piece + 128]
                    part = term if part is None else part + term
                held.append(weights.astype(jnp.bfloat16))
            values = jnp.concatenate([kv_ref[row, HD:] for row in rows], axis=0)
            result = matmul(jnp.concatenate(held, axis=1), values)
            for h in range(heads):
                sum_ref[cols, h * 128 : (h + 1) * 128] += part[h * blk : (h + 1) * blk]
                acc_ref[cols, h * HD : (h + 1) * HD] += result[h * blk : (h + 1) * blk]
            return
        for h in range(heads):
            query = q_ref[cols, h * HD : (h + 1) * HD]
            part = result = None
            for row in rows:
                capped = jnp.tanh(matmul_nt(query, kv_ref[row, :HD]) * (1.0 / soft_cap))
                weights = jnp.exp2(capped * (soft_cap * LOG2E))
                if mask is not None:
                    weights = jnp.where(mask, weights, 0.0)
                for piece in range(0, blk, 128):
                    term = weights[:, piece : piece + 128]
                    part = term if part is None else part + term
                term = matmul(weights.astype(jnp.bfloat16), kv_ref[row, HD:])
                result = term if result is None else result + term
            sum_ref[cols, h * 128 : (h + 1) * 128] += part
            acc_ref[cols, h * HD : (h + 1) * HD] += result

    visit_blocks(
        map_ref, me_ref[0], chunk, q_blocks, key_blocks, seq_blocks, reach, parts > 1, list_ref,
        tile, blk, False,
    )

    @pl.when(chunk == pl.num_programs(0) - 1)
    def _():
        for b in range(q_blocks):
            for h in range(heads):
                at = (slice(b * blk, (b + 1) * blk), slice(h * HD, (h + 1) * HD))
                lanes = (slice(b * blk, (b + 1) * blk), slice(h * 128, (h + 1) * 128))
                total = jnp.sum(sum_ref[lanes], axis=-1, keepdims=True)
                result = acc_ref[at] / total
                o_ref[at] = result
                low_ref[at] = result.astype(jnp.bfloat16)
                l_ref[lanes] = jnp.broadcast_to(total, (blk, 128))


def attend(block_map, me, queries, pieces, blk, seq_blocks):
    rows, width = queries.shape
    heads = width // HD
    total = sum(piece.shape[0] for piece in pieces)
    joined = len(pieces) > 1
    chunk_rows = total if joined else min(total, KEY_CHUNK)
    kernel = partial(
        attend_kernel, blk=blk, heads=heads, parts=len(pieces), key_blocks=chunk_rows // blk,
        seq_blocks=seq_blocks, reach=WINDOW // blk,
    )
    whole = lambda i, *_: (0, 0)
    if joined:
        kv_specs = [pl.BlockSpec(piece.shape, whole) for piece in pieces]
    else:
        kv_specs = [pl.BlockSpec((chunk_rows, 2 * HD), lambda i, *_: (i, 0))]
    out_shape = [
        jax.ShapeDtypeStruct((rows, width), jnp.float32),
        jax.ShapeDtypeStruct((rows, width), jnp.bfloat16),
        jax.ShapeDtypeStruct((rows, heads * 128), jnp.float32),
    ]
    held = [pltpu.VMEM((total, 2 * HD), jnp.bfloat16)] if joined else []
    return pl.pallas_call(
        kernel,
        out_shape=tuple(out_shape),
        grid_spec=pltpu.PrefetchScalarGridSpec(
            num_scalar_prefetch=2,
            grid=(total // chunk_rows,),
            in_specs=[pl.BlockSpec((rows, width), whole), *kv_specs],
            out_specs=[pl.BlockSpec(shape.shape, whole) for shape in out_shape],
            scratch_shapes=[
                *held,
                pltpu.VMEM((rows, width), jnp.float32),
                pltpu.VMEM((rows, heads * 128), jnp.float32),
                pltpu.SMEM((chunk_rows // blk + 1,), jnp.int32),
            ],
        ),
        compiler_params=pltpu.CompilerParams(vmem_limit_bytes=MOST),
        cost_estimate=pl.CostEstimate(
            flops=4 * rows * width * total, bytes_accessed=8 * rows * width + 8 * total * HD,
            transcendentals=2 * rows * heads * total,
        ),
        name="attend",
    )(block_map, me, queries, *pieces)


def attend_back_kernel(
    map_ref, me_ref, da_ref, out_ref, o_ref, l_ref, q_ref, kv_ref, kt_ref, cos_ref, sin_ref, *refs,
    blk, heads, swapped, key_blocks, seq_blocks, reach
):
    dq_ref, *dkv_refs = refs[: 5 if swapped else 2]
    do_ref, stat_ref, dqt_ref, dk_ref, dv_ref, list_ref = refs[5 if swapped else 2 :]
    chunk = pl.program_id(0)
    q_blocks = q_ref.shape[0] // blk

    @pl.when(chunk == 0)
    def _():
        dqt_ref[...] = jnp.zeros_like(dqt_ref)
        for h in range(heads):
            at = slice(h * HD, (h + 1) * HD)
            out_grad = matmul(da_ref[...], out_ref[:, at]).astype(jnp.bfloat16)
            do_ref[:, at] = out_grad
            delta = jnp.sum(out_grad.astype(jnp.float32) * o_ref[:, at], axis=-1, keepdims=True)
            stat_ref[heads + h : heads + h + 1, :] = jnp.broadcast_to(
                delta, (delta.shape[0], 128)
            ).T[:1, :]
            stat_ref[h : h + 1, :] = jnp.log2(l_ref[:, h * 128 : (h + 1) * 128]).T[:1, :]

    dk_ref[...] = jnp.zeros_like(dk_ref)
    dv_ref[...] = jnp.zeros_like(dv_ref)

    def tile(b, slots, mask):
        rows = [pl.ds(pl.multiple_of(slot * blk, blk), blk) for slot in slots]
        cols = slice(b * blk, (b + 1) * blk)
        keys = jnp.concatenate([kv_ref[row, :HD] for row in rows], axis=0)
        vals = jnp.concatenate([kv_ref[row, HD:] for row in rows], axis=0)
        turned = jnp.concatenate([kt_ref[:, row] for row in rows], axis=1)
        dk_part = dv_part = None
        dq_parts = []
        add = lambda total, term: term if total is None else total + term
        for h in range(heads):
            query = q_ref[cols, h * HD : (h + 1) * HD]
            out_grad = do_ref[cols, h * HD : (h + 1) * HD]
            tangent = jnp.tanh(matmul_nt(keys, query) * (1.0 / soft_cap))
            probs = jnp.exp2(tangent * (soft_cap * LOG2E) - stat_ref[h : h + 1, cols])
            if mask is not None:
                probs = jnp.where(mask, probs, 0.0)
            prob_grad = matmul_nt(vals, out_grad)
            delta = stat_ref[heads + h : heads + h + 1, cols]
            score = (probs * (prob_grad - delta) * (1.0 - tangent * tangent)).astype(jnp.bfloat16)
            dk_part = add(dk_part, matmul(score, query))
            dv_part = add(dv_part, matmul(probs.astype(jnp.bfloat16), out_grad))
            dq_parts.append(matmul(turned, score))
        for h in range(heads):
            dqt_ref[h * HD : (h + 1) * HD, cols] += dq_parts[h]
        for k, row in enumerate(rows):
            dk_ref[row, :] += dk_part[k * blk : (k + 1) * blk]
            dv_ref[row, :] += dv_part[k * blk : (k + 1) * blk]

    visit_blocks(
        map_ref, me_ref[0], chunk, q_blocks, key_blocks, seq_blocks, reach, swapped, list_ref,
        tile, blk, True,
    )

    row = 0
    for dkv_ref in dkv_refs:
        count = dkv_ref.shape[0]
        dkv_ref[:, :HD] = dk_ref[row : row + count, :].astype(jnp.bfloat16)
        dkv_ref[:, HD:] = dv_ref[row : row + count, :].astype(jnp.bfloat16)
        row += count

    @pl.when(chunk == pl.num_programs(0) - 1)
    def _():
        cosine, sine = cos_ref[...], sin_ref[...]
        for h in range(heads):
            low = dqt_ref[h * HD : h * HD + HALF, :].T * HD ** (-0.5)
            high = dqt_ref[h * HD + HALF : (h + 1) * HD, :].T * HD ** (-0.5)
            dq_ref[:, h * HD : h * HD + HALF] = (low * cosine + high * sine).astype(jnp.bfloat16)
            dq_ref[:, h * HD + HALF : (h + 1) * HD] = (high * cosine - low * sine).astype(
                jnp.bfloat16
            )


def attend_back(
    block_map, me, branch_low, full_out_t, attended, totals, queries, kv_all, key_turned, cosine,
    sine, blk, seq_blocks, swapped
):
    rows, width = queries.shape
    heads = width // HD
    depth = branch_low.shape[1]
    total = kv_all.shape[0]
    chunk_rows = total if swapped else min(total, KEY_CHUNK)
    kernel = partial(
        attend_back_kernel, blk=blk, heads=heads, swapped=swapped, key_blocks=chunk_rows // blk,
        seq_blocks=seq_blocks, reach=WINDOW // blk,
    )
    whole = lambda i, *_: (0, 0)
    parts = [3 * rows, rows, 3 * rows, rows] if swapped else [total]
    dkv_shapes = [jax.ShapeDtypeStruct((part, 2 * HD), jnp.bfloat16) for part in parts]
    dkv_specs = [
        pl.BlockSpec((min(part, chunk_rows), 2 * HD), lambda i, *_: (i, 0)) for part in parts
    ]
    return pl.pallas_call(
        kernel,
        out_shape=(jax.ShapeDtypeStruct((rows, width), jnp.bfloat16), *dkv_shapes),
        grid_spec=pltpu.PrefetchScalarGridSpec(
            num_scalar_prefetch=2,
            grid=(total // chunk_rows,),
            in_specs=[
                pl.BlockSpec((rows, depth), whole),
                pl.BlockSpec((depth, width), whole),
                pl.BlockSpec((rows, width), whole),
                pl.BlockSpec((rows, heads * 128), whole),
                pl.BlockSpec((rows, width), whole),
                pl.BlockSpec((chunk_rows, 2 * HD), lambda i, *_: (i, 0)),
                pl.BlockSpec((HD, chunk_rows), lambda i, *_: (0, i)),
                pl.BlockSpec((rows, HALF), whole),
                pl.BlockSpec((rows, HALF), whole),
            ],
            out_specs=[pl.BlockSpec((rows, width), whole), *dkv_specs],
            scratch_shapes=[
                pltpu.VMEM((rows, width), jnp.bfloat16),
                pltpu.VMEM((2 * heads, rows), jnp.float32),
                pltpu.VMEM((width, rows), jnp.float32),
                pltpu.VMEM((chunk_rows, HD), jnp.float32),
                pltpu.VMEM((chunk_rows, HD), jnp.float32),
                pltpu.SMEM((chunk_rows // blk + 1,), jnp.int32),
            ],
        ),
        compiler_params=pltpu.CompilerParams(vmem_limit_bytes=MOST),
        cost_estimate=pl.CostEstimate(
            flops=10 * rows * width * total, bytes_accessed=16 * rows * width + 10 * total * HD,
            transcendentals=2 * rows * heads * total,
        ),
        name="attend_back",
    )(
        block_map, me, branch_low, full_out_t, attended, totals, queries, kv_all, key_turned,
        cosine, sine,
    )


def body(
    tokens, block_map, w_query, w_key, w_value, w_out, w_gate, w_up, w_down, norm_gains, cotangent
):
    ctx_count = lax.axis_size("ctx")
    tok_dev, depth = tokens.shape
    block_rows = tok_dev // 2
    seq_count = max(1, ctx_count // 16)
    seq_len = tok_dev * ctx_count // seq_count
    seq_blocks = seq_len // block_rows
    me = lax.axis_index("ctx")
    me_list = me.reshape(1).astype(jnp.int32)
    heads_dev = w_query.shape[1] // HD
    q_width = heads_dev * HD
    flat_map = block_map.reshape(-1).astype(jnp.int32)
    pairs = paired()

    qkv_shard = pack(w_query, w_key, w_value, norm_gains.T)
    if pairs:
        qkv_pieces = gather_pieces(qkv_shard)
        out_shard = tie(w_out, qkv_pieces[3], qkv_pieces[4]).T
        out_near = nearby(out_shard)
    else:
        qkv_pieces = (lax.all_gather(qkv_shard, "ctx", axis=0, tiled=True),)
        out_pieces = (lax.all_gather(w_out.T, "ctx", axis=0, tiled=True),)
    own_ids = lax.dynamic_index_in_dim(block_map, me, 0, keepdims=False)
    offsets = jnp.arange(block_rows, dtype=jnp.int32)
    own_index = (own_ids[:, None] * block_rows + offsets[None, :]).reshape(-1)
    cosine, sine = angle_tables(own_index % seq_len)
    inputs = tokens.astype(jnp.float32)
    in_scale = rms_scale(inputs)
    unit_in = (inputs * in_scale).astype(jnp.bfloat16)
    queries, *kv_local = project(unit_in, cosine, sine, qkv_pieces, heads_dev)
    if pairs:
        kv_local, out_near = lax.optimization_barrier((kv_local, out_near))
        kv_near = nearby_halves(*kv_local)
        kv_pieces = gather_halves(*kv_local, kv_near)
        half = out_shard.shape[0] // 2
        out_far = (swap(out_near[0][:half], 4), swap(out_near[1][half:], 2))
        out_mine = tie_all((out_shard, *out_near, *out_far), *kv_pieces[6:8])
        out_pieces = out_mine + tuple(swap(part, 1) for part in out_mine)
        late = (*kv_pieces[2:8], *out_far)
    else:
        kv_pieces = (lax.all_gather(jnp.concatenate(kv_local), "ctx", axis=0, tiled=True),)
        late = kv_pieces
    w_gate, w_up, w_down, *_ = lax.optimization_barrier((w_gate, w_up, w_down, *late))
    if pairs:
        gate_near = nearby(w_gate)
    attended, attn_flat, totals = attend(
        flat_map, me_list, queries, kv_pieces, block_rows, seq_blocks
    )
    branch_part = out_project(attn_flat, out_pieces, depth)
    if pairs:
        branch_part, *gate_near = lax.optimization_barrier((branch_part, *gate_near))
        gate_pieces = gather_pieces(w_gate, gate_near)
        qkv_pieces = tie_all(qkv_pieces, branch_part)
    branch = lax.psum(branch_part, "tp")
    full_up = lax.all_gather(w_up, "ctx", axis=0, tiled=True)
    full_qkv = assemble(qkv_pieces)
    gains = full_qkv[:, q_width + 2 * HD : q_width + 2 * HD + 4].T.astype(jnp.float32)
    normed_in = (inputs * in_scale * gains[0]).astype(jnp.bfloat16)
    if pairs:
        down_shard, gains, normed_in, *far = lax.optimization_barrier(
            (w_down.T, gains, normed_in, *gate_pieces[3:5])
        )
        gate_pieces = (*gate_pieces[:3], *far, *gate_pieces[5:])
        down_near = nearby(down_shard)
        full_gate = assemble(gate_pieces, 3)
        full_gate, *down_near = lax.optimization_barrier((full_gate, *down_near))
        down_pieces = gather_pieces(down_shard, down_near)
    else:
        full_gate = lax.all_gather(w_gate, "ctx", axis=0, tiled=True)
        down_pieces = (lax.all_gather(w_down.T, "ctx", axis=0, tiled=True),)
    branch, full_gate, full_up, *near = lax.optimization_barrier(
        (branch, full_gate, full_up, *down_pieces[:3])
    )
    normed_mid = by_rows(mid_kernel, (tokens, branch), gains, (jnp.bfloat16,), 0, "mid_norms")
    if pairs:
        normed_mid, *far = lax.optimization_barrier((normed_mid, *down_pieces[3:5]))
        mine = (*near, *far)
        down_pieces = (*mine, *(swap(part, 1) for part in mine))
    hidden, active, slope = units(normed_mid, full_gate, full_up)
    mlp_part = out_project(hidden, down_pieces, depth, "project_down")
    mlp_part, out_pieces, kv_pieces, down_pieces = lax.optimization_barrier(
        (mlp_part, out_pieces, kv_pieces, down_pieces)
    )
    full_down_t = assemble(down_pieces, 3)
    full_out_t = assemble(out_pieces)
    kv_all, key_turned = turn(kv_pieces)
    mlp_out = lax.psum(mlp_part, "tp")
    mlp_out, full_out_t, kv_all, key_turned, full_down_t = lax.optimization_barrier(
        (mlp_out, full_out_t, kv_all, key_turned, full_down_t)
    )
    result, mlp_low, gain_four = by_rows(
        top_kernel, (tokens, branch, mlp_out, cotangent), gains, (jnp.bfloat16, jnp.bfloat16), 1,
        "top_norms",
    )
    gate_low, up_low = units_back(mlp_low, full_down_t, active, slope)
    mid_part = features_back(gate_low, up_low, full_gate, full_up)
    mid_part, hidden_t, mlp_t, gate_t, up_t = lax.optimization_barrier(
        (mid_part, hidden, mlp_low, gate_low, up_low)
    )
    mid_sum = lax.psum(mid_part, "tp")
    down_grad = matmul(hidden_t.T, mlp_t).astype(jnp.bfloat16)
    down_shard = lax.psum_scatter(down_grad, "ctx", scatter_dimension=1, tiled=True)
    gate_grad = matmul(normed_mid.T, gate_t).astype(jnp.bfloat16)
    gate_blocks = scatter_start(gate_grad)
    up_grad = matmul(normed_mid.T, up_t).astype(jnp.bfloat16)
    up_grad, gate_blocks = lax.optimization_barrier((up_grad, gate_blocks))
    gate_terms = scatter_finish(gate_blocks)
    up_chips = scatter_chips(up_grad)
    mid_sum, up_chips = lax.optimization_barrier((mid_sum, up_chips))
    resid_grad, branch_low, gain_mid = by_rows(
        low_kernel, (tokens, branch, mid_sum, cotangent), gains, (jnp.float32, jnp.bfloat16), 2,
        "low_norms",
    )
    query_low, *kv_terms = attend_back(
        flat_map, me_list, branch_low, full_out_t, attended, totals, queries, kv_all, key_turned,
        cosine, sine, block_rows, seq_blocks, pairs,
    )
    *kv_terms, down_shard, gate_terms = lax.optimization_barrier((*kv_terms, down_shard, gate_terms))
    gate_shard = add_terms(gate_terms)
    if pairs:
        far = kv_terms[1] + swap(kv_terms[3], 1)
        near = kv_terms[0] + swap(kv_terms[2], 1)
        blocks = (near[k * tok_dev : (k + 1) * tok_dev] for k in range(3))
        kv_sums = scatter_finish(scatter_corner(*blocks, far))
    else:
        kv_sums = (lax.psum_scatter(kv_terms[0], "ctx", scatter_dimension=0, tiled=True),)
    qkv_low, in_part = join(cosine, sine, query_low, full_qkv, kv_sums)
    in_part, qkv_low, branch_t, up_chips = lax.optimization_barrier(
        (in_part, qkv_low, branch_low, up_chips)
    )
    in_sum = lax.psum(in_part, "tp")
    up_shard = add_terms(scatter_finish(scatter_blocks(up_chips)))
    gain_one = jnp.sum(in_part.astype(jnp.float32) * (inputs * in_scale), axis=0)
    gain_one = sum_small_tp(gain_one)
    gains_shard = scatter_gains(jnp.concatenate([gain_one[None], gain_mid[1:], gain_mid[:1], gain_four]))
    qkv_grad = matmul(normed_in.T, qkv_low).astype(jnp.bfloat16)
    qkv_shard = add_terms(scatter_finish(scatter_start(qkv_grad)))
    out_weight_grad = matmul(branch_t.T, attn_flat).astype(jnp.bfloat16)
    out_grad_t = add_terms(scatter_finish(scatter_start(out_weight_grad)))
    shards = (
        qkv_shard[:, :q_width],
        qkv_shard[:, q_width : q_width + HD],
        qkv_shard[:, q_width + HD :],
        out_grad_t.T,
        gate_shard,
        up_shard,
        down_shard.astype(jnp.float32),
        gains_shard,
    )
    input_grad = by_rows(
        end_kernel, (tokens, in_sum, resid_grad), gains, (jnp.float32,), 0, "end_norms"
    )
    return (result, input_grad, *shards)


def solution(mesh):
    in_specs = (
        P("ctx", None),
        P(),
        P("ctx", "tp"),
        P("ctx", "tp"),
        P("ctx", "tp"),
        P("tp", "ctx"),
        P("ctx", "tp"),
        P("ctx", "tp"),
        P("tp", "ctx"),
        P(None, "ctx"),
        P("ctx", None),
    )
    out_specs = (
        P("ctx", None),
        P("ctx", None),
        P("ctx", "tp"),
        P("ctx", "tp"),
        P("ctx", "tp"),
        P("tp", "ctx"),
        P("ctx", "tp"),
        P("ctx", "tp"),
        P("tp", "ctx"),
        P(None, "ctx"),
    )
    return jax.shard_map(body, mesh=mesh, in_specs=in_specs, out_specs=out_specs, check_vma=False)
```

```python
from functools import partial

import jax
import jax.numpy as jnp
from jax import lax
from jax.experimental import pallas as pl
from jax.experimental.pallas import tpu as pltpu
from jax.sharding import PartitionSpec as P

HD = 256
HALF = 128
WINDOW = 4096
KEY_CHUNK = 4096
MOST = 60 * 2**20


epsilon = 1e-06
soft_cap = 50.0
LOG2E = 1.4426950408889634


def rms_scale(values):
    return lax.rsqrt(jnp.mean(values * values, axis=-1, keepdims=True) + epsilon)


def angle_tables(positions):
    frequency = jnp.power(10000.0, -2.0 * jnp.arange(HALF, dtype=jnp.float32) / HD)
    phases = positions.astype(jnp.float32)[:, None] * frequency[None, :]
    return (jnp.cos(phases), jnp.sin(phases))


def matmul(left, right):
    return jnp.dot(left, right, preferred_element_type=jnp.float32)


def matmul_nt(left, right):
    return lax.dot_general(left, right, (((1,), (1,)), ((), ())), preferred_element_type=jnp.float32)


def tie(value, *others):
    return lax.optimization_barrier((value,) + others)[0]


def tie_all(values, *others):
    return lax.optimization_barrier((*values, *others))[: len(values)]


def call(kernel, out_shape, args, name, scalars=0, scratch=(), flops=0, mem=32, space=None):
    spec = pl.BlockSpec(memory_space=pltpu.VMEM if space is None else space)
    outs = jax.tree.map(lambda _: spec, out_shape)
    size = sum(a.size * a.dtype.itemsize for a in args)
    size += sum(a.size * a.dtype.itemsize for a in jax.tree.leaves(out_shape))
    return pl.pallas_call(
        kernel,
        out_shape=out_shape,
        in_specs=[pl.BlockSpec(memory_space=pltpu.SMEM)] * scalars + [spec] * (len(args) - scalars),
        out_specs=outs,
        scratch_shapes=list(scratch),
        compiler_params=pltpu.CompilerParams(vmem_limit_bytes=mem * 2**20),
        cost_estimate=pl.CostEstimate(flops=flops, bytes_accessed=size, transcendentals=0),
        name=name,
    )(*args)


def swap(value, bit):
    pairs = [(i, i ^ bit) for i in range(lax.axis_size("ctx"))]
    return lax.ppermute(value, "ctx", pairs)


def paired():
    return lax.axis_size("ctx") == 8


def nearby(piece):
    return swap(piece, 2), swap(piece, 4)


def gather_pieces(piece, near=None):
    half = piece.shape[0] // 2
    by_x, by_y = nearby(piece) if near is None else near
    mine = (piece, by_x, by_y, swap(by_x[:half], 4), swap(by_y[half:], 2))
    return mine + tuple(swap(part, 1) for part in mine)


def nearby_halves(low, high):
    first = (swap(low, 2), swap(high, 4))
    return first[0], swap(high, 2), swap(low, 4), first[1]


def gather_halves(low, high, near=None):
    near = nearby_halves(low, high) if near is None else near
    mine = (low, high, *near, swap(near[0], 4), swap(near[3], 2))
    return mine + tuple(swap(part, 1) for part in mine)


def piece_rows(rows, halves):
    me = lax.axis_index("ctx")
    if halves:
        bits = [bit for core in (0, 1) for bit in (0, 2, 4, 6) for _ in range(2)]
        shift = [0, rows // 2] * 8
        places = [(me ^ (bit + k // 8)) * rows for k, bit in enumerate(bits)]
    else:
        places = [(me ^ bit) * rows for bit in (0, 2, 4, 6, 6, 1, 3, 5, 7, 7)]
        shift = [0, 0, 0, 0, rows // 2] * 2
    return jnp.stack(places).astype(jnp.int32) + jnp.array(shift, jnp.int32)


def places_of(pieces):
    if len(pieces) == 1:
        return jnp.zeros((1,), jnp.int32)
    rows = sum(piece.shape[0] for piece in pieces) // 8
    return piece_rows(rows, len(pieces) == 16)


def place(rows_ref, pieces, whole_ref):
    for k, piece in enumerate(pieces):
        whole_ref[pl.ds(pl.multiple_of(rows_ref[k], 16), piece.shape[0]), :] = piece[...]


def assemble_kernel(rows_ref, *refs):
    place(rows_ref, refs[:-1], refs[-1])


def assemble(pieces, grid=1):
    if len(pieces) == 1:
        return pieces[0]
    rows, width = sum(piece.shape[0] for piece in pieces) // 8, pieces[0].shape[1]
    column = lambda n: pl.BlockSpec((n, width // grid), lambda i: (0, i))
    return pl.pallas_call(
        assemble_kernel,
        out_shape=jax.ShapeDtypeStruct((8 * rows, width), pieces[0].dtype),
        grid=(grid,),
        in_specs=[pl.BlockSpec(memory_space=pltpu.SMEM)] + [column(p.shape[0]) for p in pieces],
        out_specs=column(8 * rows),
        compiler_params=pltpu.CompilerParams(vmem_limit_bytes=MOST),
        cost_estimate=pl.CostEstimate(flops=0, bytes_accessed=32 * rows * width, transcendentals=0),
        name="assemble",
    )(places_of(pieces), *pieces)


def scatter_corner(own, by_x, by_y, corner):
    half = own.shape[0] // 2
    from_x = swap(corner[:half], 2)
    from_y = swap(corner[half:], 4)
    by_y = jnp.concatenate([by_y[:half] + from_x, by_y[half:]], axis=0)
    by_x = jnp.concatenate([by_x[:half], by_x[half:] + from_y], axis=0)
    return own, by_x, by_y


def scatter_chips(whole):
    if not paired():
        return lax.psum_scatter(whole, "ctx", scatter_dimension=0, tiled=True)
    core = lax.axis_index("ctx") % 2
    blocks = whole.reshape(4, 2, whole.shape[0] // 8, whole.shape[1])
    theirs = lax.dynamic_index_in_dim(blocks, 1 - core, 1, keepdims=False)
    mine = lax.dynamic_index_in_dim(blocks, core, 1, keepdims=False)
    return mine + swap(theirs, 1)


def scatter_blocks(chips):
    if not paired():
        return (chips,)
    chip = lax.axis_index("ctx") // 2
    pick = lambda bits: lax.dynamic_index_in_dim(chips, chip ^ bits, 0, keepdims=False)
    return scatter_corner(pick(0), pick(1), pick(2), pick(3))


def scatter_start(whole):
    return scatter_blocks(scatter_chips(whole))


def scatter_finish(blocks):
    if len(blocks) == 1:
        return blocks
    own, by_x, by_y = blocks
    return own, swap(by_x, 2), swap(by_y, 4)


def add_terms(terms):
    total = terms[0].astype(jnp.float32)
    for term in terms[1:]:
        total = total + term.astype(jnp.float32)
    return total


def scatter_gains(whole):
    if not paired():
        return lax.psum_scatter(whole, "ctx", scatter_dimension=1, tiled=True)
    me = lax.axis_index("ctx")
    columns = whole.shape[1] // 8
    stack = whole.reshape(whole.shape[0], 8, columns).transpose(1, 0, 2)
    for bit in (4, 2, 1):
        half = stack.shape[0] // 2
        low = (me & bit) == 0
        theirs = jnp.where(low, stack[half:], stack[:half])
        mine = jnp.where(low, stack[:half], stack[half:])
        stack = mine + swap(theirs, bit)
    return stack[0]


def sum_small_tp(value):
    count = lax.axis_size("tp")
    bit = 1
    while bit < count:
        value = value + lax.ppermute(value, "tp", [(i, i ^ bit) for i in range(count)])
        bit *= 2
    return value


def pack_kernel(a_ref, b_ref, c_ref, gains_ref, out_ref):
    one, two = a_ref.shape[1], a_ref.shape[1] + b_ref.shape[1]
    three = two + c_ref.shape[1]
    out_ref[:, :one] = a_ref[...]
    out_ref[:, one:two] = b_ref[...]
    out_ref[:, two:three] = c_ref[...]
    lane = lax.broadcasted_iota(jnp.int32, (gains_ref.shape[0], HALF), 1)
    columns = jnp.broadcast_to(gains_ref[:, :1], lane.shape)
    for k in range(1, gains_ref.shape[1]):
        columns = jnp.where(lane == k, jnp.broadcast_to(gains_ref[:, k : k + 1], lane.shape), columns)
    out_ref[:, three:] = columns


def pack(first, second, third, gains):
    width = first.shape[1] + second.shape[1] + third.shape[1] + HALF
    shape = jax.ShapeDtypeStruct((first.shape[0], width), first.dtype)
    return call(pack_kernel, shape, (first, second, third, gains), "pack")


def project_kernel(rows_ref, in_ref, cos_ref, sin_ref, *refs, heads, parts):
    pieces, q_ref, kv_refs = refs[:parts], refs[parts], refs[parts + 1 : parts + 3]
    block = kv_refs[0].shape[0]
    if parts > 1:
        full_ref = refs[parts + 3]
        place(rows_ref, pieces, full_ref)
    else:
        full_ref = pieces[0]
    gain = full_ref[:, (heads + 2) * HD : (heads + 2) * HD + 1].astype(jnp.float32)
    for n in range(heads + 2):
        weight = (full_ref[:, n * HD : (n + 1) * HD].astype(jnp.float32) * gain).astype(jnp.bfloat16)
        raw = matmul(in_ref[...], weight)
        if n <= heads:
            low, high = raw[:, :HALF], raw[:, HALF:]
            cosine, sine = cos_ref[...], sin_ref[...]
            low, high = low * cosine - high * sine, high * cosine + low * sine
            if n < heads:
                q_ref[:, n * HD : n * HD + HALF] = (low * HD ** (-0.5)).astype(jnp.bfloat16)
                q_ref[:, n * HD + HALF : (n + 1) * HD] = (high * HD ** (-0.5)).astype(jnp.bfloat16)
            else:
                for k, kv_ref in enumerate(kv_refs):
                    rows = slice(k * block, (k + 1) * block)
                    kv_ref[:, :HALF] = low[rows].astype(jnp.bfloat16)
                    kv_ref[:, HALF:HD] = high[rows].astype(jnp.bfloat16)
        else:
            for k, kv_ref in enumerate(kv_refs):
                kv_ref[:, HD:] = raw[k * block : (k + 1) * block].astype(jnp.bfloat16)


def project(normed, cosine, sine, pieces, heads):
    rows, depth = normed.shape
    width = pieces[0].shape[1]
    low = lambda m, n: jax.ShapeDtypeStruct((m, n), jnp.bfloat16)
    scratch = [pltpu.VMEM((depth, width), jnp.bfloat16)] if len(pieces) > 1 else []
    return call(
        partial(project_kernel, heads=heads, parts=len(pieces)),
        (low(rows, heads * HD), low(rows // 2, 2 * HD), low(rows // 2, 2 * HD)),
        (places_of(pieces), normed, cosine, sine, *pieces), "project", scalars=1, scratch=scratch,
        flops=2 * rows * depth * width,
    )


def out_project_kernel(rows_ref, attn_ref, *refs, parts):
    pieces, branch_ref = refs[:parts], refs[parts]
    if parts > 1:
        full_ref = refs[parts + 1]
        place(rows_ref, pieces, full_ref)
    else:
        full_ref = pieces[0]
    for n in range(0, branch_ref.shape[1], 256):
        part = matmul_nt(attn_ref[...], full_ref[n : n + 256, :])
        branch_ref[:, n : n + 256] = part.astype(jnp.bfloat16)


def out_project(attn, pieces, depth, name="out_project"):
    rows, width = attn.shape
    scratch = [pltpu.VMEM((depth, width), jnp.bfloat16)] if len(pieces) > 1 else []
    return call(
        partial(out_project_kernel, parts=len(pieces)),
        jax.ShapeDtypeStruct((rows, depth), jnp.bfloat16), (places_of(pieces), attn, *pieces),
        name, scalars=1, scratch=scratch, flops=2 * rows * depth * width,
    )


def join_kernel(cos_ref, sin_ref, query_ref, full_ref, unit_ref, *refs):
    *terms, low_ref, part_ref, gain_ref = refs
    total = terms[0][...].astype(jnp.float32)
    for term in terms[1:]:
        total = total + term[...].astype(jnp.float32)
    width = query_ref.shape[1]
    cosine, sine = cos_ref[...], sin_ref[...]
    low, high = total[:, :HALF], total[:, HALF:HD]
    low_ref[:, :width] = query_ref[...]
    low_ref[:, width : width + HALF] = (low * cosine + high * sine).astype(jnp.bfloat16)
    low_ref[:, width + HALF : width + HD] = (high * cosine - low * sine).astype(jnp.bfloat16)
    low_ref[:, width + HD :] = total[:, HD:].astype(jnp.bfloat16)
    for n in range(0, part_ref.shape[1], 256):
        part = matmul_nt(low_ref[...], full_ref[n : n + 256, : low_ref.shape[1]])
        part_ref[:, n : n + 256] = part.astype(jnp.bfloat16)
        unit = unit_ref[:, n : n + 256].astype(jnp.float32)
        gain_ref[:, n : n + 256] = jnp.sum(part * unit, axis=0, keepdims=True)


def join(cosine, sine, query_low, full_qkv, unit_in, terms):
    rows = query_low.shape[0]
    depth, width = full_qkv.shape[0], query_low.shape[1] + 2 * HD
    low = lambda n: jax.ShapeDtypeStruct((rows, n), jnp.bfloat16)
    return call(
        join_kernel, (low(width), low(depth), jax.ShapeDtypeStruct((1, depth), jnp.float32)),
        (cosine, sine, query_low, full_qkv, unit_in, *terms), "join",
        flops=2 * rows * depth * width,
    )


GROUP = 16


def rms_of(values):
    return lax.rsqrt(jnp.mean(values * values, axis=-1, keepdims=True) + epsilon)


def norm_back(normed, scale, weighted):
    return scale * (weighted - normed * jnp.mean(weighted * normed, axis=-1, keepdims=True))


def fold(values):
    total = values[:8]
    for row in range(8, values.shape[0], 8):
        total = total + values[row : row + 8]
    return total


def wide(ref, rows):
    return ref[rows, :].astype(jnp.float32)


def walk(count, step):
    def run(index, carry):
        step(pl.ds(pl.multiple_of(index * GROUP, GROUP), GROUP))
        return carry

    lax.fori_loop(0, count // GROUP, run, 0, unroll=8)


def mid_kernel(tok_ref, branch_ref, gains_ref, out_ref):
    def step(rows):
        branch = wide(branch_ref, rows)
        residual = wide(tok_ref, rows) + branch * rms_of(branch) * gains_ref[1:2, :]
        out_ref[rows, :] = (residual * rms_of(residual) * gains_ref[2:3, :]).astype(jnp.bfloat16)

    walk(tok_ref.shape[0], step)


def top_kernel(tok_ref, branch_ref, mlp_ref, cot_ref, gains_ref, out_ref, grad_ref, sum_ref, acc_ref):
    @pl.when(pl.program_id(0) == 0)
    def _():
        acc_ref[...] = jnp.zeros_like(acc_ref)

    def step(rows):
        branch = wide(branch_ref, rows)
        residual = wide(tok_ref, rows) + branch * rms_of(branch) * gains_ref[1:2, :]
        mlp = wide(mlp_ref, rows)
        scale = rms_of(mlp)
        normed = mlp * scale
        out_ref[rows, :] = (residual + normed * gains_ref[3:4, :]).astype(jnp.bfloat16)
        out_grad = wide(cot_ref, rows)
        acc_ref[...] += fold(out_grad * normed)
        grad_ref[rows, :] = norm_back(normed, scale, out_grad * gains_ref[3:4, :]).astype(jnp.bfloat16)

    walk(tok_ref.shape[0], step)

    @pl.when(pl.program_id(0) == pl.num_programs(0) - 1)
    def _():
        sum_ref[...] = jnp.sum(acc_ref[...], axis=0, keepdims=True)


def low_kernel(
    tok_ref, branch_ref, mid_ref, cot_ref, gains_ref, resid_ref, grad_ref, sum_ref, acc_ref
):
    @pl.when(pl.program_id(0) == 0)
    def _():
        acc_ref[...] = jnp.zeros_like(acc_ref)

    def step(rows):
        branch = wide(branch_ref, rows)
        branch_scale = rms_of(branch)
        branch_normed = branch * branch_scale
        residual = wide(tok_ref, rows) + branch_normed * gains_ref[1:2, :]
        scale = rms_of(residual)
        normed = residual * scale
        mid_grad = wide(mid_ref, rows)
        acc_ref[:8, :] += fold(mid_grad * normed)
        grad = wide(cot_ref, rows) + norm_back(normed, scale, mid_grad * gains_ref[2:3, :])
        resid_ref[rows, :] = grad
        acc_ref[8:, :] += fold(grad * branch_normed)
        grad_ref[rows, :] = norm_back(
            branch_normed, branch_scale, grad * gains_ref[1:2, :]
        ).astype(jnp.bfloat16)

    walk(tok_ref.shape[0], step)

    @pl.when(pl.program_id(0) == pl.num_programs(0) - 1)
    def _():
        sum_ref[0:1, :] = jnp.sum(acc_ref[:8, :], axis=0, keepdims=True)
        sum_ref[1:2, :] = jnp.sum(acc_ref[8:, :], axis=0, keepdims=True)


def end_kernel(tok_ref, sum_ref, resid_ref, gains_ref, out_ref):
    def step(rows):
        values = wide(tok_ref, rows)
        scale = rms_of(values)
        weighted = wide(sum_ref, rows) * gains_ref[0:1, :]
        out_ref[rows, :] = resid_ref[rows, :] + norm_back(values * scale, scale, weighted)

    walk(tok_ref.shape[0], step)


def by_rows(kernel, args, gains, kinds, sums, name, block=128):
    rows, depth = args[0].shape
    tile = pl.BlockSpec((block, depth), lambda i: (i, 0))
    ahead = pl.BlockSpec((block, depth), lambda i: (i, 0))
    whole = lambda n: pl.BlockSpec((n, depth), lambda i: (0, 0))
    shapes = [jax.ShapeDtypeStruct((rows, depth), kind) for kind in kinds]
    out_specs = [tile] * len(kinds)
    scratch = []
    if sums:
        shapes.append(jax.ShapeDtypeStruct((sums, depth), jnp.float32))
        out_specs.append(whole(sums))
        scratch.append(pltpu.VMEM((8 * sums, depth), jnp.float32))
    size = sum(a.size * a.dtype.itemsize for a in (*args, *shapes))
    found = pl.pallas_call(
        kernel,
        out_shape=tuple(shapes),
        grid=(rows // block,),
        in_specs=[ahead] * len(args) + [whole(gains.shape[0])],
        out_specs=out_specs,
        scratch_shapes=scratch,
        compiler_params=pltpu.CompilerParams(vmem_limit_bytes=MOST),
        cost_estimate=pl.CostEstimate(flops=0, bytes_accessed=size, transcendentals=0),
        name=name,
    )(*args, gains)
    return found if len(found) > 1 else found[0]


UNITS = 768
STEP = 256


def units_kernel(in_ref, gate_ref, up_ref, hidden_ref, active_ref, slope_ref):
    for n in range(0, UNITS, UNITS):
        at = slice(n, n + UNITS)
        gate = matmul(in_ref[...], gate_ref[:, at])
        up = matmul(in_ref[...], up_ref[:, at])
        root = (2.0 / jnp.pi) ** 0.5
        square = gate * gate
        bend = jnp.tanh(root * gate * (1.0 + 0.044715 * square))
        half = 0.5 * (1.0 + bend)
        active = gate * half
        slope = half + 0.5 * gate * (1.0 - bend * bend) * (root * (1.0 + 3 * 0.044715 * square))
        hidden_ref[:, at] = (active * up).astype(jnp.bfloat16)
        active_ref[:, at] = active.astype(jnp.bfloat16)
        slope_ref[:, at] = (slope * up).astype(jnp.bfloat16)


def units(normed, full_gate, full_up):
    rows, depth = normed.shape
    count = full_gate.shape[1]
    column = lambda n: pl.BlockSpec((n, UNITS), lambda i: (0, i))
    ahead = pl.BlockSpec((depth, UNITS), lambda i: (0, i))
    return pl.pallas_call(
        units_kernel,
        out_shape=tuple(jax.ShapeDtypeStruct((rows, count), jnp.bfloat16) for _ in range(3)),
        grid=(count // UNITS,),
        in_specs=[pl.BlockSpec((rows, depth), lambda i: (0, 0)), ahead, ahead],
        out_specs=[column(rows)] * 3,
        compiler_params=pltpu.CompilerParams(vmem_limit_bytes=MOST),
        cost_estimate=pl.CostEstimate(
            flops=4 * rows * depth * count, bytes_accessed=4 * depth * count,
            transcendentals=rows * count,
        ),
        name="units",
    )(normed, full_gate, full_up)


def units_back_kernel(grad_ref, down_ref, active_ref, slope_ref, dg_ref, du_ref):
    for n in range(0, UNITS, STEP):
        at = slice(n, n + STEP)
        hidden_grad = matmul(grad_ref[...], down_ref[:, at])
        dg_ref[:, at] = (hidden_grad * slope_ref[:, at].astype(jnp.float32)).astype(jnp.bfloat16)
        du_ref[:, at] = (hidden_grad * active_ref[:, at].astype(jnp.float32)).astype(jnp.bfloat16)


def units_back(mlp_low, full_down_t, active, slope):
    rows, depth = mlp_low.shape
    count = active.shape[1]
    column = lambda n: pl.BlockSpec((n, UNITS), lambda i: (0, i))
    ahead = pl.BlockSpec((depth, UNITS), lambda i: (0, i))
    return pl.pallas_call(
        units_back_kernel,
        out_shape=tuple(jax.ShapeDtypeStruct((rows, count), jnp.bfloat16) for _ in range(2)),
        grid=(count // UNITS,),
        in_specs=[pl.BlockSpec((rows, depth), lambda i: (0, 0)), ahead, column(rows), column(rows)],
        out_specs=[column(rows)] * 2,
        compiler_params=pltpu.CompilerParams(vmem_limit_bytes=MOST),
        cost_estimate=pl.CostEstimate(
            flops=2 * rows * depth * count, bytes_accessed=2 * depth * count, transcendentals=0
        ),
        name="units_back",
    )(mlp_low, full_down_t, active, slope)


def features_back_kernel(dg_ref, du_ref, gate_ref, up_ref, out_ref):
    for n in range(0, UNITS, STEP):
        at = slice(n, n + STEP)
        part = matmul_nt(dg_ref[...], gate_ref[at, :]) + matmul_nt(du_ref[...], up_ref[at, :])
        out_ref[:, at] = part.astype(jnp.bfloat16)


def features_back(gate_low, up_low, full_gate, full_up):
    rows, count = gate_low.shape
    depth = full_gate.shape[0]
    whole = pl.BlockSpec((rows, count), lambda i: (0, 0))
    tile = pl.BlockSpec((UNITS, count), lambda i: (i, 0))
    return pl.pallas_call(
        features_back_kernel,
        out_shape=jax.ShapeDtypeStruct((rows, depth), jnp.bfloat16),
        grid=(depth // UNITS,),
        in_specs=[whole, whole, tile, tile],
        out_specs=pl.BlockSpec((rows, UNITS), lambda i: (0, i)),
        compiler_params=pltpu.CompilerParams(vmem_limit_bytes=MOST),
        cost_estimate=pl.CostEstimate(
            flops=4 * rows * depth * count, bytes_accessed=4 * depth * count, transcendentals=0
        ),
        name="features_back",
    )(gate_low, up_low, full_gate, full_up)


def slot_block(map_ref, me, slot, swapped):
    device = slot >> 1
    if swapped:
        device = me ^ (((device & 3) << 1) | (device >> 2))
    return map_ref[device * 2 + (slot & 1)]


def block_list(lookup, key_blocks, own, seq_blocks, reach, list_ref):
    def look(slot, count):
        other = lookup(slot)
        gap = own - other
        whole = (gap > 0) & (gap < reach) & (own // seq_blocks == other // seq_blocks)
        list_ref[count] = slot
        return count + whole.astype(jnp.int32)

    return lax.fori_loop(0, key_blocks, look, jnp.int32(0))


def find_block(lookup, key_blocks, wanted):
    def look(slot, found):
        return jnp.where(lookup(slot) == wanted, slot, found)

    return lax.fori_loop(0, key_blocks, look, jnp.int32(-1))


def visit_blocks(map_ref, me, chunk, q_blocks, key_blocks, seq_blocks, reach, swapped, list_ref, tile, blk, keys_first):
    first = chunk * key_blocks
    lookup = lambda slot: slot_block(map_ref, me, first + slot, swapped)
    row_no = lax.broadcasted_iota(jnp.int32, (blk, blk), 0)
    col_no = lax.broadcasted_iota(jnp.int32, (blk, blk), 1)
    query_no, key_no = (col_no, row_no) if keys_first else (row_no, col_no)
    for b in range(q_blocks):
        own = map_ref[me * q_blocks + b]
        count = block_list(lookup, key_blocks, own, seq_blocks, reach, list_ref)

        def four(step, carry):
            tile(b, tuple(list_ref[4 * step + k] for k in range(4)), None)
            return carry

        lax.fori_loop(0, count // 4, four, 0)

        @pl.when(count % 4 >= 2)
        def _():
            first = (count // 4) * 4
            tile(b, (list_ref[first], list_ref[first + 1]), None)

        @pl.when(count % 2 == 1)
        def _():
            tile(b, (list_ref[count - 1],), None)

        diagonal = find_block(lookup, key_blocks, own)

        @pl.when(diagonal >= 0)
        def _():
            tile(b, (diagonal,), query_no >= key_no)

        if reach < seq_blocks:
            edge = find_block(lookup, key_blocks, own - reach)

            @pl.when((edge >= 0) & (own % seq_blocks >= reach))
            def _():
                tile(b, (edge,), query_no < key_no)


def turn_kernel(*refs):
    *pieces, whole_ref, turned_ref = refs
    row = 0
    for piece in pieces:
        count = piece.shape[0]
        whole_ref[row : row + count, :] = piece[...]
        turned_ref[:, row : row + count] = piece[:, :HD].T
        row += count


def turn(pieces):
    if len(pieces) == 1:
        return pieces[0], pieces[0][:, :HD].T
    total = sum(piece.shape[0] for piece in pieces)
    low = lambda a, b: jax.ShapeDtypeStruct((a, b), jnp.bfloat16)
    return call(turn_kernel, (low(total, 2 * HD), low(HD, total)), pieces, "turn")


def attend_kernel(
    map_ref, me_ref, q_ref, *refs, blk, heads, parts, key_blocks, seq_blocks, reach
):
    pieces = refs[:parts]
    o_ref, low_ref, l_ref = refs[parts : parts + 3]
    chunk = pl.program_id(0)
    if parts > 1:
        kv_ref = refs[parts + 3]
        row = 0
        for piece in pieces:
            kv_ref[row : row + piece.shape[0], :] = piece[...]
            row += piece.shape[0]
    else:
        kv_ref = pieces[0]
    acc_ref, sum_ref, list_ref = refs[-3:]
    q_blocks = q_ref.shape[0] // blk

    @pl.when(chunk == 0)
    def _():
        acc_ref[...] = jnp.zeros_like(acc_ref)
        sum_ref[...] = jnp.zeros_like(sum_ref)

    def tile(b, slots, mask):
        rows = [pl.ds(pl.multiple_of(slot * blk, blk), blk) for slot in slots]
        cols = slice(b * blk, (b + 1) * blk)
        if mask is None:
            query = jnp.concatenate([q_ref[cols, h * HD : (h + 1) * HD] for h in range(heads)], axis=0)
            part, held = None, []
            for row in rows:
                capped = jnp.tanh(matmul_nt(query, kv_ref[row, :HD]) * (1.0 / soft_cap))
                weights = jnp.exp2(capped * (soft_cap * LOG2E))
                for piece in range(0, blk, 128):
                    term = weights[:, piece : piece + 128]
                    part = term if part is None else part + term
                held.append(weights.astype(jnp.bfloat16))
            values = jnp.concatenate([kv_ref[row, HD:] for row in rows], axis=0)
            result = matmul(jnp.concatenate(held, axis=1), values)
            for h in range(heads):
                sum_ref[cols, h * 128 : (h + 1) * 128] += part[h * blk : (h + 1) * blk]
                acc_ref[cols, h * HD : (h + 1) * HD] += result[h * blk : (h + 1) * blk]
            return
        for h in range(heads):
            query = q_ref[cols, h * HD : (h + 1) * HD]
            part = result = None
            for row in rows:
                capped = jnp.tanh(matmul_nt(query, kv_ref[row, :HD]) * (1.0 / soft_cap))
                weights = jnp.exp2(capped * (soft_cap * LOG2E))
                if mask is not None:
                    weights = jnp.where(mask, weights, 0.0)
                for piece in range(0, blk, 128):
                    term = weights[:, piece : piece + 128]
                    part = term if part is None else part + term
                term = matmul(weights.astype(jnp.bfloat16), kv_ref[row, HD:])
                result = term if result is None else result + term
            sum_ref[cols, h * 128 : (h + 1) * 128] += part
            acc_ref[cols, h * HD : (h + 1) * HD] += result

    visit_blocks(
        map_ref, me_ref[0], chunk, q_blocks, key_blocks, seq_blocks, reach, parts > 1, list_ref,
        tile, blk, False,
    )

    @pl.when(chunk == pl.num_programs(0) - 1)
    def _():
        for b in range(q_blocks):
            for h in range(heads):
                at = (slice(b * blk, (b + 1) * blk), slice(h * HD, (h + 1) * HD))
                lanes = (slice(b * blk, (b + 1) * blk), slice(h * 128, (h + 1) * 128))
                total = jnp.sum(sum_ref[lanes], axis=-1, keepdims=True)
                result = acc_ref[at] / total
                o_ref[at] = result
                low_ref[at] = result.astype(jnp.bfloat16)
                l_ref[lanes] = jnp.broadcast_to(total, (blk, 128))


def attend(block_map, me, queries, pieces, blk, seq_blocks):
    rows, width = queries.shape
    heads = width // HD
    total = sum(piece.shape[0] for piece in pieces)
    joined = len(pieces) > 1
    chunk_rows = total if joined else min(total, KEY_CHUNK)
    kernel = partial(
        attend_kernel, blk=blk, heads=heads, parts=len(pieces), key_blocks=chunk_rows // blk,
        seq_blocks=seq_blocks, reach=WINDOW // blk,
    )
    whole = lambda i, *_: (0, 0)
    if joined:
        kv_specs = [pl.BlockSpec(piece.shape, whole) for piece in pieces]
    else:
        kv_specs = [pl.BlockSpec((chunk_rows, 2 * HD), lambda i, *_: (i, 0))]
    out_shape = [
        jax.ShapeDtypeStruct((rows, width), jnp.float32),
        jax.ShapeDtypeStruct((rows, width), jnp.bfloat16),
        jax.ShapeDtypeStruct((rows, heads * 128), jnp.float32),
    ]
    held = [pltpu.VMEM((total, 2 * HD), jnp.bfloat16)] if joined else []
    return pl.pallas_call(
        kernel,
        out_shape=tuple(out_shape),
        grid_spec=pltpu.PrefetchScalarGridSpec(
            num_scalar_prefetch=2,
            grid=(total // chunk_rows,),
            in_specs=[pl.BlockSpec((rows, width), whole), *kv_specs],
            out_specs=[pl.BlockSpec(shape.shape, whole) for shape in out_shape],
            scratch_shapes=[
                *held,
                pltpu.VMEM((rows, width), jnp.float32),
                pltpu.VMEM((rows, heads * 128), jnp.float32),
                pltpu.SMEM((chunk_rows // blk + 1,), jnp.int32),
            ],
        ),
        compiler_params=pltpu.CompilerParams(vmem_limit_bytes=MOST),
        cost_estimate=pl.CostEstimate(
            flops=4 * rows * width * total, bytes_accessed=8 * rows * width + 8 * total * HD,
            transcendentals=2 * rows * heads * total,
        ),
        name="attend",
    )(block_map, me, queries, *pieces)


def attend_back_kernel(
    map_ref, me_ref, da_ref, out_ref, o_ref, l_ref, q_ref, kv_ref, kt_ref, cos_ref, sin_ref, *refs,
    blk, heads, swapped, key_blocks, seq_blocks, reach
):
    dq_ref, *dkv_refs = refs[: 5 if swapped else 2]
    do_ref, stat_ref, dqt_ref, dk_ref, dv_ref, list_ref = refs[5 if swapped else 2 :]
    chunk = pl.program_id(0)
    q_blocks = q_ref.shape[0] // blk

    @pl.when(chunk == 0)
    def _():
        dqt_ref[...] = jnp.zeros_like(dqt_ref)
        for h in range(heads):
            at = slice(h * HD, (h + 1) * HD)
            out_grad = matmul(da_ref[...], out_ref[:, at]).astype(jnp.bfloat16)
            do_ref[:, at] = out_grad
            delta = jnp.sum(out_grad.astype(jnp.float32) * o_ref[:, at], axis=-1, keepdims=True)
            stat_ref[heads + h : heads + h + 1, :] = jnp.broadcast_to(
                delta, (delta.shape[0], 128)
            ).T[:1, :]
            stat_ref[h : h + 1, :] = jnp.log2(l_ref[:, h * 128 : (h + 1) * 128]).T[:1, :]

    dk_ref[...] = jnp.zeros_like(dk_ref)
    dv_ref[...] = jnp.zeros_like(dv_ref)

    def tile(b, slots, mask):
        rows = [pl.ds(pl.multiple_of(slot * blk, blk), blk) for slot in slots]
        cols = slice(b * blk, (b + 1) * blk)
        keys = jnp.concatenate([kv_ref[row, :HD] for row in rows], axis=0)
        vals = jnp.concatenate([kv_ref[row, HD:] for row in rows], axis=0)
        turned = jnp.concatenate([kt_ref[:, row] for row in rows], axis=1)
        dk_part = dv_part = None
        dq_parts = []
        add = lambda total, term: term if total is None else total + term
        for h in range(heads):
            query = q_ref[cols, h * HD : (h + 1) * HD]
            out_grad = do_ref[cols, h * HD : (h + 1) * HD]
            tangent = jnp.tanh(matmul_nt(keys, query) * (1.0 / soft_cap))
            probs = jnp.exp2(tangent * (soft_cap * LOG2E) - stat_ref[h : h + 1, cols])
            if mask is not None:
                probs = jnp.where(mask, probs, 0.0)
            prob_grad = matmul_nt(vals, out_grad)
            delta = stat_ref[heads + h : heads + h + 1, cols]
            score = (probs * (prob_grad - delta) * (1.0 - tangent * tangent)).astype(jnp.bfloat16)
            dk_part = add(dk_part, matmul(score, query))
            dv_part = add(dv_part, matmul(probs.astype(jnp.bfloat16), out_grad))
            dq_parts.append(matmul(turned, score))
        for h in range(heads):
            dqt_ref[h * HD : (h + 1) * HD, cols] += dq_parts[h]
        for k, row in enumerate(rows):
            dk_ref[row, :] += dk_part[k * blk : (k + 1) * blk]
            dv_ref[row, :] += dv_part[k * blk : (k + 1) * blk]

    visit_blocks(
        map_ref, me_ref[0], chunk, q_blocks, key_blocks, seq_blocks, reach, swapped, list_ref,
        tile, blk, True,
    )

    row = 0
    for dkv_ref in dkv_refs:
        count = dkv_ref.shape[0]
        dkv_ref[:, :HD] = dk_ref[row : row + count, :].astype(jnp.bfloat16)
        dkv_ref[:, HD:] = dv_ref[row : row + count, :].astype(jnp.bfloat16)
        row += count

    @pl.when(chunk == pl.num_programs(0) - 1)
    def _():
        cosine, sine = cos_ref[...], sin_ref[...]
        for h in range(heads):
            low = dqt_ref[h * HD : h * HD + HALF, :].T * HD ** (-0.5)
            high = dqt_ref[h * HD + HALF : (h + 1) * HD, :].T * HD ** (-0.5)
            dq_ref[:, h * HD : h * HD + HALF] = (low * cosine + high * sine).astype(jnp.bfloat16)
            dq_ref[:, h * HD + HALF : (h + 1) * HD] = (high * cosine - low * sine).astype(
                jnp.bfloat16
            )


def attend_back(
    block_map, me, branch_low, full_out_t, attended, totals, queries, kv_all, key_turned, cosine,
    sine, blk, seq_blocks, swapped
):
    rows, width = queries.shape
    heads = width // HD
    depth = branch_low.shape[1]
    total = kv_all.shape[0]
    chunk_rows = total if swapped else min(total, KEY_CHUNK)
    kernel = partial(
        attend_back_kernel, blk=blk, heads=heads, swapped=swapped, key_blocks=chunk_rows // blk,
        seq_blocks=seq_blocks, reach=WINDOW // blk,
    )
    whole = lambda i, *_: (0, 0)
    parts = [3 * rows, rows, 3 * rows, rows] if swapped else [total]
    dkv_shapes = [jax.ShapeDtypeStruct((part, 2 * HD), jnp.bfloat16) for part in parts]
    dkv_specs = [
        pl.BlockSpec((min(part, chunk_rows), 2 * HD), lambda i, *_: (i, 0)) for part in parts
    ]
    return pl.pallas_call(
        kernel,
        out_shape=(jax.ShapeDtypeStruct((rows, width), jnp.bfloat16), *dkv_shapes),
        grid_spec=pltpu.PrefetchScalarGridSpec(
            num_scalar_prefetch=2,
            grid=(total // chunk_rows,),
            in_specs=[
                pl.BlockSpec((rows, depth), whole),
                pl.BlockSpec((depth, width), whole),
                pl.BlockSpec((rows, width), whole),
                pl.BlockSpec((rows, heads * 128), whole),
                pl.BlockSpec((rows, width), whole),
                pl.BlockSpec((chunk_rows, 2 * HD), lambda i, *_: (i, 0)),
                pl.BlockSpec((HD, chunk_rows), lambda i, *_: (0, i)),
                pl.BlockSpec((rows, HALF), whole),
                pl.BlockSpec((rows, HALF), whole),
            ],
            out_specs=[pl.BlockSpec((rows, width), whole), *dkv_specs],
            scratch_shapes=[
                pltpu.VMEM((rows, width), jnp.bfloat16),
                pltpu.VMEM((2 * heads, rows), jnp.float32),
                pltpu.VMEM((width, rows), jnp.float32),
                pltpu.VMEM((chunk_rows, HD), jnp.float32),
                pltpu.VMEM((chunk_rows, HD), jnp.float32),
                pltpu.SMEM((chunk_rows // blk + 1,), jnp.int32),
            ],
        ),
        compiler_params=pltpu.CompilerParams(vmem_limit_bytes=MOST),
        cost_estimate=pl.CostEstimate(
            flops=10 * rows * width * total, bytes_accessed=16 * rows * width + 10 * total * HD,
            transcendentals=2 * rows * heads * total,
        ),
        name="attend_back",
    )(
        block_map, me, branch_low, full_out_t, attended, totals, queries, kv_all, key_turned,
        cosine, sine,
    )


def body(
    tokens, block_map, w_query, w_key, w_value, w_out, w_gate, w_up, w_down, norm_gains, cotangent
):
    ctx_count = lax.axis_size("ctx")
    tok_dev, depth = tokens.shape
    block_rows = tok_dev // 2
    seq_count = max(1, ctx_count // 16)
    seq_len = tok_dev * ctx_count // seq_count
    seq_blocks = seq_len // block_rows
    me = lax.axis_index("ctx")
    me_list = me.reshape(1).astype(jnp.int32)
    heads_dev = w_query.shape[1] // HD
    q_width = heads_dev * HD
    flat_map = block_map.reshape(-1).astype(jnp.int32)
    pairs = paired()

    qkv_shard = pack(w_query, w_key, w_value, norm_gains.T)
    if pairs:
        qkv_pieces = gather_pieces(qkv_shard)
        out_shard = tie(w_out, qkv_pieces[3], qkv_pieces[4]).T
        out_near = nearby(out_shard)
    else:
        qkv_pieces = (lax.all_gather(qkv_shard, "ctx", axis=0, tiled=True),)
        out_pieces = (lax.all_gather(w_out.T, "ctx", axis=0, tiled=True),)
    own_ids = lax.dynamic_index_in_dim(block_map, me, 0, keepdims=False)
    offsets = jnp.arange(block_rows, dtype=jnp.int32)
    own_index = (own_ids[:, None] * block_rows + offsets[None, :]).reshape(-1)
    cosine, sine = angle_tables(own_index % seq_len)
    inputs = tokens.astype(jnp.float32)
    in_scale = rms_scale(inputs)
    unit_in = (inputs * in_scale).astype(jnp.bfloat16)
    queries, *kv_local = project(unit_in, cosine, sine, qkv_pieces, heads_dev)
    if pairs:
        kv_local, out_near = lax.optimization_barrier((kv_local, out_near))
        kv_near = nearby_halves(*kv_local)
        kv_pieces = gather_halves(*kv_local, kv_near)
        half = out_shard.shape[0] // 2
        out_far = (swap(out_near[0][:half], 4), swap(out_near[1][half:], 2))
        out_mine = tie_all((out_shard, *out_near, *out_far), *kv_pieces[6:8])
        out_pieces = out_mine + tuple(swap(part, 1) for part in out_mine)
        late = (*kv_pieces[2:8], *out_far)
    else:
        kv_pieces = (lax.all_gather(jnp.concatenate(kv_local), "ctx", axis=0, tiled=True),)
        late = kv_pieces
    w_gate, w_up, w_down, *_ = lax.optimization_barrier((w_gate, w_up, w_down, *late))
    if pairs:
        gate_near = nearby(w_gate)
    attended, attn_flat, totals = attend(
        flat_map, me_list, queries, kv_pieces, block_rows, seq_blocks
    )
    branch_part = out_project(attn_flat, out_pieces, depth)
    if pairs:
        branch_part, *gate_near = lax.optimization_barrier((branch_part, *gate_near))
        gate_pieces = gather_pieces(w_gate, gate_near)
        qkv_pieces = tie_all(qkv_pieces, branch_part)
    branch = lax.psum(branch_part, "tp")
    full_up = lax.all_gather(w_up, "ctx", axis=0, tiled=True)
    full_qkv = assemble(qkv_pieces)
    gains = full_qkv[:, q_width + 2 * HD : q_width + 2 * HD + 4].T.astype(jnp.float32)
    normed_in = (inputs * in_scale * gains[0]).astype(jnp.bfloat16)
    if pairs:
        down_shard, gains, normed_in, *far = lax.optimization_barrier(
            (w_down.T, gains, normed_in, *gate_pieces[3:5])
        )
        gate_pieces = (*gate_pieces[:3], *far, *gate_pieces[5:])
        down_near = nearby(down_shard)
        full_gate = assemble(gate_pieces, 3)
        full_gate, *down_near = lax.optimization_barrier((full_gate, *down_near))
        down_pieces = gather_pieces(down_shard, down_near)
    else:
        full_gate = lax.all_gather(w_gate, "ctx", axis=0, tiled=True)
        down_pieces = (lax.all_gather(w_down.T, "ctx", axis=0, tiled=True),)
    branch, full_gate, full_up, *near = lax.optimization_barrier(
        (branch, full_gate, full_up, *down_pieces[:3])
    )
    normed_mid = by_rows(mid_kernel, (tokens, branch), gains, (jnp.bfloat16,), 0, "mid_norms")
    hidden, active, slope = units(normed_mid, full_gate, full_up)
    if pairs:
        hidden, *far = lax.optimization_barrier((hidden, *down_pieces[3:5]))
        mine = (*near, *far)
        down_pieces = (*mine, *(swap(part, 1) for part in mine))
    mlp_part = out_project(hidden, down_pieces, depth, "project_down")
    mlp_part, out_pieces, kv_pieces, down_pieces = lax.optimization_barrier(
        (mlp_part, out_pieces, kv_pieces, down_pieces)
    )
    full_down_t = assemble(down_pieces, 3)
    full_out_t = assemble(out_pieces)
    kv_all, key_turned = turn(kv_pieces)
    mlp_out = lax.psum(mlp_part, "tp")
    mlp_out, full_out_t, kv_all, key_turned, full_down_t = lax.optimization_barrier(
        (mlp_out, full_out_t, kv_all, key_turned, full_down_t)
    )
    result, mlp_low, gain_four = by_rows(
        top_kernel, (tokens, branch, mlp_out, cotangent), gains, (jnp.bfloat16, jnp.bfloat16), 1,
        "top_norms",
    )
    gate_low, up_low = units_back(mlp_low, full_down_t, active, slope)
    mid_part = features_back(gate_low, up_low, full_gate, full_up)
    mid_part, hidden_t, mlp_t, gate_t, up_t = lax.optimization_barrier(
        (mid_part, hidden, mlp_low, gate_low, up_low)
    )
    mid_sum = lax.psum(mid_part, "tp")
    down_grad = matmul(hidden_t.T, mlp_t).astype(jnp.bfloat16)
    down_shard = lax.psum_scatter(down_grad, "ctx", scatter_dimension=1, tiled=True)
    gate_grad = matmul(normed_mid.T, gate_t).astype(jnp.bfloat16)
    gate_blocks = scatter_start(gate_grad)
    up_grad = matmul(normed_mid.T, up_t).astype(jnp.bfloat16)
    up_grad, gate_blocks = lax.optimization_barrier((up_grad, gate_blocks))
    gate_terms = scatter_finish(gate_blocks)
    up_chips = scatter_chips(up_grad)
    mid_sum, up_chips = lax.optimization_barrier((mid_sum, up_chips))
    resid_grad, branch_low, gain_mid = by_rows(
        low_kernel, (tokens, branch, mid_sum, cotangent), gains, (jnp.float32, jnp.bfloat16), 2,
        "low_norms",
    )
    query_low, *kv_terms = attend_back(
        flat_map, me_list, branch_low, full_out_t, attended, totals, queries, kv_all, key_turned,
        cosine, sine, block_rows, seq_blocks, pairs,
    )
    *kv_terms, down_shard, gate_terms = lax.optimization_barrier((*kv_terms, down_shard, gate_terms))
    if pairs:
        far = kv_terms[1] + swap(kv_terms[3], 1)
        near = kv_terms[0] + swap(kv_terms[2], 1)
        blocks = (near[k * tok_dev : (k + 1) * tok_dev] for k in range(3))
        kv_sums = scatter_finish(scatter_corner(*blocks, far))
    else:
        kv_sums = (lax.psum_scatter(kv_terms[0], "ctx", scatter_dimension=0, tiled=True),)
    qkv_low, in_part, gain_one = join(cosine, sine, query_low, full_qkv, unit_in, kv_sums)
    in_part, qkv_low, branch_t, up_chips, gate_terms, down_shard = lax.optimization_barrier(
        (in_part, qkv_low, branch_low, up_chips, gate_terms, down_shard)
    )
    in_sum = lax.psum(in_part, "tp")
    up_shard = add_terms(scatter_finish(scatter_blocks(up_chips)))
    gain_one = sum_small_tp(gain_one)
    gains_shard = scatter_gains(jnp.concatenate([gain_one, gain_mid[1:], gain_mid[:1], gain_four]))
    qkv_grad = matmul(normed_in.T, qkv_low).astype(jnp.bfloat16)
    qkv_shard = add_terms(scatter_finish(scatter_start(qkv_grad)))
    out_weight_grad = matmul(branch_t.T, attn_flat).astype(jnp.bfloat16)
    out_grad_t = add_terms(scatter_finish(scatter_start(out_weight_grad)))
    shards = (
        qkv_shard[:, :q_width],
        qkv_shard[:, q_width : q_width + HD],
        qkv_shard[:, q_width + HD :],
        out_grad_t.T,
        add_terms(gate_terms),
        up_shard,
        down_shard.astype(jnp.float32),
        gains_shard,
    )
    input_grad = by_rows(
        end_kernel, (tokens, in_sum, resid_grad), gains, (jnp.float32,), 0, "end_norms"
    )
    return (result, input_grad, *shards)


def solution(mesh):
    in_specs = (
        P("ctx", None),
        P(),
        P("ctx", "tp"),
        P("ctx", "tp"),
        P("ctx", "tp"),
        P("tp", "ctx"),
        P("ctx", "tp"),
        P("ctx", "tp"),
        P("tp", "ctx"),
        P(None, "ctx"),
        P("ctx", None),
    )
    out_specs = (
        P("ctx", None),
        P("ctx", None),
        P("ctx", "tp"),
        P("ctx", "tp"),
        P("ctx", "tp"),
        P("tp", "ctx"),
        P("ctx", "tp"),
        P("ctx", "tp"),
        P("tp", "ctx"),
        P(None, "ctx"),
    )
    return jax.shard_map(body, mesh=mesh, in_specs=in_specs, out_specs=out_specs, check_vma=False)
```
